32 devices in a mesh: seq: 4 (over x, core), nbr: 8 (over z, y).
Axes of the slice: x: 2, y: 2, z: 4, core: 2. Of those that a mesh axis runs over, the one named last changes fastest.
Arguments:
- tokens: bfloat16 [32, 256, 768], P(('seq', 'nbr')), may hold values from -6 to 6
- neighbours: bfloat16 [256, 128, 768], P(('seq', 'nbr')), may hold values from -6 to 6
- out_grad: bfloat16 [32, 256, 768], P(('seq', 'nbr')), may hold values from -6 to 6
- lengths: int32 [32], P(('seq', 'nbr')), may hold values from 64 to 256, as said below
- slot_order: int32 [32, 8], P(('seq', 'nbr')), may hold values from 0 to 7, each once within a row
- selfgain: float32 [768], replicated, may hold values from 0.1 to 1.9
- selfjoint: bfloat16 [768, 2304], replicated, may hold values from -0.21875 to 0.21875
- selfmerge: bfloat16 [768, 768], replicated, may hold values from -0.875 to 0.875
- crossgain: float32 [768], replicated, may hold values from 0.1 to 1.9
- crossquery: bfloat16 [768, 768], replicated, may hold values from -0.21875 to 0.21875
- crossmerge: bfloat16 [768, 768], replicated, may hold values from -0.875 to 0.875
- feedgain: float32 [768], replicated, may hold values from 0.1 to 1.9
- feedup: bfloat16 [768, 3072], replicated, may hold values from -0.21875 to 0.21875
- feeddown: bfloat16 [3072, 768], replicated, may hold values from -0.109375 to 0.109375
- codergain: float32 [768], replicated, may hold values from 0.1 to 1.9
- coderjoint: bfloat16 [768, 2304], replicated, may hold values from -0.21875 to 0.21875
- codermerge: bfloat16 [768, 768], replicated, may hold values from -0.875 to 0.875
- codermid: float32 [768], replicated, may hold values from 0.1 to 1.9
- coderup: bfloat16 [768, 3072], replicated, may hold values from -0.21875 to 0.21875
- coderdown: bfloat16 [3072, 768], replicated, may hold values from -0.109375 to 0.109375
- codertop: float32 [768], replicated, may hold values from 0.1 to 1.9
- memorymap: bfloat16 [768, 1536], replicated, may hold values from -0.21875 to 0.21875
Outputs:
- output: bfloat16 [32, 256, 768], P(('seq', 'nbr'))
- input_grad: float32 [32, 256, 768], P(('seq', 'nbr'))
- grad_selfgain: float32 [768], P('nbr')
- grad_selfjoint: float32 [768, 2304], P('nbr')
- grad_selfmerge: float32 [768, 768], P('nbr')
- grad_crossgain: float32 [768], P('nbr')
- grad_crossquery: float32 [768, 768], P('nbr')
- grad_crossmerge: float32 [768, 768], P('nbr')
- grad_feedgain: float32 [768], P('nbr')
- grad_feedup: float32 [768, 3072], P('nbr')
- grad_feeddown: float32 [3072, 768], P('nbr')
- grad_codergain: float32 [768], P('nbr')
- grad_coderjoint: float32 [768, 2304], P('nbr')
- grad_codermerge: float32 [768, 768], P('nbr')
- grad_codermid: float32 [768], P('nbr')
- grad_coderup: float32 [768, 3072], P('nbr')
- grad_coderdown: float32 [3072, 768], P('nbr')
- grad_codertop: float32 [768], P('nbr')
- grad_memorymap: float32 [768, 1536], P('nbr')
The draws below stay inside these ranges and needn't reach their ends.
Inputs may be any that keep to these rules, and one draw needn't show every extreme that they name: `lengths`: some sequence has exactly 256 tokens in every draw. `slot_order`: each row is a permutation of its 8 places.
All inputs are finite; a program needn't handle non-finite values.
Results may differ from the reference program's by a relative error of at most 0.025.
Values may be sent and summed in bfloat16 or wider, within the bound.
A program may use at most 256 MiB of HBM per device.

```python
import jax
import jax.numpy as jnp
from jax import lax

D = 768
HEADS = 12
HD = 64
FF = 3072
CH = 64
NT = 128
LEN = 256
SEQS = 32
SPANS = 4
SLOTS = 8
CAP = 2
N_NBR = 8


def draw_lengths(key, part):
    key = jax.random.fold_in(key, 7)
    first_key, second_key = jax.random.split(key)
    drawn = jax.random.randint(first_key, (SEQS,), LEN // 4, LEN + 1)
    chosen = jax.random.randint(second_key, (), 0, SEQS)
    return drawn.at[chosen].set(LEN).astype(jnp.int32)


def block_scale(key, shape, cuts, least, largest):
    def one(position, blocks):
        steps = jax.random.uniform(jax.random.fold_in(jax.random.fold_in(key, 6), position), (blocks,), jnp.float32, least / len(cuts), largest / len(cuts))
        return jnp.repeat(jnp.exp(steps), shape[position] // blocks).reshape((-1,) + (1,) * (len(shape) - position - 1))

    loudness = one(*cuts[0])
    for cut in cuts[1:]:
        loudness = loudness * one(*cut)
    return loudness


def noise(key, shape, deviation, most, shards=(), held_as=jnp.bfloat16):
    values = jax.random.normal(key, shape, jnp.float32) * deviation
    if len(shards) > 0:
        values = block_scale(key, shape, shards, -0.22, 0.18) * values
    return jnp.clip(values, min=-most, max=most).astype(held_as)


def setup_inputs(seed: int = 0) -> dict:
    key_list = jax.random.split(jax.random.key(seed), 23)
    tokens = noise(key_list[0], (SEQS, LEN, D), 1.0, 6.0, ((0, 32),))
    neighbours = noise(key_list[1], (SEQS * SLOTS, NT, D), 1.0, 6.0, ((0, 32),))
    out_grad = noise(key_list[2], (SEQS, LEN, D), 1.0, 6.0, ((0, 32),))
    lengths = draw_lengths(jax.random.fold_in(key_list[22], 71), 0)
    slot_order = jax.vmap(lambda own: jax.random.permutation(own, SLOTS))(jax.random.split(key_list[4], SEQS)).reshape((SEQS, SLOTS)).astype(jnp.int32)
    selfgain = jnp.clip(1.0 + 0.18 * jax.random.normal(key_list[5], (D,), jnp.float32), 0.1, 1.9)
    selfjoint = noise(key_list[6], (D, 3 * D), D ** -0.5, 0.21875)
    selfmerge = noise(key_list[7], (D, D), (D // 16) ** -0.5, 0.875)
    crossgain = jnp.clip(1.0 + 0.18 * jax.random.normal(key_list[8], (D,), jnp.float32), 0.1, 1.9)
    crossquery = noise(key_list[9], (D, D), D ** -0.5, 0.21875)
    crossmerge = noise(key_list[10], (D, D), (D // 16) ** -0.5, 0.875)
    feedgain = jnp.clip(1.0 + 0.18 * jax.random.normal(key_list[11], (D,), jnp.float32), 0.1, 1.9)
    feedup = noise(key_list[12], (D, FF), D ** -0.5, 0.21875)
    feeddown = noise(key_list[13], (FF, D), FF ** -0.5, 0.109375)
    codergain = jnp.clip(1.0 + 0.18 * jax.random.normal(key_list[14], (D,), jnp.float32), 0.1, 1.9)
    coderjoint = noise(key_list[15], (D, 3 * D), D ** -0.5, 0.21875)
    codermerge = noise(key_list[16], (D, D), (D // 16) ** -0.5, 0.875)
    codermid = jnp.clip(1.0 + 0.18 * jax.random.normal(key_list[17], (D,), jnp.float32), 0.1, 1.9)
    coderup = noise(key_list[18], (D, FF), D ** -0.5, 0.21875)
    coderdown = noise(key_list[19], (FF, D), FF ** -0.5, 0.109375)
    codertop = jnp.clip(1.0 + 0.18 * jax.random.normal(key_list[20], (D,), jnp.float32), 0.1, 1.9)
    memorymap = noise(key_list[21], (D, 2 * D), D ** -0.5, 0.21875)
    return dict(tokens=tokens, neighbours=neighbours, out_grad=out_grad, lengths=lengths, slot_order=slot_order, selfgain=selfgain, selfjoint=selfjoint, selfmerge=selfmerge, crossgain=crossgain, crossquery=crossquery, crossmerge=crossmerge, feedgain=feedgain, feedup=feedup, feeddown=feeddown, codergain=codergain, coderjoint=coderjoint, codermerge=codermerge, codermid=codermid, coderup=coderup, coderdown=coderdown, codertop=codertop, memorymap=memorymap)


@jax.custom_vjp
def low(v):
    return lax.optimization_barrier(v.astype(jnp.bfloat16)).astype(jnp.float32)

@jax.custom_vjp
def low_back(v):
    return v

def low_keep(v):
    return (low(v), None)

def low_pass(kept, grad):
    return (grad,)

def back_keep(v):
    return (v, None)

def back_low(kept, grad):
    return (low(grad),)
low.defvjp(low_keep, low_pass)
low_back.defvjp(back_keep, back_low)

def layer_norm(values, gain):
    centred = values - lax.optimization_barrier(jnp.mean(values, axis=-1, keepdims=True))
    spread = lax.optimization_barrier(jnp.mean(centred * centred, axis=-1, keepdims=True))
    return centred * lax.rsqrt(spread + 1e-05) * gain

def linear(values, weight):
    return low_back(jnp.matmul(values, weight, precision=lax.Precision.HIGHEST))

def split_heads(joint, index):
    piece = joint[:, :, index * D:(index + 1) * D]
    return piece.reshape(piece.shape[0], piece.shape[1], HEADS, HD)

def attend(queries, keys, values, allowed):
    scores = low_back(jnp.einsum('brhd,bshd->bhrs', queries, keys, precision=lax.Precision.HIGHEST)) * HD ** (-0.5)
    scores = jnp.where(allowed[:, None], scores, -1000000000.0)
    probs = low(jax.nn.softmax(scores, axis=-1))
    mixed = jnp.einsum('bhrs,bshd->brhd', probs, values, precision=lax.Precision.HIGHEST)
    return low(low_back(mixed.reshape(mixed.shape[0], mixed.shape[1], HEADS * HD)))

def encode(block, params):
    bottom_gain, joint_weight, merge_weight, middle_gain, up_weight, down_weight, top_gain, memory_weight = params
    normed = low(layer_norm(block, bottom_gain))
    joint = low(linear(normed, joint_weight))
    everywhere = jnp.ones((1, NT, NT), jnp.bool_)
    mixed = attend(split_heads(joint, 0), split_heads(joint, 1), split_heads(joint, 2), everywhere)
    middle = block + linear(mixed, merge_weight)
    hidden = low(jax.nn.gelu(linear(low(layer_norm(middle, middle_gain)), up_weight), approximate=True))
    upper = middle + linear(hidden, down_weight)
    return low(linear(low(layer_norm(upper, top_gain)), memory_weight))

def decode(sequence, memory, length, params):
    self_gain, self_joint, self_merge, cross_gain, cross_query, cross_merge, feed_gain, feed_up, feed_down = params
    places = jnp.arange(LEN, dtype=jnp.int32)
    normed = low(layer_norm(sequence, self_gain))
    joint = low(linear(normed, self_joint))[None]
    causal = ((places[None, :] <= places[:, None]) & (places[None, :] < length))[None]
    mixed = attend(split_heads(joint, 0), split_heads(joint, 1), split_heads(joint, 2), causal)[0]
    after_self = sequence + linear(mixed, self_merge)
    asked = low(linear(low(layer_norm(after_self, cross_gain)), cross_query)).reshape(SPANS, CH, HEADS, HD)
    memory_keys = memory[:, :, :D].reshape(SPANS, 2 * NT, HEADS, HD)
    memory_values = memory[:, :, D:].reshape(SPANS, 2 * NT, HEADS, HD)
    everywhere = jnp.ones((1, CH, 2 * NT), jnp.bool_)
    crossed = attend(asked, memory_keys, memory_values, everywhere).reshape(LEN, D)
    live = (places // CH * CH < length).astype(jnp.float32)[:, None]
    after_cross = after_self + linear(crossed, cross_merge) * live
    hidden = low(jax.nn.gelu(linear(low(layer_norm(after_cross, feed_gain)), feed_up), approximate=True))
    return after_cross + linear(hidden, feed_down)

def reference(tokens, neighbours, out_grad, lengths, slot_order, selfgain, selfjoint, selfmerge, crossgain, crossquery, crossmerge, feedgain, feedup, feeddown, codergain, coderjoint, codermerge, codermid, coderup, coderdown, codertop, memorymap):
    decoder_params = tuple((item.astype(jnp.float32) for item in (selfgain, selfjoint, selfmerge, crossgain, crossquery, crossmerge, feedgain, feedup, feeddown)))
    encoder_params = tuple((item.astype(jnp.float32) for item in (codergain, coderjoint, codermerge, codermid, coderup, coderdown, codertop, memorymap)))
    receiver = jnp.arange(SEQS, dtype=jnp.int32)
    group = receiver // N_NBR
    column = receiver % N_NBR
    sender = slot_order // CAP * N_NBR + column[:, None]
    source = (sender * SLOTS + group[:, None] * CAP + slot_order % CAP).astype(jnp.int32)
    embedded = neighbours.astype(jnp.float32).reshape(SEQS, SLOTS, NT, D)

    def forward(sequences, dec_params, enc_params):
        memory = lax.map(jax.checkpoint(lambda block: encode(block, enc_params)), embedded)
        memory = memory.reshape(SEQS * SLOTS, NT, 2 * D)[source.reshape(-1)]
        memory = memory.reshape(SEQS, SPANS, 2 * NT, 2 * D)
        return lax.map(jax.checkpoint(lambda item: decode(item[0], item[1], item[2], dec_params)), (sequences, memory, lengths))
    output, pullback = jax.vjp(forward, tokens.astype(jnp.float32), decoder_params, encoder_params)
    input_grad, dec_grads, enc_grads = pullback(out_grad.astype(jnp.float32))
    return (output.astype(jnp.bfloat16), input_grad, dec_grads[0], dec_grads[1], dec_grads[2], dec_grads[3], dec_grads[4], dec_grads[5], dec_grads[6], dec_grads[7], dec_grads[8], enc_grads[0], enc_grads[1], enc_grads[2], enc_grads[3], enc_grads[4], enc_grads[5], enc_grads[6], enc_grads[7])
```

```python
from functools import partial

import jax
import jax.numpy as jnp
from jax import lax
from jax.experimental import pallas as pl
from jax.experimental.pallas import tpu as pltpu
from jax.sharding import PartitionSpec as P

D = 768
HEADS = 12
HD = 64
CH = 64
PAIRS = HEADS // 2
LANES = 2 * HD
SCALE = HD ** (-0.5)
F32 = jnp.float32
BF16 = jnp.bfloat16


def norm_forward(values, gain):
    centred = values - jnp.mean(values, axis=-1, keepdims=True)
    inverse = lax.rsqrt(jnp.mean(centred * centred, axis=-1, keepdims=True) + 1e-05)
    normed = centred * inverse
    return ((normed * gain).astype(BF16), normed, inverse)


def norm_backward(grad, normed, inverse, gain):
    scaled = grad * gain
    inner = jnp.mean(scaled * normed, axis=-1, keepdims=True)
    return inverse * (scaled - jnp.mean(scaled, axis=-1, keepdims=True) - normed * inner)


def times(values, weight):
    return lax.dot_general(values, weight, (((1,), (0,)), ((), ())), preferred_element_type=F32)


def times_back(grad, weight):
    return lax.dot_general(grad, weight, (((1,), (1,)), ((), ())), preferred_element_type=F32)


def weight_grad(values, grad):
    return lax.dot_general(values, grad, (((0,), (0,)), ((), ())), preferred_element_type=F32)


def curve_grad(rising, upstream):
    return jax.vjp(partial(jax.nn.gelu, approximate=True), rising)[1](upstream)[0]


def dot_nt(a, b):
    return lax.dot_general(a, b, (((1,), (1,)), ((), ())), preferred_element_type=F32)


def dot_nn(a, b):
    return lax.dot_general(a, b, (((1,), (0,)), ((), ())), preferred_element_type=F32)


def dot_tn(a, b):
    return lax.dot_general(a, b, (((0,), (0,)), ((), ())), preferred_element_type=F32)


def stack_pair(block):
    lane = lax.broadcasted_iota(jnp.int32, block.shape, 1)
    zero = jnp.zeros_like(block)
    return jnp.concatenate([jnp.where(lane < HD, block, zero), jnp.where(lane >= HD, block, zero)], axis=0)


def unstack_pair(stacked):
    half = stacked.shape[0] // 2
    lane = lax.broadcasted_iota(jnp.int32, (half, LANES), 1)
    return jnp.where(lane < HD, stacked[:half], stacked[half:])


def softmax_halves(products, allowed):
    width = products.shape[1] // 2
    parts = []
    for h in range(2):
        scores = products[:, h * width : (h + 1) * width] * SCALE
        if allowed is not None:
            scores = jnp.where(allowed, scores, -1000000000.0)
        exponent = jnp.exp(scores - jnp.max(scores, axis=-1, keepdims=True))
        parts.append(exponent * (1.0 / jnp.sum(exponent, axis=-1, keepdims=True)))
    return parts


def pair_forward(queries, keys, values, allowed):
    probs = softmax_halves(dot_nt(queries, stack_pair(keys)), allowed)
    probs = jnp.concatenate([p.astype(BF16) for p in probs], axis=1)
    return dot_nn(probs, stack_pair(values)).astype(BF16)


def pair_backward(queries, keys, values, outgoing, allowed):
    keys2 = stack_pair(keys)
    probs = softmax_halves(dot_nt(queries, keys2), allowed)
    rounded = jnp.concatenate([p.astype(BF16) for p in probs], axis=1)
    value_grad = unstack_pair(dot_tn(rounded, outgoing))
    prob_grad = dot_nt(outgoing, stack_pair(values))
    width = prob_grad.shape[1] // 2
    parts = []
    for h in range(2):
        part = prob_grad[:, h * width : (h + 1) * width]
        inner = jnp.sum(probs[h] * part, axis=-1, keepdims=True)
        parts.append((probs[h] * (part - inner) * SCALE).astype(BF16))
    score_grad = jnp.concatenate(parts, axis=1)
    query_grad = dot_nn(score_grad, keys2)
    key_grad = unstack_pair(dot_tn(score_grad, queries))
    return query_grad.astype(BF16), key_grad.astype(BF16), value_grad.astype(BF16)


def col(pair, third=0):
    return slice(third * D + pair * LANES, third * D + (pair + 1) * LANES)


def estimate(flops, nbytes, exps=0):
    return pl.CostEstimate(flops=int(flops), bytes_accessed=int(nbytes), transcendentals=int(exps))


def enc_attend_kernel(joint_ref, mixed_ref):
    for p in range(PAIRS):
        mixed_ref[0, :, col(p)] = pair_forward(
            joint_ref[0, :, col(p, 0)], joint_ref[0, :, col(p, 1)], joint_ref[0, :, col(p, 2)], None
        )


def enc_attend(joint):
    count, rows, _ = joint.shape
    return pl.pallas_call(
        enc_attend_kernel,
        grid=(count,),
        in_specs=[pl.BlockSpec((1, rows, 3 * D), lambda i: (i, 0, 0))],
        out_specs=pl.BlockSpec((1, rows, D), lambda i: (i, 0, 0)),
        out_shape=jax.ShapeDtypeStruct((count, rows, D), BF16),
        cost_estimate=estimate(4 * count * rows * rows * D * 4, count * rows * D * 8, count * rows * rows * HEADS),
        name="enc_attend",
    )(joint)


def enc_attend_back_kernel(joint_ref, grad_ref, out_ref):
    for p in range(PAIRS):
        grads = pair_backward(
            joint_ref[0, :, col(p, 0)], joint_ref[0, :, col(p, 1)], joint_ref[0, :, col(p, 2)], grad_ref[0, :, col(p)], None
        )
        for third in range(3):
            out_ref[0, :, col(p, third)] = grads[third]


def enc_attend_back(joint, grad):
    count, rows, _ = joint.shape
    return pl.pallas_call(
        enc_attend_back_kernel,
        grid=(count,),
        in_specs=[
            pl.BlockSpec((1, rows, 3 * D), lambda i: (i, 0, 0)),
            pl.BlockSpec((1, rows, D), lambda i: (i, 0, 0)),
        ],
        out_specs=pl.BlockSpec((1, rows, 3 * D), lambda i: (i, 0, 0)),
        out_shape=jax.ShapeDtypeStruct((count, rows, 3 * D), BF16),
        cost_estimate=estimate(10 * count * rows * rows * D * 4, count * rows * D * 14, count * rows * rows * HEADS),
        name="enc_attend_back",
    )(joint, grad)


def causal_mask(rows, length):
    row = lax.broadcasted_iota(jnp.int32, (rows, rows), 0)
    column = lax.broadcasted_iota(jnp.int32, (rows, rows), 1)
    return (column <= row) & (column < length)


def self_attend_kernel(length_ref, q_ref, k_ref, v_ref, out_ref):
    allowed = causal_mask(q_ref.shape[0], length_ref[0])
    out_ref[...] = pair_forward(q_ref[...], k_ref[...], v_ref[...], allowed)


def self_attend(joint, lengths):
    rows = joint.shape[0]
    return pl.pallas_call(
        self_attend_kernel,
        grid_spec=pltpu.PrefetchScalarGridSpec(
            num_scalar_prefetch=1,
            grid=(PAIRS,),
            in_specs=[pl.BlockSpec((rows, LANES), lambda p, _, t=t: (0, t * PAIRS + p)) for t in range(3)],
            out_specs=pl.BlockSpec((rows, LANES), lambda p, _: (0, p)),
        ),
        out_shape=jax.ShapeDtypeStruct((rows, D), BF16),
        cost_estimate=estimate(4 * rows * rows * D * 4, rows * D * 8, rows * rows * HEADS),
        name="self_attend",
    )(lengths, joint, joint, joint)


def self_attend_back_kernel(length_ref, q_ref, k_ref, v_ref, grad_ref, dq_ref, dk_ref, dv_ref):
    allowed = causal_mask(q_ref.shape[0], length_ref[0])
    grads = pair_backward(q_ref[...], k_ref[...], v_ref[...], grad_ref[...], allowed)
    dq_ref[...] = grads[0]
    dk_ref[...] = grads[1]
    dv_ref[...] = grads[2]


def self_attend_back(joint, grad, lengths):
    rows = joint.shape[0]
    block = pl.BlockSpec((rows, LANES), lambda p, _: (0, p))
    return pl.pallas_call(
        self_attend_back_kernel,
        grid_spec=pltpu.PrefetchScalarGridSpec(
            num_scalar_prefetch=1,
            grid=(PAIRS,),
            in_specs=[pl.BlockSpec((rows, LANES), lambda p, _, t=t: (0, t * PAIRS + p)) for t in range(3)] + [block],
            out_specs=[block] * 3,
        ),
        out_shape=[jax.ShapeDtypeStruct((rows, D), BF16)] * 3,
        cost_estimate=estimate(10 * rows * rows * D * 4, rows * D * 14, rows * rows * HEADS),
        name="self_attend_back",
    )(lengths, joint, joint, joint, grad)


def cross_attend_kernel(order_ref, asked_ref, first_ref, second_ref, out_ref):
    for p in range(PAIRS):
        keys = jnp.concatenate([first_ref[0, :, col(p, 0)], second_ref[0, :, col(p, 0)]], axis=0)
        values = jnp.concatenate([first_ref[0, :, col(p, 1)], second_ref[0, :, col(p, 1)]], axis=0)
        out_ref[:, col(p)] = pair_forward(asked_ref[:, col(p)], keys, values, None)


def cross_attend(asked, memory, order):
    rows = asked.shape[0]
    count, places, _ = memory.shape
    return pl.pallas_call(
        cross_attend_kernel,
        grid_spec=pltpu.PrefetchScalarGridSpec(
            num_scalar_prefetch=1,
            grid=(rows // CH,),
            in_specs=[
                pl.BlockSpec((CH, D), lambda c, order: (c, 0)),
                pl.BlockSpec((1, places, 2 * D), lambda c, order: (order[2 * c], 0, 0)),
                pl.BlockSpec((1, places, 2 * D), lambda c, order: (order[2 * c + 1], 0, 0)),
            ],
            out_specs=pl.BlockSpec((CH, D), lambda c, order: (c, 0)),
        ),
        out_shape=jax.ShapeDtypeStruct((rows, D), BF16),
        cost_estimate=estimate(4 * rows * 2 * places * D * 4, rows * D * 4 + count * places * D * 4, rows * 2 * places * HEADS),
        name="cross_attend",
    )(order, asked, memory, memory)


def cross_attend_back_kernel(order_ref, asked_ref, first_ref, second_ref, grad_ref, dq_ref, dmem_ref):
    c = pl.program_id(0)
    first, second = order_ref[2 * c], order_ref[2 * c + 1]
    places = first_ref.shape[1]
    for p in range(PAIRS):
        keys = jnp.concatenate([first_ref[0, :, col(p, 0)], second_ref[0, :, col(p, 0)]], axis=0)
        values = jnp.concatenate([first_ref[0, :, col(p, 1)], second_ref[0, :, col(p, 1)]], axis=0)
        dq, dk, dv = pair_backward(asked_ref[:, col(p)], keys, values, grad_ref[:, col(p)], None)
        dq_ref[:, col(p)] = dq
        dmem_ref[first, :, col(p, 0)] = dk[:places]
        dmem_ref[second, :, col(p, 0)] = dk[places:]
        dmem_ref[first, :, col(p, 1)] = dv[:places]
        dmem_ref[second, :, col(p, 1)] = dv[places:]


def cross_attend_back(asked, memory, grad, order):
    rows = asked.shape[0]
    count, places, _ = memory.shape
    return pl.pallas_call(
        cross_attend_back_kernel,
        grid_spec=pltpu.PrefetchScalarGridSpec(
            num_scalar_prefetch=1,
            grid=(rows // CH,),
            in_specs=[
                pl.BlockSpec((CH, D), lambda c, order: (c, 0)),
                pl.BlockSpec((1, places, 2 * D), lambda c, order: (order[2 * c], 0, 0)),
                pl.BlockSpec((1, places, 2 * D), lambda c, order: (order[2 * c + 1], 0, 0)),
                pl.BlockSpec((CH, D), lambda c, order: (c, 0)),
            ],
            out_specs=[
                pl.BlockSpec((CH, D), lambda c, order: (c, 0)),
                pl.BlockSpec((count, places, 2 * D), lambda c, order: (0, 0, 0)),
            ],
        ),
        out_shape=[jax.ShapeDtypeStruct((rows, D), BF16), jax.ShapeDtypeStruct(memory.shape, BF16)],
        cost_estimate=estimate(10 * rows * 2 * places * D * 4, rows * D * 6 + count * places * D * 8, rows * 2 * places * HEADS),
        name="cross_attend_back",
    )(order, asked, memory, memory, grad)


def swap(value, axis, size, mask):
    return lax.ppermute(value, axis, [(i, i ^ mask) for i in range(size)])


def bit_of(axis, mask):
    return (lax.axis_index(axis) // mask) % 2


def pick(value, dim, index):
    return lax.dynamic_index_in_dim(value, index, dim, keepdims=False)


def halve(value, dim, axis, size, mask):
    bit = bit_of(axis, mask)
    arrived = swap(pick(value, dim, 1 - bit), axis, size, mask)
    return (pick(value, dim, bit).astype(F32) + arrived.astype(F32)).astype(BF16)


def join(value, dim, axis, size, mask):
    arrived = swap(value, axis, size, mask)
    bit = bit_of(axis, mask)
    return jnp.where(
        bit == 0, jnp.concatenate([value, arrived], axis=dim), jnp.concatenate([arrived, value], axis=dim)
    )


def masks(size):
    found, mask = [], 1
    while mask < size:
        found.append(mask)
        mask *= 2
    return found


def reduce_group(pairs, sizes, rows_first):
    nseq, nnbr = sizes
    core = bit_of("seq", 1)
    parts = []
    for values, grad in pairs:
        half = grad.shape[1] // 2
        theirs = lax.dynamic_slice_in_dim(grad, (1 - core) * half, half, 1)
        ours = lax.dynamic_slice_in_dim(grad, core * half, half, 1)
        arrived = swap(weight_grad(values, theirs).astype(BF16), "seq", nseq, 1)
        parts.append((weight_grad(values, ours) + arrived.astype(F32)).astype(BF16))
    widths = [part.shape[1] for part in parts]
    total = parts[0] if len(parts) == 1 else jnp.concatenate(parts, axis=1)
    bits = masks(nnbr)
    rows = total.shape[0] // nnbr
    total = total.reshape((2,) * len(bits) + (rows, total.shape[1]))
    seq_bits = masks(nseq)[1:]

    def over_seq(total):
        for mask in seq_bits:
            shape = total.shape
            total = total.reshape(shape[:-2] + (2, shape[-2] // 2, shape[-1]))
            total = halve(total, total.ndim - 3, "seq", nseq, mask)
        return total

    def over_nbr(total):
        left = list(reversed(bits))
        for mask in bits:
            total = halve(total, left.index(mask), "nbr", nnbr, mask)
            left.remove(mask)
        return total

    if rows_first:
        total = over_nbr(over_seq(total))
        for mask in reversed(seq_bits):
            total = join(total, 0, "seq", nseq, mask)
    else:
        total = over_nbr(total)
        for mask in seq_bits:
            total = (total.astype(F32) + swap(total, "seq", nseq, mask).astype(F32)).astype(BF16)
    other = swap(total, "seq", nseq, 1)
    results, start = [], 0
    for width in widths:
        mine, theirs = total[:, start : start + width], other[:, start : start + width]
        results.append(
            jnp.where(
                core == 0, jnp.concatenate([mine, theirs], axis=1), jnp.concatenate([theirs, mine], axis=1)
            ).astype(F32)
        )
        start += width
    return results


def gain_grad(gain, weight, grad, nnbr):
    rows = weight.shape[0] // nnbr
    start = lax.axis_index("nbr") * rows
    own = lax.dynamic_slice_in_dim(weight, start, rows, 0).astype(F32)
    return jnp.sum(own * grad, axis=1) / lax.dynamic_slice_in_dim(gain, start, rows, 0)


def body(
    sizes,
    tokens,
    neighbours,
    out_grad,
    lengths,
    slot_order,
    selfgain,
    selfjoint,
    selfmerge,
    crossgain,
    crossquery,
    crossmerge,
    feedgain,
    feedup,
    feeddown,
    codergain,
    coderjoint,
    codermerge,
    codermid,
    coderup,
    coderdown,
    codertop,
    memorymap,
):
    nseq, nnbr = sizes
    me = lax.axis_index("seq")
    count, places, _ = neighbours.shape
    cap = count // nseq
    flat = count * places

    ordered = jnp.concatenate(
        [lax.dynamic_slice_in_dim(neighbours, (me ^ m) * cap, cap, 0) for m in range(nseq)], axis=0
    )
    embedded = ordered.reshape(flat, D).astype(F32)
    enc_normed, _, _ = norm_forward(embedded, codergain)
    enc_joint = times(enc_normed, coderjoint).astype(BF16).reshape(count, places, 3 * D)
    enc_mixed = enc_attend(enc_joint).reshape(flat, D)
    enc_middle = embedded + times(enc_mixed, codermerge)
    enc_normed_b, enc_plain_b, enc_inverse_b = norm_forward(enc_middle, codermid)
    enc_rising = times(enc_normed_b, coderup)
    enc_hidden = jax.nn.gelu(enc_rising, approximate=True).astype(BF16)
    enc_upper = enc_middle + times(enc_hidden, coderdown)
    enc_normed_c, enc_plain_c, enc_inverse_c = norm_forward(enc_upper, codertop)
    blocks = enc_normed_c.reshape(nseq, cap * places, D)
    received = jnp.concatenate(
        [blocks[m] if m == 0 else swap(blocks[m], "seq", nseq, m) for m in range(nseq)], axis=0
    )

    sequence = tokens[0].astype(F32)
    rows = sequence.shape[0]
    normed_a, plain_a, inverse_a = norm_forward(sequence, selfgain)
    joint = times(normed_a, selfjoint).astype(BF16)
    mixed = self_attend(joint, lengths)
    after_self = sequence + times(mixed, selfmerge)
    normed_b, plain_b, inverse_b = norm_forward(after_self, crossgain)
    asked = times(normed_b, crossquery).astype(BF16)

    memory = times(received, memorymap).astype(BF16).reshape(count, places, 2 * D)
    order = slot_order[0]
    order = ((order // cap) ^ me) * cap + order % cap
    crossed = cross_attend(asked, memory, order)
    live = (jnp.arange(rows, dtype=jnp.int32) // CH * CH < lengths[0]).astype(F32)[:, None]
    after_cross = after_self + times(crossed, crossmerge) * live
    normed_c, plain_c, inverse_c = norm_forward(after_cross, feedgain)
    rising = times(normed_c, feedup)
    hidden = jax.nn.gelu(rising, approximate=True).astype(BF16)
    output = (after_cross + times(hidden, feeddown)).astype(BF16)[None]

    down_in = out_grad[0]
    (grad_feeddown,) = reduce_group([(hidden, down_in)], sizes, False)
    rising_grad = curve_grad(rising, times_back(down_in, feeddown)).astype(BF16)
    (grad_feedup,) = reduce_group([(normed_c, rising_grad)], sizes, True)
    cross_total = down_in.astype(F32) + norm_backward(times_back(rising_grad, feedup), plain_c, inverse_c, feedgain)
    cross_in = (cross_total * live).astype(BF16)
    crossed_grad = times_back(cross_in, crossmerge).astype(BF16)
    asked_grad, memory_grad = cross_attend_back(asked, memory, crossed_grad, order)
    memory_grad = memory_grad.reshape(flat, 2 * D)
    back = times_back(memory_grad, memorymap).astype(BF16).reshape(nseq, cap * places, D)
    returned = jnp.concatenate(
        [back[m] if m == 0 else swap(back[m], "seq", nseq, m) for m in range(nseq)], axis=0
    ).astype(F32)
    grad_crossmerge, grad_crossquery, grad_memorymap = reduce_group(
        [(crossed, cross_in), (normed_b, asked_grad), (received, memory_grad)], sizes, False
    )
    self_total = cross_total + norm_backward(times_back(asked_grad, crossquery), plain_b, inverse_b, crossgain)
    self_in = self_total.astype(BF16)
    mixed_grad = times_back(self_in, selfmerge).astype(BF16)
    joint_grad = jnp.concatenate(self_attend_back(joint, mixed_grad, lengths), axis=1)
    grad_selfmerge, grad_selfjoint = reduce_group([(mixed, self_in), (normed_a, joint_grad)], sizes, False)
    input_grad = (self_total + norm_backward(times_back(joint_grad, selfjoint), plain_a, inverse_a, selfgain))[None]

    upper_total = norm_backward(returned, enc_plain_c, enc_inverse_c, codertop)
    enc_down_in = upper_total.astype(BF16)
    (grad_coderdown,) = reduce_group([(enc_hidden, enc_down_in)], sizes, True)
    enc_rising_grad = curve_grad(enc_rising, times_back(enc_down_in, coderdown)).astype(BF16)
    (grad_coderup,) = reduce_group([(enc_normed_b, enc_rising_grad)], sizes, False)
    middle_total = upper_total + norm_backward(
        times_back(enc_rising_grad, coderup), enc_plain_b, enc_inverse_b, codermid
    )
    enc_merge_in = middle_total.astype(BF16)
    enc_mixed_grad = times_back(enc_merge_in, codermerge).astype(BF16).reshape(count, places, D)
    enc_joint_grad = enc_attend_back(enc_joint, enc_mixed_grad).reshape(flat, 3 * D)
    grad_codermerge, grad_coderjoint = reduce_group(
        [(enc_mixed, enc_merge_in), (enc_normed, enc_joint_grad)], sizes, True
    )
    return (
        output,
        input_grad,
        gain_grad(selfgain, selfjoint, grad_selfjoint, nnbr),
        grad_selfjoint,
        grad_selfmerge,
        gain_grad(crossgain, crossquery, grad_crossquery, nnbr),
        grad_crossquery,
        grad_crossmerge,
        gain_grad(feedgain, feedup, grad_feedup, nnbr),
        grad_feedup,
        grad_feeddown,
        gain_grad(codergain, coderjoint, grad_coderjoint, nnbr),
        grad_coderjoint,
        grad_codermerge,
        gain_grad(codermid, coderup, grad_coderup, nnbr),
        grad_coderup,
        grad_coderdown,
        gain_grad(codertop, memorymap, grad_memorymap, nnbr),
        grad_memorymap,
    )


def solution(mesh):
    spread = ("seq", "nbr")
    sizes = (mesh.shape["seq"], mesh.shape["nbr"])
    placed = (
        P(spread, None, None),
        P(spread, None, None),
        P(spread, None, None),
        P(spread),
        P(spread, None),
    ) + (P(),) * 17
    gain, weight = P("nbr"), P("nbr", None)
    return jax.shard_map(
        partial(body, sizes),
        mesh=mesh,
        in_specs=placed,
        out_specs=(
            P(spread, None, None),
            P(spread, None, None),
            gain,
            weight,
            weight,
            gain,
            weight,
            weight,
            gain,
            weight,
            weight,
            gain,
            weight,
            weight,
            gain,
            weight,
            weight,
            gain,
            weight,
        ),
        check_vma=False,
    )
```

```python
from functools import partial

import jax
import jax.numpy as jnp
from jax import lax
from jax.experimental import pallas as pl
from jax.experimental.pallas import tpu as pltpu
from jax.sharding import PartitionSpec as P

D = 768
HEADS = 12
HD = 64
CH = 64
PAIRS = HEADS // 2
LANES = 2 * HD
SCALE = HD ** (-0.5)
F32 = jnp.float32
BF16 = jnp.bfloat16


def norm_forward(values, gain):
    centred = values - jnp.mean(values, axis=-1, keepdims=True)
    inverse = lax.rsqrt(jnp.mean(centred * centred, axis=-1, keepdims=True) + 1e-05)
    normed = centred * inverse
    return ((normed * gain).astype(BF16), normed, inverse)


def norm_backward(grad, normed, inverse, gain):
    scaled = grad * gain
    inner = jnp.mean(scaled * normed, axis=-1, keepdims=True)
    return inverse * (scaled - jnp.mean(scaled, axis=-1, keepdims=True) - normed * inner)


def times(values, weight):
    return lax.dot_general(values, weight, (((1,), (0,)), ((), ())), preferred_element_type=F32)


def times_back(grad, weight):
    return lax.dot_general(grad, weight, (((1,), (1,)), ((), ())), preferred_element_type=F32)


def weight_grad(values, grad):
    return lax.dot_general(values, grad, (((0,), (0,)), ((), ())), preferred_element_type=F32)


def curve_grad(rising, upstream):
    return jax.vjp(partial(jax.nn.gelu, approximate=True), rising)[1](upstream)[0]


def dot_nt(a, b):
    return lax.dot_general(a, b, (((1,), (1,)), ((), ())), preferred_element_type=F32)


def dot_nn(a, b):
    return lax.dot_general(a, b, (((1,), (0,)), ((), ())), preferred_element_type=F32)


def dot_tn(a, b):
    return lax.dot_general(a, b, (((0,), (0,)), ((), ())), preferred_element_type=F32)


def stack_pair(block):
    lane = lax.broadcasted_iota(jnp.int32, block.shape, 1)
    zero = jnp.zeros_like(block)
    return jnp.concatenate([jnp.where(lane < HD, block, zero), jnp.where(lane >= HD, block, zero)], axis=0)


def unstack_pair(stacked):
    half = stacked.shape[0] // 2
    lane = lax.broadcasted_iota(jnp.int32, (half, LANES), 1)
    return jnp.where(lane < HD, stacked[:half], stacked[half:])


def softmax_halves(products, allowed):
    width = products.shape[1] // 2
    parts = []
    for h in range(2):
        scores = products[:, h * width : (h + 1) * width] * SCALE
        if allowed is not None:
            scores = jnp.where(allowed, scores, -1000000000.0)
        exponent = jnp.exp(scores - jnp.max(scores, axis=-1, keepdims=True))
        parts.append(exponent * (1.0 / jnp.sum(exponent, axis=-1, keepdims=True)))
    return parts


def pair_forward(queries, keys, values, allowed):
    probs = softmax_halves(dot_nt(queries, stack_pair(keys)), allowed)
    probs = jnp.concatenate([p.astype(BF16) for p in probs], axis=1)
    return dot_nn(probs, stack_pair(values)).astype(BF16)


def pair_backward(queries, keys, values, outgoing, allowed):
    keys2 = stack_pair(keys)
    probs = softmax_halves(dot_nt(queries, keys2), allowed)
    rounded = jnp.concatenate([p.astype(BF16) for p in probs], axis=1)
    value_grad = unstack_pair(dot_tn(rounded, outgoing))
    prob_grad = dot_nt(outgoing, stack_pair(values))
    width = prob_grad.shape[1] // 2
    parts = []
    for h in range(2):
        part = prob_grad[:, h * width : (h + 1) * width]
        inner = jnp.sum(probs[h] * part, axis=-1, keepdims=True)
        parts.append((probs[h] * (part - inner) * SCALE).astype(BF16))
    score_grad = jnp.concatenate(parts, axis=1)
    query_grad = dot_nn(score_grad, keys2)
    key_grad = unstack_pair(dot_tn(score_grad, queries))
    return query_grad.astype(BF16), key_grad.astype(BF16), value_grad.astype(BF16)


def col(pair, third=0):
    return slice(third * D + pair * LANES, third * D + (pair + 1) * LANES)


def estimate(flops, nbytes, exps=0):
    return pl.CostEstimate(flops=int(flops), bytes_accessed=int(nbytes), transcendentals=int(exps))


def enc_attend_kernel(joint_ref, mixed_ref):
    for p in range(PAIRS):
        mixed_ref[0, :, col(p)] = pair_forward(
            joint_ref[0, :, col(p, 0)], joint_ref[0, :, col(p, 1)], joint_ref[0, :, col(p, 2)], None
        )


def enc_attend(joint):
    count, rows, _ = joint.shape
    return pl.pallas_call(
        enc_attend_kernel,
        grid=(count,),
        in_specs=[pl.BlockSpec((1, rows, 3 * D), lambda i: (i, 0, 0))],
        out_specs=pl.BlockSpec((1, rows, D), lambda i: (i, 0, 0)),
        out_shape=jax.ShapeDtypeStruct((count, rows, D), BF16),
        cost_estimate=estimate(4 * count * rows * rows * D * 4, count * rows * D * 8, count * rows * rows * HEADS),
        name="enc_attend",
    )(joint)


def enc_attend_back_kernel(joint_ref, grad_ref, out_ref):
    for p in range(PAIRS):
        grads = pair_backward(
            joint_ref[0, :, col(p, 0)], joint_ref[0, :, col(p, 1)], joint_ref[0, :, col(p, 2)], grad_ref[0, :, col(p)], None
        )
        for third in range(3):
            out_ref[0, :, col(p, third)] = grads[third]


def enc_attend_back(joint, grad):
    count, rows, _ = joint.shape
    return pl.pallas_call(
        enc_attend_back_kernel,
        grid=(count,),
        in_specs=[
            pl.BlockSpec((1, rows, 3 * D), lambda i: (i, 0, 0)),
            pl.BlockSpec((1, rows, D), lambda i: (i, 0, 0)),
        ],
        out_specs=pl.BlockSpec((1, rows, 3 * D), lambda i: (i, 0, 0)),
        out_shape=jax.ShapeDtypeStruct((count, rows, 3 * D), BF16),
        cost_estimate=estimate(10 * count * rows * rows * D * 4, count * rows * D * 14, count * rows * rows * HEADS),
        name="enc_attend_back",
    )(joint, grad)


def causal_mask(rows, length):
    row = lax.broadcasted_iota(jnp.int32, (rows, rows), 0)
    column = lax.broadcasted_iota(jnp.int32, (rows, rows), 1)
    return (column <= row) & (column < length)


def self_attend_kernel(length_ref, q_ref, k_ref, v_ref, out_ref):
    allowed = causal_mask(q_ref.shape[0], length_ref[0])
    out_ref[...] = pair_forward(q_ref[...], k_ref[...], v_ref[...], allowed)


def self_attend(joint, lengths):
    rows = joint.shape[0]
    return pl.pallas_call(
        self_attend_kernel,
        grid_spec=pltpu.PrefetchScalarGridSpec(
            num_scalar_prefetch=1,
            grid=(PAIRS,),
            in_specs=[pl.BlockSpec((rows, LANES), lambda p, _, t=t: (0, t * PAIRS + p)) for t in range(3)],
            out_specs=pl.BlockSpec((rows, LANES), lambda p, _: (0, p)),
        ),
        out_shape=jax.ShapeDtypeStruct((rows, D), BF16),
        cost_estimate=estimate(4 * rows * rows * D * 4, rows * D * 8, rows * rows * HEADS),
        name="self_attend",
    )(lengths, joint, joint, joint)


def self_attend_back_kernel(length_ref, q_ref, k_ref, v_ref, grad_ref, dq_ref, dk_ref, dv_ref):
    allowed = causal_mask(q_ref.shape[0], length_ref[0])
    grads = pair_backward(q_ref[...], k_ref[...], v_ref[...], grad_ref[...], allowed)
    dq_ref[...] = grads[0]
    dk_ref[...] = grads[1]
    dv_ref[...] = grads[2]


def self_attend_back(joint, grad, lengths):
    rows = joint.shape[0]
    block = pl.BlockSpec((rows, LANES), lambda p, _: (0, p))
    return pl.pallas_call(
        self_attend_back_kernel,
        grid_spec=pltpu.PrefetchScalarGridSpec(
            num_scalar_prefetch=1,
            grid=(PAIRS,),
            in_specs=[pl.BlockSpec((rows, LANES), lambda p, _, t=t: (0, t * PAIRS + p)) for t in range(3)] + [block],
            out_specs=[block] * 3,
        ),
        out_shape=[jax.ShapeDtypeStruct((rows, D), BF16)] * 3,
        cost_estimate=estimate(10 * rows * rows * D * 4, rows * D * 14, rows * rows * HEADS),
        name="self_attend_back",
    )(lengths, joint, joint, joint, grad)


def cross_attend_kernel(order_ref, asked_ref, first_ref, second_ref, out_ref):
    for p in range(PAIRS):
        keys = jnp.concatenate([first_ref[0, :, col(p, 0)], second_ref[0, :, col(p, 0)]], axis=0)
        values = jnp.concatenate([first_ref[0, :, col(p, 1)], second_ref[0, :, col(p, 1)]], axis=0)
        out_ref[:, col(p)] = pair_forward(asked_ref[:, col(p)], keys, values, None)


def cross_attend(asked, memory, order):
    rows = asked.shape[0]
    count, places, _ = memory.shape
    return pl.pallas_call(
        cross_attend_kernel,
        grid_spec=pltpu.PrefetchScalarGridSpec(
            num_scalar_prefetch=1,
            grid=(rows // CH,),
            in_specs=[
                pl.BlockSpec((CH, D), lambda c, order: (c, 0)),
                pl.BlockSpec((1, places, 2 * D), lambda c, order: (order[2 * c], 0, 0)),
                pl.BlockSpec((1, places, 2 * D), lambda c, order: (order[2 * c + 1], 0, 0)),
            ],
            out_specs=pl.BlockSpec((CH, D), lambda c, order: (c, 0)),
        ),
        out_shape=jax.ShapeDtypeStruct((rows, D), BF16),
        cost_estimate=estimate(4 * rows * 2 * places * D * 4, rows * D * 4 + count * places * D * 4, rows * 2 * places * HEADS),
        name="cross_attend",
    )(order, asked, memory, memory)


def cross_attend_back_kernel(order_ref, asked_ref, first_ref, second_ref, grad_ref, dq_ref, dmem_ref):
    c = pl.program_id(0)
    first, second = order_ref[2 * c], order_ref[2 * c + 1]
    places = first_ref.shape[1]
    for p in range(PAIRS):
        keys = jnp.concatenate([first_ref[0, :, col(p, 0)], second_ref[0, :, col(p, 0)]], axis=0)
        values = jnp.concatenate([first_ref[0, :, col(p, 1)], second_ref[0, :, col(p, 1)]], axis=0)
        dq, dk, dv = pair_backward(asked_ref[:, col(p)], keys, values, grad_ref[:, col(p)], None)
        dq_ref[:, col(p)] = dq
        dmem_ref[first, :, col(p, 0)] = dk[:places]
        dmem_ref[second, :, col(p, 0)] = dk[places:]
        dmem_ref[first, :, col(p, 1)] = dv[:places]
        dmem_ref[second, :, col(p, 1)] = dv[places:]


def cross_attend_back(asked, memory, grad, order):
    rows = asked.shape[0]
    count, places, _ = memory.shape
    return pl.pallas_call(
        cross_attend_back_kernel,
        grid_spec=pltpu.PrefetchScalarGridSpec(
            num_scalar_prefetch=1,
            grid=(rows // CH,),
            in_specs=[
                pl.BlockSpec((CH, D), lambda c, order: (c, 0)),
                pl.BlockSpec((1, places, 2 * D), lambda c, order: (order[2 * c], 0, 0)),
                pl.BlockSpec((1, places, 2 * D), lambda c, order: (order[2 * c + 1], 0, 0)),
                pl.BlockSpec((CH, D), lambda c, order: (c, 0)),
            ],
            out_specs=[
                pl.BlockSpec((CH, D), lambda c, order: (c, 0)),
                pl.BlockSpec((count, places, 2 * D), lambda c, order: (0, 0, 0)),
            ],
        ),
        out_shape=[jax.ShapeDtypeStruct((rows, D), BF16), jax.ShapeDtypeStruct(memory.shape, BF16)],
        cost_estimate=estimate(10 * rows * 2 * places * D * 4, rows * D * 6 + count * places * D * 8, rows * 2 * places * HEADS),
        name="cross_attend_back",
    )(order, asked, memory, memory, grad)


def swap(value, axis, size, mask):
    return lax.ppermute(value, axis, [(i, i ^ mask) for i in range(size)])


def bit_of(axis, mask):
    return (lax.axis_index(axis) // mask) % 2


def pick(value, dim, index):
    return lax.dynamic_index_in_dim(value, index, dim, keepdims=False)


def halve(value, dim, axis, size, mask):
    bit = bit_of(axis, mask)
    arrived = swap(pick(value, dim, 1 - bit), axis, size, mask)
    return (pick(value, dim, bit).astype(F32) + arrived.astype(F32)).astype(BF16)


def join(value, dim, axis, size, mask):
    arrived = swap(value, axis, size, mask)
    bit = bit_of(axis, mask)
    return jnp.where(
        bit == 0, jnp.concatenate([value, arrived], axis=dim), jnp.concatenate([arrived, value], axis=dim)
    )


def masks(size):
    found, mask = [], 1
    while mask < size:
        found.append(mask)
        mask *= 2
    return found


def reduce_group(totals, sizes, rows_first):
    nseq, nnbr = sizes
    core = bit_of("seq", 1)
    parts = []
    for whole in totals:
        height, width = whole.shape
        parts.append(halve(whole.reshape(height, 2, width // 2), 1, "seq", nseq, 1))
    widths = [part.shape[1] for part in parts]
    total = parts[0] if len(parts) == 1 else jnp.concatenate(parts, axis=1)
    bits = masks(nnbr)
    rows = total.shape[0] // nnbr
    total = total.reshape((2,) * len(bits) + (rows, total.shape[1]))
    seq_bits = masks(nseq)[1:]

    def over_seq(total):
        for mask in seq_bits:
            shape = total.shape
            total = total.reshape(shape[:-2] + (2, shape[-2] // 2, shape[-1]))
            total = halve(total, total.ndim - 3, "seq", nseq, mask)
        return total

    def over_nbr(total):
        left = list(reversed(bits))
        for mask in bits:
            total = halve(total, left.index(mask), "nbr", nnbr, mask)
            left.remove(mask)
        return total

    if rows_first:
        total = over_nbr(over_seq(total))
        for mask in reversed(seq_bits):
            total = join(total, 0, "seq", nseq, mask)
    else:
        total = over_nbr(total)
        for mask in seq_bits:
            total = (total.astype(F32) + swap(total, "seq", nseq, mask).astype(F32)).astype(BF16)
    other = swap(total, "seq", nseq, 1)
    results, start = [], 0
    for width in widths:
        mine, theirs = total[:, start : start + width], other[:, start : start + width]
        results.append(
            jnp.where(
                core == 0, jnp.concatenate([mine, theirs], axis=1), jnp.concatenate([theirs, mine], axis=1)
            ).astype(F32)
        )
        start += width
    return results


MESH = pl.DeviceIdType.MESH
HALF = D // 2


def add_into(total, part):
    def one(k, carry):
        total[k] = (total[k].astype(F32) + part[k].astype(F32)).astype(BF16)
        return carry

    lax.fori_loop(0, total.shape[0], one, 0)


def sum_kernel(layout, *refs):
    count = 1 + max(m for group in layout for m, _ in group)
    ins, outs = refs[:count], refs[count : 2 * count]
    own, first, mid, low, end, tail, result, send_sem, recv_sem, load_sem, store_sem = refs[2 * count :]
    s, n = lax.axis_index("seq"), lax.axis_index("nbr")
    c, x = s % 2, s // 2
    y, z1, z2 = n % 2, (n // 2) % 2, n // 4
    at_core, at_x = (s + 1 - 2 * c, n), (s + 2 - 4 * x, n)
    at_y, at_z1, at_z2 = (s, n + 1 - 2 * y), (s, n + 2 - 4 * z1), (s, n + 4 - 8 * z2)
    mine, other = pl.multiple_of(c * HALF, 128), pl.multiple_of((1 - c) * HALF, 128)

    barrier = pltpu.get_barrier_semaphore()
    for partner in (at_core, at_x, at_y, at_z1, at_z2):
        pl.semaphore_signal(barrier, inc=1, device_id=partner, device_id_type=MESH)
    pl.semaphore_wait(barrier, 5)

    pending = {}

    def remote(key, index, src, dst, partner):
        copy = pltpu.make_async_remote_copy(
            src_ref=src,
            dst_ref=dst,
            send_sem=send_sem.at[index],
            recv_sem=recv_sem.at[index],
            device_id=partner,
            device_id_type=MESH,
        )
        copy.start()
        pending[key] = copy

    def source(group, j, lanes):
        matrix, block = layout[group][j]
        ref = ins[matrix]
        if ref.shape[3] != own.shape[5]:
            return ref.at[:, :, :, pl.ds(block * own.shape[5], own.shape[5]), pl.ds(lanes, HALF)]
        return ref.at[:, :, :, :, pl.ds(block * D + lanes, HALF)]

    def target(group, j):
        matrix, block = layout[group][j]
        ref = outs[matrix]
        rows = own.shape[5]
        if ref.shape[0] != rows:
            return ref.at[pl.ds(block * rows, rows)]
        return ref.at[:, pl.ds(block * D, D)]

    def second(group):
        return group % 2 == 0

    def stage0(g):
        for j in range(4):
            remote(("core", g, j), (g, j), source(g, j, other), first.at[g, j], at_core)
            copy = pltpu.make_async_copy(source(g, j, mine), own.at[g, j], load_sem.at[g, j])
            copy.start()
            pending[("load", g, j)] = copy

    def stage1(g):
        for j in range(4):
            pending.pop(("core", g, j)).wait()
            pending.pop(("load", g, j)).wait()
        for j in range(4):
            for a in range(2):
                for b in range(2):
                    add_into(own.at[g, j, a, b], first.at[g, j, a, b])
        remote(("a", g), (g, 4), own.at[g, 1 - x], mid.at[g], at_x)
        remote(("b", g), (g, 5), own.at[g, 2, :, :, 1 - y], low.at[g, 1], at_y)
        if second(g):
            remote(("d", g), (g, 6), own.at[g, 3, :, 1 - z1], low.at[g, 2], at_z1)
        else:
            remote(("d", g), (g, 6), own.at[g, 3, :, :, 1 - y], low.at[g, 2], at_y)

    def stage2(g):
        for key in "abd":
            pending.pop((key, g)).wait()
        for a in range(2):
            for b in range(2):
                add_into(own.at[g, x, a, b], mid.at[g, a, b])
            add_into(own.at[g, 2, a, :, y], low.at[g, 1, a])
            if second(g):
                add_into(own.at[g, 3, a, z1], low.at[g, 2, a])
            else:
                add_into(own.at[g, 3, a, :, y], low.at[g, 2, a])
        remote(("a", g), (g, 7), own.at[g, x, :, :, 1 - y], low.at[g, 0], at_y)
        remote(("b", g), (g, 8), own.at[g, 2, :, 1 - z1, y], end.at[g, 1], at_z1)
        if second(g):
            remote(("d", g), (g, 9), own.at[g, 3, 1 - z2, z1], end.at[g, 2], at_z2)
        else:
            remote(("d", g), (g, 9), own.at[g, 3, :, 1 - z1, y], end.at[g, 2], at_z1)

    def stage3(g):
        for key in "abd":
            pending.pop((key, g)).wait()
        for a in range(2):
            add_into(own.at[g, x, a, :, y], low.at[g, 0, a])
        add_into(own.at[g, 2, :, z1, y], end.at[g, 1])
        if second(g):
            add_into(own.at[g, 3, z2, z1], end.at[g, 2])
        else:
            add_into(own.at[g, 3, :, z1, y], end.at[g, 2])
        remote(("a", g), (g, 10), own.at[g, x, :, 1 - z1, y], end.at[g, 0], at_z1)
        remote(("b", g), (g, 11), own.at[g, 2, 1 - z2, z1, y], tail.at[g, 1], at_z2)
        if second(g):
            remote(("d", g), (g, 12), own.at[g, 3, z2, z1, 1 - y], tail.at[g, 2], at_y)
        else:
            remote(("d", g), (g, 12), own.at[g, 3, 1 - z2, z1, y], tail.at[g, 2], at_z2)

    def stage4(g):
        for key in "abd":
            pending.pop((key, g)).wait()
        add_into(own.at[g, x, :, z1, y], end.at[g, 0])
        for j in (2, 3):
            block = own.at[g, j, z2, z1, y]
            block[...] = (block[...].astype(F32) + tail[g, j - 1].astype(F32)).astype(BF16)
        remote(("a", g), (g, 13), own.at[g, x, 1 - z2, z1, y], tail.at[g, 0], at_z2)
        for j, key in ((2, "b"), (3, "d")):
            remote((key, g), (g, 12 + j), own.at[g, j, z2, z1, y], tail.at[g, 1 + j], at_x)

    def stage5(g):
        for key in "abd":
            pending.pop((key, g)).wait()
        done = own.at[g, x, z2, z1, y]
        result[g, x, :, pl.ds(mine, HALF)] = (done[...].astype(F32) + tail[g, 0].astype(F32)).astype(BF16)
        for j in (2, 3):
            block = own.at[g, j, z2, z1, y]
            result[g, j, :, pl.ds(mine, HALF)] = (block[...].astype(F32) + tail[g, 1 + j].astype(F32)).astype(BF16)
        part = result.at[g, x, :, pl.ds(mine, HALF)]
        remote(("a", g), (g, 16), part, part, at_x)

    def stage6(g):
        pending.pop(("a", g)).wait()
        part = result.at[g, :, :, pl.ds(mine, HALF)]
        remote(("a", g), (g, 17), part, part, at_core)

    def stage7(g):
        pending.pop(("a", g)).wait()
        for j in range(4):
            copy = pltpu.make_async_copy(result.at[g, j], target(g, j), store_sem.at[g, j])
            copy.start()
            pending[("store", g, j)] = copy

    def stage8(g):
        for j in range(4):
            pending.pop(("store", g, j)).wait()

    stages = [stage0, stage1, stage2, stage3, stage4, stage5, stage6, stage7, stage8]
    for tick in range(len(layout) + len(stages) - 1):
        for level in reversed(range(len(stages))):
            if 0 <= tick - level < len(layout):
                stages[level](tick - level)


def sum_all(matrices, layout, sizes):
    nseq, nnbr = sizes
    rows = D // nnbr
    groups = len(layout)
    cut = (2, 2, 2)
    operands = [m.reshape(cut + (m.shape[0] // nnbr, m.shape[1])) for m in matrices]
    anywhere = pl.BlockSpec(memory_space=pl.ANY)
    return pl.pallas_call(
        partial(sum_kernel, layout),
        in_specs=[anywhere] * len(matrices),
        out_specs=[anywhere] * len(matrices),
        out_shape=[jax.ShapeDtypeStruct((m.shape[0] // nnbr, m.shape[1]), BF16) for m in matrices],
        scratch_shapes=[
            pltpu.VMEM((groups, 4) + cut + (rows, HALF), BF16),
            pltpu.VMEM((groups, 4) + cut + (rows, HALF), BF16),
            pltpu.VMEM((groups,) + cut + (rows, HALF), BF16),
            pltpu.VMEM((groups, 3, 2, 2, rows, HALF), BF16),
            pltpu.VMEM((groups, 3, 2, rows, HALF), BF16),
            pltpu.VMEM((groups, 5, rows, HALF), BF16),
            pltpu.VMEM((groups, 4, rows, D), BF16),
            pltpu.SemaphoreType.DMA((groups, 18)),
            pltpu.SemaphoreType.DMA((groups, 18)),
            pltpu.SemaphoreType.DMA((groups, 4)),
            pltpu.SemaphoreType.DMA((groups, 4)),
        ],
        compiler_params=pltpu.CompilerParams(
            collective_id=0, has_side_effects=True, vmem_limit_bytes=62 * 2**20
        ),
        cost_estimate=estimate(sum(m.size for m in matrices) * 2, sum(m.size for m in matrices) * 4),
        name="sum_all",
    )(*operands)


def gain_grad(gain, weight, grad, nnbr):
    rows = weight.shape[0] // nnbr
    start = lax.axis_index("nbr") * rows
    own = lax.dynamic_slice_in_dim(weight, start, rows, 0).astype(F32)
    return jnp.sum(own * grad, axis=1) / lax.dynamic_slice_in_dim(gain, start, rows, 0)


GROUPS = (
    tuple((0, j) for j in range(4)),
    tuple((1, j) for j in range(4)),
    ((2, 0), (3, 0), (4, 0), (4, 1)),
    ((5, 0), (6, 0), (6, 1), (6, 2)),
    tuple((7, j) for j in range(4)),
    tuple((8, j) for j in range(4)),
    ((9, 0), (10, 0), (10, 1), (10, 2)),
)


def body(
    sizes,
    tokens,
    neighbours,
    out_grad,
    lengths,
    slot_order,
    selfgain,
    selfjoint,
    selfmerge,
    crossgain,
    crossquery,
    crossmerge,
    feedgain,
    feedup,
    feeddown,
    codergain,
    coderjoint,
    codermerge,
    codermid,
    coderup,
    coderdown,
    codertop,
    memorymap,
):
    nseq, nnbr = sizes
    me = lax.axis_index("seq")
    count, places, _ = neighbours.shape
    cap = count // nseq
    flat = count * places

    ordered = jnp.concatenate(
        [lax.dynamic_slice_in_dim(neighbours, (me ^ m) * cap, cap, 0) for m in range(nseq)], axis=0
    )
    embedded = ordered.reshape(flat, D).astype(F32)
    enc_normed, _, _ = norm_forward(embedded, codergain)
    enc_joint = times(enc_normed, coderjoint).astype(BF16).reshape(count, places, 3 * D)
    enc_mixed = enc_attend(enc_joint).reshape(flat, D)
    enc_middle = embedded + times(enc_mixed, codermerge)
    enc_normed_b, enc_plain_b, enc_inverse_b = norm_forward(enc_middle, codermid)
    enc_rising = times(enc_normed_b, coderup)
    enc_hidden = jax.nn.gelu(enc_rising, approximate=True).astype(BF16)
    enc_upper = enc_middle + times(enc_hidden, coderdown)
    enc_normed_c, enc_plain_c, enc_inverse_c = norm_forward(enc_upper, codertop)
    blocks = enc_normed_c.reshape(nseq, cap * places, D)
    received = jnp.concatenate(
        [blocks[m] if m == 0 else swap(blocks[m], "seq", nseq, m) for m in range(nseq)], axis=0
    )

    sequence = tokens[0].astype(F32)
    rows = sequence.shape[0]
    normed_a, plain_a, inverse_a = norm_forward(sequence, selfgain)
    joint = times(normed_a, selfjoint).astype(BF16)
    mixed = self_attend(joint, lengths)
    after_self = sequence + times(mixed, selfmerge)
    normed_b, plain_b, inverse_b = norm_forward(after_self, crossgain)
    asked = times(normed_b, crossquery).astype(BF16)

    memory = times(received, memorymap).astype(BF16).reshape(count, places, 2 * D)
    order = slot_order[0]
    order = ((order // cap) ^ me) * cap + order % cap
    crossed = cross_attend(asked, memory, order)
    live = (jnp.arange(rows, dtype=jnp.int32) // CH * CH < lengths[0]).astype(F32)[:, None]
    after_cross = after_self + times(crossed, crossmerge) * live
    normed_c, plain_c, inverse_c = norm_forward(after_cross, feedgain)
    rising = times(normed_c, feedup)
    hidden = jax.nn.gelu(rising, approximate=True).astype(BF16)
    output = (after_cross + times(hidden, feeddown)).astype(BF16)[None]

    down_in = out_grad[0]
    rising_grad = curve_grad(rising, times_back(down_in, feeddown)).astype(BF16)
    cross_total = down_in.astype(F32) + norm_backward(times_back(rising_grad, feedup), plain_c, inverse_c, feedgain)
    cross_in = (cross_total * live).astype(BF16)
    crossed_grad = times_back(cross_in, crossmerge).astype(BF16)
    asked_grad, memory_grad = cross_attend_back(asked, memory, crossed_grad, order)
    memory_grad = memory_grad.reshape(flat, 2 * D)
    back = times_back(memory_grad, memorymap).astype(BF16).reshape(nseq, cap * places, D)
    returned = jnp.concatenate(
        [back[m] if m == 0 else swap(back[m], "seq", nseq, m) for m in range(nseq)], axis=0
    ).astype(F32)
    self_total = cross_total + norm_backward(times_back(asked_grad, crossquery), plain_b, inverse_b, crossgain)
    self_in = self_total.astype(BF16)
    mixed_grad = times_back(self_in, selfmerge).astype(BF16)
    joint_grad = jnp.concatenate(self_attend_back(joint, mixed_grad, lengths), axis=1)
    input_grad = (self_total + norm_backward(times_back(joint_grad, selfjoint), plain_a, inverse_a, selfgain))[None]

    upper_total = norm_backward(returned, enc_plain_c, enc_inverse_c, codertop)
    enc_down_in = upper_total.astype(BF16)
    enc_rising_grad = curve_grad(enc_rising, times_back(enc_down_in, coderdown)).astype(BF16)
    middle_total = upper_total + norm_backward(
        times_back(enc_rising_grad, coderup), enc_plain_b, enc_inverse_b, codermid
    )
    enc_merge_in = middle_total.astype(BF16)
    enc_mixed_grad = times_back(enc_merge_in, codermerge).astype(BF16).reshape(count, places, D)
    enc_joint_grad = enc_attend_back(enc_joint, enc_mixed_grad).reshape(flat, 3 * D)

    pairs = [
        (hidden, down_in),
        (normed_c, rising_grad),
        (crossed, cross_in),
        (normed_b, asked_grad),
        (received, memory_grad),
        (mixed, self_in),
        (normed_a, joint_grad),
        (enc_hidden, enc_down_in),
        (enc_normed_b, enc_rising_grad),
        (enc_mixed, enc_merge_in),
        (enc_normed, enc_joint_grad),
    ]
    sums = [weight_grad(values, grad).astype(BF16) for values, grad in pairs]
    if nseq == 4 and nnbr == 8:
        sums = sum_all(sums, GROUPS, sizes)
    else:
        ways = (False, True, False, False, False, False, False, True, False, True, True)
        sums = [reduce_group([total], sizes, way)[0] for total, way in zip(sums, ways)]
    (
        grad_feeddown,
        grad_feedup,
        grad_crossmerge,
        grad_crossquery,
        grad_memorymap,
        grad_selfmerge,
        grad_selfjoint,
        grad_coderdown,
        grad_coderup,
        grad_codermerge,
        grad_coderjoint,
    ) = [total.astype(F32) for total in sums]
    return (
        output,
        input_grad,
        gain_grad(selfgain, selfjoint, grad_selfjoint, nnbr),
        grad_selfjoint,
        grad_selfmerge,
        gain_grad(crossgain, crossquery, grad_crossquery, nnbr),
        grad_crossquery,
        grad_crossmerge,
        gain_grad(feedgain, feedup, grad_feedup, nnbr),
        grad_feedup,
        grad_feeddown,
        gain_grad(codergain, coderjoint, grad_coderjoint, nnbr),
        grad_coderjoint,
        grad_codermerge,
        gain_grad(codermid, coderup, grad_coderup, nnbr),
        grad_coderup,
        grad_coderdown,
        gain_grad(codertop, memorymap, grad_memorymap, nnbr),
        grad_memorymap,
    )


def solution(mesh):
    spread = ("seq", "nbr")
    sizes = (mesh.shape["seq"], mesh.shape["nbr"])
    placed = (
        P(spread, None, None),
        P(spread, None, None),
        P(spread, None, None),
        P(spread),
        P(spread, None),
    ) + (P(),) * 17
    gain, weight = P("nbr"), P("nbr", None)
    return jax.shard_map(
        partial(body, sizes),
        mesh=mesh,
        in_specs=placed,
        out_specs=(
            P(spread, None, None),
            P(spread, None, None),
            gain,
            weight,
            weight,
            gain,
            weight,
            weight,
            gain,
            weight,
            weight,
            gain,
            weight,
            weight,
            gain,
            weight,
            weight,
            gain,
            weight,
        ),
        check_vma=False,
    )
```

```python
from functools import partial

import jax
import jax.numpy as jnp
from jax import lax
from jax.experimental import pallas as pl
from jax.experimental.pallas import tpu as pltpu
from jax.sharding import PartitionSpec as P

D = 768
HEADS = 12
HD = 64
CH = 64
PAIRS = HEADS // 2
LANES = 2 * HD
SCALE = HD ** (-0.5)
F32 = jnp.float32
BF16 = jnp.bfloat16


def norm_forward(values, gain):
    centred = values - jnp.mean(values, axis=-1, keepdims=True)
    inverse = lax.rsqrt(jnp.mean(centred * centred, axis=-1, keepdims=True) + 1e-05)
    normed = centred * inverse
    return ((normed * gain).astype(BF16), normed, inverse)


def norm_backward(grad, normed, inverse, gain):
    scaled = grad * gain
    inner = jnp.mean(scaled * normed, axis=-1, keepdims=True)
    return inverse * (scaled - jnp.mean(scaled, axis=-1, keepdims=True) - normed * inner)


def times(values, weight):
    return lax.dot_general(values, weight, (((1,), (0,)), ((), ())), preferred_element_type=F32)


def times_back(grad, weight):
    return lax.dot_general(grad, weight, (((1,), (1,)), ((), ())), preferred_element_type=F32)


def weight_grad(values, grad):
    return lax.dot_general(values, grad, (((0,), (0,)), ((), ())), preferred_element_type=F32)


def curve(rising):
    square = rising * rising
    bend = jnp.tanh(rising * (0.7978845608028654 + 0.035677408136300125 * square))
    half = 0.5 * (1.0 + bend)
    slope = half + 0.5 * rising * (1.0 - bend * bend) * (0.7978845608028654 + 0.10703222440890037 * square)
    return (rising * half).astype(BF16), slope.astype(BF16)


def dot_nt(a, b):
    return lax.dot_general(a, b, (((1,), (1,)), ((), ())), preferred_element_type=F32)


def dot_nn(a, b):
    return lax.dot_general(a, b, (((1,), (0,)), ((), ())), preferred_element_type=F32)


def dot_tn(a, b):
    return lax.dot_general(a, b, (((0,), (0,)), ((), ())), preferred_element_type=F32)


def stack_pair(block):
    lane = lax.broadcasted_iota(jnp.int32, block.shape, 1)
    zero = jnp.zeros_like(block)
    return jnp.concatenate([jnp.where(lane < HD, block, zero), jnp.where(lane >= HD, block, zero)], axis=0)


def unstack_pair(stacked):
    half = stacked.shape[0] // 2
    lane = lax.broadcasted_iota(jnp.int32, (half, LANES), 1)
    return jnp.where(lane < HD, stacked[:half], stacked[half:])


def softmax_halves(products, allowed):
    width = products.shape[1] // 2
    parts = []
    for h in range(2):
        scores = products[:, h * width : (h + 1) * width] * SCALE
        if allowed is not None:
            scores = jnp.where(allowed, scores, -1000000000.0)
        exponent = jnp.exp(scores - jnp.max(scores, axis=-1, keepdims=True))
        parts.append(exponent * (1.0 / jnp.sum(exponent, axis=-1, keepdims=True)))
    return parts


def pair_forward(queries, keys, values, allowed):
    probs = softmax_halves(dot_nt(queries, stack_pair(keys)), allowed)
    probs = jnp.concatenate([p.astype(BF16) for p in probs], axis=1)
    return dot_nn(probs, stack_pair(values)).astype(BF16)


def pair_backward(queries, keys, values, outgoing, allowed):
    keys2 = stack_pair(keys)
    probs = softmax_halves(dot_nt(queries, keys2), allowed)
    rounded = jnp.concatenate([p.astype(BF16) for p in probs], axis=1)
    value_grad = unstack_pair(dot_tn(rounded, outgoing))
    prob_grad = dot_nt(outgoing, stack_pair(values))
    width = prob_grad.shape[1] // 2
    parts = []
    for h in range(2):
        part = prob_grad[:, h * width : (h + 1) * width]
        inner = jnp.sum(probs[h] * part, axis=-1, keepdims=True)
        parts.append((probs[h] * (part - inner) * SCALE).astype(BF16))
    score_grad = jnp.concatenate(parts, axis=1)
    query_grad = dot_nn(score_grad, keys2)
    key_grad = unstack_pair(dot_tn(score_grad, queries))
    return query_grad.astype(BF16), key_grad.astype(BF16), value_grad.astype(BF16)


def col(pair, third=0):
    return slice(third * D + pair * LANES, third * D + (pair + 1) * LANES)


def estimate(flops, nbytes, exps=0):
    return pl.CostEstimate(flops=int(flops), bytes_accessed=int(nbytes), transcendentals=int(exps))


def enc_attend_kernel(joint_ref, mixed_ref):
    for p in range(PAIRS):
        mixed_ref[0, :, col(p)] = pair_forward(
            joint_ref[0, :, col(p, 0)], joint_ref[0, :, col(p, 1)], joint_ref[0, :, col(p, 2)], None
        )


def enc_attend(joint):
    count, rows, _ = joint.shape
    return pl.pallas_call(
        enc_attend_kernel,
        grid=(count,),
        in_specs=[pl.BlockSpec((1, rows, 3 * D), lambda i: (i, 0, 0))],
        out_specs=pl.BlockSpec((1, rows, D), lambda i: (i, 0, 0)),
        out_shape=jax.ShapeDtypeStruct((count, rows, D), BF16),
        cost_estimate=estimate(4 * count * rows * rows * D * 4, count * rows * D * 8, count * rows * rows * HEADS),
        name="enc_attend",
    )(joint)


def enc_attend_back_kernel(joint_ref, grad_ref, out_ref):
    for p in range(PAIRS):
        grads = pair_backward(
            joint_ref[0, :, col(p, 0)], joint_ref[0, :, col(p, 1)], joint_ref[0, :, col(p, 2)], grad_ref[0, :, col(p)], None
        )
        for third in range(3):
            out_ref[0, :, col(p, third)] = grads[third]


def enc_attend_back(joint, grad):
    count, rows, _ = joint.shape
    return pl.pallas_call(
        enc_attend_back_kernel,
        grid=(count,),
        in_specs=[
            pl.BlockSpec((1, rows, 3 * D), lambda i: (i, 0, 0)),
            pl.BlockSpec((1, rows, D), lambda i: (i, 0, 0)),
        ],
        out_specs=pl.BlockSpec((1, rows, 3 * D), lambda i: (i, 0, 0)),
        out_shape=jax.ShapeDtypeStruct((count, rows, 3 * D), BF16),
        cost_estimate=estimate(10 * count * rows * rows * D * 4, count * rows * D * 14, count * rows * rows * HEADS),
        name="enc_attend_back",
    )(joint, grad)


def causal_mask(rows, length):
    row = lax.broadcasted_iota(jnp.int32, (rows, rows), 0)
    column = lax.broadcasted_iota(jnp.int32, (rows, rows), 1)
    return (column <= row) & (column < length)


def self_attend_kernel(length_ref, q_ref, k_ref, v_ref, out_ref):
    allowed = causal_mask(q_ref.shape[0], length_ref[0])
    out_ref[...] = pair_forward(q_ref[...], k_ref[...], v_ref[...], allowed)


def self_attend(joint, lengths):
    rows = joint.shape[0]
    return pl.pallas_call(
        self_attend_kernel,
        grid_spec=pltpu.PrefetchScalarGridSpec(
            num_scalar_prefetch=1,
            grid=(PAIRS,),
            in_specs=[pl.BlockSpec((rows, LANES), lambda p, _, t=t: (0, t * PAIRS + p)) for t in range(3)],
            out_specs=pl.BlockSpec((rows, LANES), lambda p, _: (0, p)),
        ),
        out_shape=jax.ShapeDtypeStruct((rows, D), BF16),
        cost_estimate=estimate(4 * rows * rows * D * 4, rows * D * 8, rows * rows * HEADS),
        name="self_attend",
    )(lengths, joint, joint, joint)


def self_attend_back_kernel(length_ref, q_ref, k_ref, v_ref, grad_ref, out_ref):
    allowed = causal_mask(q_ref.shape[0], length_ref[0])
    grads = pair_backward(q_ref[...], k_ref[...], v_ref[...], grad_ref[...], allowed)
    for third in range(3):
        begin = pl.multiple_of((third * PAIRS + pl.program_id(0)) * LANES, LANES)
        out_ref[:, pl.ds(begin, LANES)] = grads[third]


def self_attend_back(joint, grad, lengths):
    rows = joint.shape[0]
    block = pl.BlockSpec((rows, LANES), lambda p, _: (0, p))
    return pl.pallas_call(
        self_attend_back_kernel,
        grid_spec=pltpu.PrefetchScalarGridSpec(
            num_scalar_prefetch=1,
            grid=(PAIRS,),
            in_specs=[pl.BlockSpec((rows, LANES), lambda p, _, t=t: (0, t * PAIRS + p)) for t in range(3)] + [block],
            out_specs=pl.BlockSpec((rows, 3 * D), lambda p, _: (0, 0)),
        ),
        out_shape=jax.ShapeDtypeStruct((rows, 3 * D), BF16),
        cost_estimate=estimate(10 * rows * rows * D * 4, rows * D * 14, rows * rows * HEADS),
        name="self_attend_back",
    )(lengths, joint, joint, joint, grad)


def cross_attend_kernel(order_ref, asked_ref, first_ref, second_ref, out_ref):
    for p in range(PAIRS):
        keys = jnp.concatenate([first_ref[0, :, col(p, 0)], second_ref[0, :, col(p, 0)]], axis=0)
        values = jnp.concatenate([first_ref[0, :, col(p, 1)], second_ref[0, :, col(p, 1)]], axis=0)
        out_ref[:, col(p)] = pair_forward(asked_ref[:, col(p)], keys, values, None)


def cross_attend(asked, memory, order):
    rows = asked.shape[0]
    count, places, _ = memory.shape
    return pl.pallas_call(
        cross_attend_kernel,
        grid_spec=pltpu.PrefetchScalarGridSpec(
            num_scalar_prefetch=1,
            grid=(rows // CH,),
            in_specs=[
                pl.BlockSpec((CH, D), lambda c, order: (c, 0)),
                pl.BlockSpec((1, places, 2 * D), lambda c, order: (order[2 * c], 0, 0)),
                pl.BlockSpec((1, places, 2 * D), lambda c, order: (order[2 * c + 1], 0, 0)),
            ],
            out_specs=pl.BlockSpec((CH, D), lambda c, order: (c, 0)),
        ),
        out_shape=jax.ShapeDtypeStruct((rows, D), BF16),
        cost_estimate=estimate(4 * rows * 2 * places * D * 4, rows * D * 4 + count * places * D * 4, rows * 2 * places * HEADS),
        name="cross_attend",
    )(order, asked, memory, memory)


def cross_attend_back_kernel(order_ref, asked_ref, first_ref, second_ref, grad_ref, dq_ref, dmem_ref):
    c = pl.program_id(0)
    first, second = order_ref[2 * c], order_ref[2 * c + 1]
    places = first_ref.shape[1]
    for p in range(PAIRS):
        keys = jnp.concatenate([first_ref[0, :, col(p, 0)], second_ref[0, :, col(p, 0)]], axis=0)
        values = jnp.concatenate([first_ref[0, :, col(p, 1)], second_ref[0, :, col(p, 1)]], axis=0)
        dq, dk, dv = pair_backward(asked_ref[:, col(p)], keys, values, grad_ref[:, col(p)], None)
        dq_ref[:, col(p)] = dq
        dmem_ref[first, :, col(p, 0)] = dk[:places]
        dmem_ref[second, :, col(p, 0)] = dk[places:]
        dmem_ref[first, :, col(p, 1)] = dv[:places]
        dmem_ref[second, :, col(p, 1)] = dv[places:]


def cross_attend_back(asked, memory, grad, order):
    rows = asked.shape[0]
    count, places, _ = memory.shape
    return pl.pallas_call(
        cross_attend_back_kernel,
        grid_spec=pltpu.PrefetchScalarGridSpec(
            num_scalar_prefetch=1,
            grid=(rows // CH,),
            in_specs=[
                pl.BlockSpec((CH, D), lambda c, order: (c, 0)),
                pl.BlockSpec((1, places, 2 * D), lambda c, order: (order[2 * c], 0, 0)),
                pl.BlockSpec((1, places, 2 * D), lambda c, order: (order[2 * c + 1], 0, 0)),
                pl.BlockSpec((CH, D), lambda c, order: (c, 0)),
            ],
            out_specs=[
                pl.BlockSpec((CH, D), lambda c, order: (c, 0)),
                pl.BlockSpec((count, places, 2 * D), lambda c, order: (0, 0, 0)),
            ],
        ),
        out_shape=[jax.ShapeDtypeStruct((rows, D), BF16), jax.ShapeDtypeStruct(memory.shape, BF16)],
        cost_estimate=estimate(10 * rows * 2 * places * D * 4, rows * D * 6 + count * places * D * 8, rows * 2 * places * HEADS),
        name="cross_attend_back",
    )(order, asked, memory, memory, grad)


def swap(value, axis, size, mask):
    return lax.ppermute(value, axis, [(i, i ^ mask) for i in range(size)])


def bit_of(axis, mask):
    return (lax.axis_index(axis) // mask) % 2


def pick(value, dim, index):
    return lax.dynamic_index_in_dim(value, index, dim, keepdims=False)


def halve(value, dim, axis, size, mask):
    bit = bit_of(axis, mask)
    arrived = swap(pick(value, dim, 1 - bit), axis, size, mask)
    return (pick(value, dim, bit).astype(F32) + arrived.astype(F32)).astype(BF16)


def join(value, dim, axis, size, mask):
    arrived = swap(value, axis, size, mask)
    bit = bit_of(axis, mask)
    return jnp.where(
        bit == 0, jnp.concatenate([value, arrived], axis=dim), jnp.concatenate([arrived, value], axis=dim)
    )


def masks(size):
    found, mask = [], 1
    while mask < size:
        found.append(mask)
        mask *= 2
    return found


def reduce_group(totals, sizes, rows_first):
    nseq, nnbr = sizes
    core = bit_of("seq", 1)
    parts = []
    for whole in totals:
        height, width = whole.shape
        parts.append(halve(whole.reshape(height, 2, width // 2), 1, "seq", nseq, 1))
    widths = [part.shape[1] for part in parts]
    total = parts[0] if len(parts) == 1 else jnp.concatenate(parts, axis=1)
    bits = masks(nnbr)
    rows = total.shape[0] // nnbr
    total = total.reshape((2,) * len(bits) + (rows, total.shape[1]))
    seq_bits = masks(nseq)[1:]

    def over_seq(total):
        for mask in seq_bits:
            shape = total.shape
            total = total.reshape(shape[:-2] + (2, shape[-2] // 2, shape[-1]))
            total = halve(total, total.ndim - 3, "seq", nseq, mask)
        return total

    def over_nbr(total):
        left = list(reversed(bits))
        for mask in bits:
            total = halve(total, left.index(mask), "nbr", nnbr, mask)
            left.remove(mask)
        return total

    if rows_first:
        total = over_nbr(over_seq(total))
        for mask in reversed(seq_bits):
            total = join(total, 0, "seq", nseq, mask)
    else:
        total = over_nbr(total)
        for mask in seq_bits:
            total = (total.astype(F32) + swap(total, "seq", nseq, mask).astype(F32)).astype(BF16)
    other = swap(total, "seq", nseq, 1)
    results, start = [], 0
    for width in widths:
        mine, theirs = total[:, start : start + width], other[:, start : start + width]
        results.append(
            jnp.where(
                core == 0, jnp.concatenate([mine, theirs], axis=1), jnp.concatenate([theirs, mine], axis=1)
            ).astype(F32)
        )
        start += width
    return results


MESH = pl.DeviceIdType.MESH
HALF = D // 2


def norm_back_tile(grad, normed, inverse, gain):
    scaled = grad * gain
    inner = jnp.mean(scaled * normed, axis=-1, keepdims=True)
    return inverse * (scaled - jnp.mean(scaled, axis=-1, keepdims=True) - normed * inner)


MATRICES = 11
DOWN = (0, 7)
UNITS = (
    ((0, 0), (0, 1)),
    ((0, 2), (0, 3)),
    ((1, 0), (1, 1)),
    ((1, 2), (1, 3)),
    ((2, 0), (3, 0)),
    ((4, 0), (4, 1)),
    ((5, 0), (6, 0)),
    ((6, 1), (6, 2)),
    ((7, 0), (7, 1)),
    ((7, 2), (7, 3)),
    ((8, 0), (8, 1)),
    ((8, 2), (8, 3)),
    ((9, 0), (10, 0)),
    ((10, 1), (10, 2)),
)
CARRIED = {
    0: ("rows", 0),
    2: ("rows", 1),
    3: ("heads", 0),
    4: ("rows", 2),
    5: ("heads", 1),
    6: ("rows", 3),
    8: ("heads", 2),
    9: ("heads", 3),
}
TILE = 256


def backward_kernel(blocks, *refs):
    refs = list(refs)

    def take(number):
        taken = refs[:number]
        del refs[:number]
        return taken

    returned = take(blocks)
    plain_c, inverse_c, slope, plain_b, inverse_b, joint = take(6)
    gain_c, gain_b = take(2)
    coderdown, coderup, codermerge = take(3)
    values = take(MATRICES)
    grads = take(7)
    outs = take(MATRICES)
    (
        stage, first, own, mid, low_a, end_a, tail_a, low_b, end_b, tail_b, low_d, end_d, tail_d, tail_x, result,
        down_w, wide, merge_w, rising_grad, down_in, merge_in, joint_grad, mixed_grad,
        y_in, plain_in, inverse_in, slope_in, plain_in_b, inverse_in_b, joint_in, upper,
        feed_a, some_a, some_b,
        send_sem, recv_sem, local_sem,
    ) = refs
    rows = D // 8
    part = rows // 2
    flat = blocks * TILE
    s, n = lax.axis_index("seq"), lax.axis_index("nbr")
    c, x = s % 2, s // 2
    y, z1, z2 = n % 2, (n // 2) % 2, n // 4
    at_core, at_x = (s + 1 - 2 * c, n), (s + 2 - 4 * x, n)
    at_y, at_z1, at_z2 = (s, n + 1 - 2 * y), (s, n + 2 - 4 * z1), (s, n + 4 - 8 * z2)
    mine = pl.ds(pl.multiple_of(c * HALF, 128), HALF)
    other = pl.ds(pl.multiple_of((1 - c) * HALF, 128), HALF)
    kept = pl.ds(pl.multiple_of(x * part, 16), part)
    given = pl.ds(pl.multiple_of((1 - x) * part, 16), part)

    barrier = pltpu.get_barrier_semaphore()
    for partner in (at_core, at_x, at_y, at_z1, at_z2):
        pl.semaphore_signal(barrier, inc=1, device_id=partner, device_id_type=MESH)
    pl.semaphore_wait(barrier, 5)

    pending = {}
    counts = {"local": 0, "remote": 0}

    def remote(key, src, dst, partner):
        index = counts["remote"]
        counts["remote"] += 1
        copy = pltpu.make_async_remote_copy(
            src_ref=src,
            dst_ref=dst,
            send_sem=send_sem.at[index],
            recv_sem=recv_sem.at[index],
            device_id=partner,
            device_id_type=MESH,
        )
        copy.start()
        pending[key] = copy

    def local(key, src, dst):
        copy = pltpu.make_async_copy(src, dst, local_sem.at[counts["local"]])
        counts["local"] += 1
        copy.start()
        pending.setdefault(key, []).append(copy)

    def arrived(key):
        for copy in pending.pop(key, []):
            copy.wait()


    def fetch(u):
        if u == 0:
            local(("unit", 0), values[0], feed_a)
            local(("unit", 0), grads[0], some_b.at[pl.ds(0, TILE), pl.ds(0, D)])
        elif u in (2, 3):
            if u == 2:
                local(("unit", u), values[1], some_a.at[pl.ds(0, TILE)])
            local(("unit", u), grads[1].at[:, pl.ds((u - 2) * 2 * D, 2 * D)], some_b.at[pl.ds(0, TILE)])
        elif u == 4:
            for k in range(2):
                local(("unit", u), values[2 + k], some_a.at[pl.ds(k * TILE, TILE)])
                local(("unit", u), grads[2 + k], some_b.at[pl.ds(0, TILE), pl.ds(k * D, D)])
        elif u == 5:
            local(("unit", u), values[4], some_a)
            local(("unit", u), grads[4], some_b)
        elif u == 6:
            for k in range(2):
                local(("unit", u), values[5 + k], some_a.at[pl.ds(k * TILE, TILE)])
            local(("unit", u), grads[5], some_b.at[pl.ds(0, TILE), pl.ds(0, D)])
            local(("unit", u), grads[6].at[:, pl.ds(0, D)], some_b.at[pl.ds(0, TILE), pl.ds(D, D)])
        elif u == 7:
            local(("unit", u), grads[6].at[:, pl.ds(D, 2 * D)], some_b.at[pl.ds(0, TILE)])
        elif u == 8:
            local(("unit", 8), values[7], wide)
            for k in range(3):
                local(("unit", 10), values[8 + k], down_w.at[pl.ds(k * flat, flat)])

    def operands(u, k):
        left = pl.ds(k * D, D)
        if u in (2, 3):
            return some_a.at[pl.ds(0, TILE)], some_b.at[pl.ds(0, TILE), left]
        if u in (4, 6):
            return some_a.at[pl.ds(k * TILE, TILE)], some_b.at[pl.ds(0, TILE), left]
        if u == 5:
            return some_a, some_b.at[:, left]
        if u == 7:
            return some_a.at[pl.ds(TILE, TILE)], some_b.at[pl.ds(0, TILE), left]
        if u in (10, 11):
            return down_w.at[pl.ds(0, flat)], rising_grad.at[:, pl.ds(((u - 10) * 2 + k) * D, D)]
        if u == 12:
            return down_w.at[pl.ds((1 + k) * flat, flat)], merge_in if k == 0 else joint_grad.at[:, pl.ds(0, D)]
        return down_w.at[pl.ds(2 * flat, flat)], joint_grad.at[:, pl.ds((1 + k) * D, D)]

    def product(u):
        if UNITS[u][0][0] in DOWN:
            left = feed_a if u < 2 else wide
            right = some_b.at[pl.ds(0, TILE), pl.ds(0, D)] if u < 2 else down_in
            begin = (u % 2) * 2 * rows

            def one(shard, carry):
                columns = left[:, pl.ds(pl.multiple_of(shard * 4 * rows, 128), 4 * rows)]
                tile = dot_tn(columns[:, begin : begin + 2 * rows], right[...]).astype(BF16)
                stage[0, shard] = tile[:rows]
                stage[1, shard] = tile[rows:]
                return carry

            lax.fori_loop(0, 8, one, 0)
            return
        for k in range(2):
            left, right = operands(u, k)
            for half in range(2):
                lanes = slice(half * HALF, (half + 1) * HALF)
                tile = dot_tn(left[...], right[:, lanes]).astype(BF16)
                stage[k, :, :, lanes] = tile.reshape(8, rows, HALF)


    def slot(u):
        return u % 4, u % 2, (u // 2) % 2

    def straight(u):
        return u % 4 != 0

    def stage0(u):
        arrived(("unit", u))
        product(u)
        _, two, _ = slot(u)
        remote(("core", u), stage.at[:, :, :, other], first.at[two], at_core)

    def stage1(u):
        four, two, alt = slot(u)
        pending.pop(("core", u)).wait()

        def one(k, carry):
            k, a, b, d = k // 8, (k // 4) % 2, (k // 2) % 2, k % 2
            shard = 4 * a + 2 * b + d
            own[four, k, a, b, d] = stage[k, shard, :, mine] + first[two, k, shard]
            return carry

        lax.fori_loop(0, 16, one, 0)
        remote(("a", u), own.at[four, 0, :, :, :, given], mid.at[two], at_x)
        if straight(u):
            remote(("b", u), own.at[four, 1, :, :, 1 - y], low_b.at[two], at_y)
        else:
            remote(("b", u), own.at[four, 1, :, 1 - z1], low_d.at[alt], at_z1)

    def stage2(u):
        four, two, alt = slot(u)
        pending.pop(("a", u)).wait()
        pending.pop(("b", u)).wait()
        for a in range(2):
            for b in range(2):
                for d in range(2):
                    own[four, 0, a, b, d, kept] = own[four, 0, a, b, d, kept] + mid[two, a, b, d]
        for a in range(2):
            for b in range(2):
                if straight(u):
                    own[four, 1, a, b, y] = own[four, 1, a, b, y] + low_b[two, a, b]
                else:
                    own[four, 1, a, z1, b] = own[four, 1, a, z1, b] + low_d[alt, a, b]
        remote(("a", u), own.at[four, 0, :, :, 1 - y, kept], low_a.at[two], at_y)
        if straight(u):
            remote(("b", u), own.at[four, 1, :, 1 - z1, y], end_b.at[two], at_z1)
        else:
            remote(("b", u), own.at[four, 1, 1 - z2, z1], end_d.at[alt], at_z2)

    def stage3(u):
        four, two, alt = slot(u)
        pending.pop(("a", u)).wait()
        pending.pop(("b", u)).wait()
        for a in range(2):
            for b in range(2):
                own[four, 0, a, b, y, kept] = own[four, 0, a, b, y, kept] + low_a[two, a, b]
            if straight(u):
                own[four, 1, a, z1, y] = own[four, 1, a, z1, y] + end_b[two, a]
            else:
                own[four, 1, z2, z1, a] = own[four, 1, z2, z1, a] + end_d[alt, a]
        remote(("a", u), own.at[four, 0, :, 1 - z1, y, kept], end_a.at[two], at_z1)
        if straight(u):
            remote(("b", u), own.at[four, 1, 1 - z2, z1, y], tail_b.at[two], at_z2)
        else:
            remote(("b", u), own.at[four, 1, z2, z1, 1 - y], tail_d.at[alt], at_y)

    def stage4(u):
        four, two, alt = slot(u)
        pending.pop(("a", u)).wait()
        pending.pop(("b", u)).wait()
        for a in range(2):
            own[four, 0, a, z1, y, kept] = own[four, 0, a, z1, y, kept] + end_a[two, a]
        own[four, 1, z2, z1, y] = own[four, 1, z2, z1, y] + (tail_b[two] if straight(u) else tail_d[alt])
        remote(("a", u), own.at[four, 0, 1 - z2, z1, y, kept], tail_a.at[two], at_z2)
        remote(("b", u), own.at[four, 1, z2, z1, y], tail_x.at[two], at_x)

    def stage5(u):
        four, two, _ = slot(u)
        pending.pop(("a", u)).wait()
        pending.pop(("b", u)).wait()
        result[four, 0, kept, mine] = own[four, 0, z2, z1, y, kept] + tail_a[two]
        result[four, 1, :, mine] = own[four, 1, z2, z1, y] + tail_x[two]
        piece = result.at[four, 0, kept, mine]
        remote(("a", u), piece, piece, at_x)

    def stage6(u):
        four = u % 4
        pending.pop(("a", u)).wait()
        piece = result.at[four, :, :, mine]
        remote(("a", u), piece, piece, at_core)

    def stage7(u):
        pending.pop(("a", u)).wait()
        for k, (matrix, block) in enumerate(UNITS[u]):
            if matrix in DOWN:
                target = outs[matrix].at[pl.ds(block * rows, rows)]
            else:
                target = outs[matrix].at[:, pl.ds(block * D, D)]
            local(("out", u), result.at[u % 4, k], target)

    def stage8(u):
        arrived(("out", u))

    stages = (stage0, stage1, stage2, stage3, stage4, stage5, stage6, stage7, stage8)


    def fetch_rows(block):
        window = pl.ds(block * TILE, TILE)
        local("rows", returned[block], y_in)
        local("rows", plain_c.at[window], plain_in)
        local("rows", inverse_c.at[window], inverse_in)
        local("rows", slope.at[window], slope_in)
        local("rows", plain_b.at[window], plain_in_b)
        local("rows", inverse_b.at[window], inverse_in_b)

    def fetch_heads(block):
        local("heads", joint.at[pl.ds(block * TILE, TILE)], joint_in)

    def carry_rows(block):
        window = pl.ds(block * TILE, TILE)
        arrived("rows")
        total = norm_back_tile(
            y_in[...].astype(F32), plain_in[...].astype(F32), inverse_in[:, :1], gain_c[...]
        )
        upper[...] = total
        down_in[window] = total.astype(BF16)
        if block == 0:
            arrived("weights")
        for f in range(4):
            lanes = pl.ds(f * D, D)
            slopes = slope_in[:, lanes].astype(F32)
            rounded = (dot_nt(down_in[window], down_w[lanes]) * slopes).astype(BF16)
            rising_grad[window, lanes] = rounded
            back = dot_nt(rounded, wide[pl.ds(0, D), lanes])
            if f == 0:
                total = back
            else:
                total = total + back
        total = upper[...] + norm_back_tile(total, plain_in_b[...].astype(F32), inverse_in_b[:, :1], gain_b[...])
        rounded = total.astype(BF16)
        merge_in[window] = rounded
        mixed_grad[block] = dot_nt(rounded, merge_w[...]).astype(BF16)
        if block + 1 < blocks:
            fetch_rows(block + 1)
        else:
            fetch(8)

    def carry_heads(block):
        arrived("heads")
        places = TILE // 2

        def one(k, carry):
            inside = pl.ds(pl.multiple_of(k * places, 128), places)
            outside = pl.ds(pl.multiple_of(block * TILE + k * places, 128), places)
            for p in range(PAIRS):
                pieces = pair_backward(
                    joint_in[inside, col(p, 0)],
                    joint_in[inside, col(p, 1)],
                    joint_in[inside, col(p, 2)],
                    mixed_grad[block, inside, col(p)],
                    None,
                )
                for third in range(3):
                    joint_grad[outside, col(p, third)] = pieces[third]
            return carry

        lax.fori_loop(0, 2, one, 0)
        if block + 1 < blocks:
            fetch_heads(block + 1)

    fetch(0)
    fetch_rows(0)
    local("weights", coderdown, down_w)
    local("weights", coderup, wide.at[pl.ds(0, D)])
    local("weights", codermerge, merge_w)
    fetch_heads(0)
    for tick in range(len(UNITS) + len(stages) - 1):
        for level in reversed(range(len(stages))):
            if 0 <= tick - level < len(UNITS):
                stages[level](tick - level)
        if 1 <= tick < 7:
            fetch(tick + 1)
        if tick in CARRIED:
            kind, block = CARRIED[tick]
            (carry_rows if kind == "rows" else carry_heads)(block)


def backward(returned, kept, gains, weights, values, grads, heights):
    blocks = len(returned)
    rows = D // 8
    part = rows // 2
    flat = blocks * TILE
    flat = kept[0].shape[0]
    widths = [v.shape[1] if m in DOWN else 0 for m, v in enumerate(values)]
    anywhere = pl.BlockSpec(memory_space=pl.ANY)
    inside = pl.BlockSpec(memory_space=pltpu.VMEM)
    operands = list(returned) + list(kept) + list(gains) + list(weights) + list(values) + list(grads)
    specs = [anywhere] * len(operands)
    specs[blocks + 6] = specs[blocks + 7] = inside

    def room(*shape, dtype=BF16):
        return pltpu.VMEM(shape, dtype)

    return pl.pallas_call(
        partial(backward_kernel, blocks),
        in_specs=specs,
        out_specs=[anywhere] * MATRICES,
        out_shape=[jax.ShapeDtypeStruct(height, BF16) for height in heights],
        scratch_shapes=[
            room(2, 8, rows, D),
            room(2, 2, 8, rows, HALF),
            room(4, 2, 2, 2, 2, rows, HALF),
            room(2, 2, 2, 2, part, HALF),
            room(2, 2, 2, part, HALF),
            room(2, 2, part, HALF),
            room(2, part, HALF),
            room(2, 2, 2, rows, HALF),
            room(2, 2, rows, HALF),
            room(2, rows, HALF),
            room(2, 2, 2, rows, HALF),
            room(2, 2, rows, HALF),
            room(2, rows, HALF),
            room(2, rows, HALF),
            room(4, 2, rows, D),
            room(4 * D, D),
            room(flat, 4 * D),
            room(D, D),
            room(flat, 4 * D),
            room(flat, D),
            room(flat, D),
            room(flat, 3 * D),
            room(blocks, TILE, D),
            room(TILE, D),
            room(TILE, D),
            room(TILE, LANES, dtype=F32),
            room(TILE, 4 * D),
            room(TILE, D),
            room(TILE, LANES, dtype=F32),
            room(TILE, 3 * D),
            room(TILE, D, dtype=F32),
            room(TILE, 4 * D),
            room(flat, D),
            room(flat, 2 * D),
            pltpu.SemaphoreType.DMA((len(UNITS) * 12,)),
            pltpu.SemaphoreType.DMA((len(UNITS) * 12,)),
            pltpu.SemaphoreType.DMA((128,)),
        ],
        compiler_params=pltpu.CompilerParams(
            collective_id=0, has_side_effects=True, vmem_limit_bytes=62 * 2**20
        ),
        cost_estimate=estimate(45e9, 120e6),
        name="encoder_backward_and_sums",
    )(*operands)


def gain_grad(gain, weight, grad, nnbr):
    rows = weight.shape[0] // nnbr
    start = lax.axis_index("nbr") * rows
    own = lax.dynamic_slice_in_dim(weight, start, rows, 0).astype(F32)
    return jnp.sum(own * grad, axis=1) / lax.dynamic_slice_in_dim(gain, start, rows, 0)


def body(
    sizes,
    tokens,
    neighbours,
    out_grad,
    lengths,
    slot_order,
    selfgain,
    selfjoint,
    selfmerge,
    crossgain,
    crossquery,
    crossmerge,
    feedgain,
    feedup,
    feeddown,
    codergain,
    coderjoint,
    codermerge,
    codermid,
    coderup,
    coderdown,
    codertop,
    memorymap,
):
    nseq, nnbr = sizes
    me = lax.axis_index("seq")
    count, places, _ = neighbours.shape
    cap = count // nseq
    flat = count * places

    ordered = jnp.concatenate(
        [lax.dynamic_slice_in_dim(neighbours, (me ^ m) * cap, cap, 0) for m in range(nseq)], axis=0
    )
    embedded = ordered.reshape(flat, D).astype(F32)
    enc_normed, _, _ = norm_forward(embedded, codergain)
    enc_joint = times(enc_normed, coderjoint).astype(BF16).reshape(count, places, 3 * D)
    enc_mixed = enc_attend(enc_joint).reshape(flat, D)
    enc_middle = embedded + times(enc_mixed, codermerge)
    enc_normed_b, enc_plain_b, enc_inverse_b = norm_forward(enc_middle, codermid)
    enc_hidden, enc_slope = curve(times(enc_normed_b, coderup))
    enc_upper = enc_middle + times(enc_hidden, coderdown)
    enc_normed_c, enc_plain_c, enc_inverse_c = norm_forward(enc_upper, codertop)
    blocks = enc_normed_c.reshape(nseq, cap * places, D)
    received = jnp.concatenate(
        [blocks[m] if m == 0 else swap(blocks[m], "seq", nseq, m) for m in range(nseq)], axis=0
    )

    sequence = tokens[0].astype(F32)
    rows = sequence.shape[0]
    normed_a, plain_a, inverse_a = norm_forward(sequence, selfgain)
    joint = times(normed_a, selfjoint).astype(BF16)
    mixed = self_attend(joint, lengths)
    after_self = sequence + times(mixed, selfmerge)
    normed_b, plain_b, inverse_b = norm_forward(after_self, crossgain)
    asked = times(normed_b, crossquery).astype(BF16)

    memory = times(received, memorymap).astype(BF16).reshape(count, places, 2 * D)
    order = slot_order[0]
    order = ((order // cap) ^ me) * cap + order % cap
    crossed = cross_attend(asked, memory, order)
    live = (jnp.arange(rows, dtype=jnp.int32) // CH * CH < lengths[0]).astype(F32)[:, None]
    after_cross = after_self + times(crossed, crossmerge) * live
    normed_c, plain_c, inverse_c = norm_forward(after_cross, feedgain)
    hidden, slope = curve(times(normed_c, feedup))
    output = (after_cross + times(hidden, feeddown)).astype(BF16)[None]

    down_in = out_grad[0]
    rising_grad = (slope.astype(F32) * times_back(down_in, feeddown)).astype(BF16)
    cross_total = down_in.astype(F32) + norm_backward(times_back(rising_grad, feedup), plain_c, inverse_c, feedgain)
    cross_in = (cross_total * live).astype(BF16)
    crossed_grad = times_back(cross_in, crossmerge).astype(BF16)
    asked_grad, memory_grad = cross_attend_back(asked, memory, crossed_grad, order)
    memory_grad = memory_grad.reshape(flat, 2 * D)
    back = times_back(memory_grad, memorymap).astype(BF16).reshape(nseq, cap * places, D)
    returned = [back[m] if m == 0 else swap(back[m], "seq", nseq, m) for m in range(nseq)]
    self_total = cross_total + norm_backward(times_back(asked_grad, crossquery), plain_b, inverse_b, crossgain)
    self_in = self_total.astype(BF16)
    mixed_grad = times_back(self_in, selfmerge).astype(BF16)
    joint_grad = self_attend_back(joint, mixed_grad, lengths)
    input_grad = (self_total + norm_backward(times_back(joint_grad, selfjoint), plain_a, inverse_a, selfgain))[None]

    values = [
        hidden, normed_c, crossed, normed_b, received, mixed, normed_a, enc_hidden, enc_normed_b, enc_mixed, enc_normed
    ]
    grads = [down_in, rising_grad, cross_in, asked_grad, memory_grad, self_in, joint_grad]
    if nseq == 4 and nnbr == 8:
        heights = [
            (v.shape[1] // nnbr, w.shape[1])
            for v, w in zip(
                values,
                [feeddown, feedup, crossmerge, crossquery, memorymap, selfmerge, selfjoint, coderdown, coderup, codermerge, coderjoint],
            )
        ]
        sums = backward(
            returned,
            [
                enc_plain_c.astype(BF16),
                jnp.broadcast_to(enc_inverse_c, (flat, LANES)),
                enc_slope,
                enc_plain_b.astype(BF16),
                jnp.broadcast_to(enc_inverse_b, (flat, LANES)),
                enc_joint.reshape(flat, 3 * D),
            ],
            [codertop[None], codermid[None]],
            [coderdown, coderup, codermerge],
            values,
            grads,
            heights,
        )
    else:
        upper_total = norm_backward(
            jnp.concatenate(returned, axis=0).astype(F32), enc_plain_c, enc_inverse_c, codertop
        )
        enc_down_in = upper_total.astype(BF16)
        enc_rising_grad = (enc_slope.astype(F32) * times_back(enc_down_in, coderdown)).astype(BF16)
        middle_total = upper_total + norm_backward(
            times_back(enc_rising_grad, coderup), enc_plain_b, enc_inverse_b, codermid
        )
        enc_merge_in = middle_total.astype(BF16)
        enc_mixed_grad = times_back(enc_merge_in, codermerge).astype(BF16).reshape(count, places, D)
        enc_joint_grad = enc_attend_back(enc_joint, enc_mixed_grad).reshape(flat, 3 * D)
        grads += [enc_down_in, enc_rising_grad, enc_merge_in, enc_joint_grad]
        sums = [weight_grad(v, g).astype(BF16) for v, g in zip(values, grads)]
        ways = (False, True, False, False, False, False, False, True, False, True, True)
        sums = [reduce_group([total], sizes, way)[0] for total, way in zip(sums, ways)]
    (
        grad_feeddown,
        grad_feedup,
        grad_crossmerge,
        grad_crossquery,
        grad_memorymap,
        grad_selfmerge,
        grad_selfjoint,
        grad_coderdown,
        grad_coderup,
        grad_codermerge,
        grad_coderjoint,
    ) = [total.astype(F32) for total in sums]
    return (
        output,
        input_grad,
        gain_grad(selfgain, selfjoint, grad_selfjoint, nnbr),
        grad_selfjoint,
        grad_selfmerge,
        gain_grad(crossgain, crossquery, grad_crossquery, nnbr),
        grad_crossquery,
        grad_crossmerge,
        gain_grad(feedgain, feedup, grad_feedup, nnbr),
        grad_feedup,
        grad_feeddown,
        gain_grad(codergain, coderjoint, grad_coderjoint, nnbr),
        grad_coderjoint,
        grad_codermerge,
        gain_grad(codermid, coderup, grad_coderup, nnbr),
        grad_coderup,
        grad_coderdown,
        gain_grad(codertop, memorymap, grad_memorymap, nnbr),
        grad_memorymap,
    )


def solution(mesh):
    spread = ("seq", "nbr")
    sizes = (mesh.shape["seq"], mesh.shape["nbr"])
    placed = (
        P(spread, None, None),
        P(spread, None, None),
        P(spread, None, None),
        P(spread),
        P(spread, None),
    ) + (P(),) * 17
    gain, weight = P("nbr"), P("nbr", None)
    return jax.shard_map(
        partial(body, sizes),
        mesh=mesh,
        in_specs=placed,
        out_specs=(
            P(spread, None, None),
            P(spread, None, None),
            gain,
            weight,
            weight,
            gain,
            weight,
            weight,
            gain,
            weight,
            weight,
            gain,
            weight,
            weight,
            gain,
            weight,
            weight,
            gain,
            weight,
        ),
        check_vma=False,
    )
```

```python
from functools import partial

import jax
import jax.numpy as jnp
from jax import lax
from jax.experimental import pallas as pl
from jax.experimental.pallas import tpu as pltpu
from jax.sharding import PartitionSpec as P

D = 768
HEADS = 12
HD = 64
CH = 64
PAIRS = HEADS // 2
LANES = 2 * HD
SCALE = HD ** (-0.5)
F32 = jnp.float32
BF16 = jnp.bfloat16


def norm_forward(values, gain):
    centred = values - jnp.mean(values, axis=-1, keepdims=True)
    inverse = lax.rsqrt(jnp.mean(centred * centred, axis=-1, keepdims=True) + 1e-05)
    normed = centred * inverse
    return ((normed * gain).astype(BF16), normed, inverse)


def norm_backward(grad, normed, inverse, gain):
    scaled = grad * gain
    inner = jnp.mean(scaled * normed, axis=-1, keepdims=True)
    return inverse * (scaled - jnp.mean(scaled, axis=-1, keepdims=True) - normed * inner)


def times(values, weight):
    return lax.dot_general(values, weight, (((1,), (0,)), ((), ())), preferred_element_type=F32)


def times_back(grad, weight):
    return lax.dot_general(grad, weight, (((1,), (1,)), ((), ())), preferred_element_type=F32)


def weight_grad(values, grad):
    return lax.dot_general(values, grad, (((0,), (0,)), ((), ())), preferred_element_type=F32)


def curve(rising):
    square = rising * rising
    bend = jnp.tanh(rising * (0.7978845608028654 + 0.035677408136300125 * square))
    half = 0.5 * (1.0 + bend)
    slope = half + 0.5 * rising * (1.0 - bend * bend) * (0.7978845608028654 + 0.10703222440890037 * square)
    return (rising * half).astype(BF16), slope.astype(BF16)


def dot_nt(a, b):
    return lax.dot_general(a, b, (((1,), (1,)), ((), ())), preferred_element_type=F32)


def dot_nn(a, b):
    return lax.dot_general(a, b, (((1,), (0,)), ((), ())), preferred_element_type=F32)


def dot_tn(a, b):
    return lax.dot_general(a, b, (((0,), (0,)), ((), ())), preferred_element_type=F32)


def stack_pair(block):
    lane = lax.broadcasted_iota(jnp.int32, block.shape, 1)
    zero = jnp.zeros_like(block)
    return jnp.concatenate([jnp.where(lane < HD, block, zero), jnp.where(lane >= HD, block, zero)], axis=0)


def unstack_pair(stacked):
    half = stacked.shape[0] // 2
    lane = lax.broadcasted_iota(jnp.int32, (half, LANES), 1)
    return jnp.where(lane < HD, stacked[:half], stacked[half:])


def halves(block):
    width = block.shape[1] // 2
    return block[:, :width], block[:, width:]


def softmax_halves(products, allowed):
    parts = []
    for scores in halves(products):
        scores = scores * SCALE
        if allowed is not None:
            scores = jnp.where(allowed, scores, -1000000000.0)
        exponent = jnp.exp(scores - jnp.max(scores, axis=-1, keepdims=True))
        parts.append(exponent * (1.0 / jnp.sum(exponent, axis=-1, keepdims=True)))
    return parts


def rounded_halves(parts):
    return jnp.concatenate([part.astype(BF16) for part in parts], axis=1)


def pairs_forward(items, allowed=None):
    scores = [dot_nt(queries, stack_pair(keys)) for queries, keys, _ in items]
    probs = [rounded_halves(softmax_halves(block, allowed)) for block in scores]
    return [dot_nn(block, stack_pair(values)).astype(BF16) for block, (_, _, values) in zip(probs, items)]


def pairs_backward(items, allowed=None):
    stacked = [stack_pair(keys) for _, keys, _, _ in items]
    scores = [dot_nt(item[0], keys) for item, keys in zip(items, stacked)]
    prob_grads = [dot_nt(item[3], stack_pair(item[2])) for item in items]
    probs = [softmax_halves(block, allowed) for block in scores]
    value_grads = [unstack_pair(dot_tn(rounded_halves(block), item[3])) for block, item in zip(probs, items)]
    score_grads = []
    for block, grad in zip(probs, prob_grads):
        parts = []
        for prob, part in zip(block, halves(grad)):
            inner = jnp.sum(prob * part, axis=-1, keepdims=True)
            parts.append(prob * (part - inner) * SCALE)
        score_grads.append(rounded_halves(parts))
    query_grads = [dot_nn(grad, keys) for grad, keys in zip(score_grads, stacked)]
    key_grads = [unstack_pair(dot_tn(grad, item[0])) for grad, item in zip(score_grads, items)]
    return [tuple(g.astype(BF16) for g in grads) for grads in zip(query_grads, key_grads, value_grads)]


def col(pair, third=0):
    return slice(third * D + pair * LANES, third * D + (pair + 1) * LANES)


def estimate(flops, nbytes, exps=0):
    return pl.CostEstimate(flops=int(flops), bytes_accessed=int(nbytes), transcendentals=int(exps))


def enc_attend_kernel(joint_ref, mixed_ref):
    items = [tuple(joint_ref[0, :, col(p, third)] for third in range(3)) for p in range(PAIRS)]
    for p, mixed in enumerate(pairs_forward(items)):
        mixed_ref[0, :, col(p)] = mixed


def enc_attend(joint):
    count, rows, _ = joint.shape
    return pl.pallas_call(
        enc_attend_kernel,
        grid=(count,),
        in_specs=[pl.BlockSpec((1, rows, 3 * D), lambda i: (i, 0, 0))],
        out_specs=pl.BlockSpec((1, rows, D), lambda i: (i, 0, 0)),
        out_shape=jax.ShapeDtypeStruct((count, rows, D), BF16),
        cost_estimate=estimate(4 * count * rows * rows * D * 4, count * rows * D * 8, count * rows * rows * HEADS),
        name="enc_attend",
    )(joint)


def enc_attend_back_kernel(joint_ref, grad_ref, out_ref):
    items = [
        tuple(joint_ref[0, :, col(p, third)] for third in range(3)) + (grad_ref[0, :, col(p)],) for p in range(PAIRS)
    ]
    for p, grads in enumerate(pairs_backward(items)):
        for third in range(3):
            out_ref[0, :, col(p, third)] = grads[third]


def enc_attend_back(joint, grad):
    count, rows, _ = joint.shape
    return pl.pallas_call(
        enc_attend_back_kernel,
        grid=(count,),
        in_specs=[
            pl.BlockSpec((1, rows, 3 * D), lambda i: (i, 0, 0)),
            pl.BlockSpec((1, rows, D), lambda i: (i, 0, 0)),
        ],
        out_specs=pl.BlockSpec((1, rows, 3 * D), lambda i: (i, 0, 0)),
        out_shape=jax.ShapeDtypeStruct((count, rows, 3 * D), BF16),
        cost_estimate=estimate(10 * count * rows * rows * D * 4, count * rows * D * 14, count * rows * rows * HEADS),
        name="enc_attend_back",
    )(joint, grad)


def causal_mask(rows, length):
    row = lax.broadcasted_iota(jnp.int32, (rows, rows), 0)
    column = lax.broadcasted_iota(jnp.int32, (rows, rows), 1)
    return (column <= row) & (column < length)


def split(ref):
    return [ref[:, k * LANES : (k + 1) * LANES] for k in range(ref.shape[1] // LANES)]


def self_attend_kernel(length_ref, q_ref, k_ref, v_ref, out_ref):
    allowed = causal_mask(q_ref.shape[0], length_ref[0])
    items = list(zip(split(q_ref), split(k_ref), split(v_ref)))
    for p, mixed in enumerate(pairs_forward(items, allowed)):
        out_ref[:, col(p)] = mixed


SELF_STEPS = 2


def self_specs(rows):
    width = D // SELF_STEPS
    return [pl.BlockSpec((rows, width), lambda p, _, t=t: (0, t * SELF_STEPS + p)) for t in range(3)]


def self_attend(joint, lengths):
    rows = joint.shape[0]
    return pl.pallas_call(
        self_attend_kernel,
        grid_spec=pltpu.PrefetchScalarGridSpec(
            num_scalar_prefetch=1,
            grid=(SELF_STEPS,),
            in_specs=self_specs(rows),
            out_specs=pl.BlockSpec((rows, D // SELF_STEPS), lambda p, _: (0, p)),
        ),
        out_shape=jax.ShapeDtypeStruct((rows, D), BF16),
        cost_estimate=estimate(4 * rows * rows * D * 4, rows * D * 8, rows * rows * HEADS),
        name="self_attend",
    )(lengths, joint, joint, joint)


def self_attend_back_kernel(length_ref, q_ref, k_ref, v_ref, grad_ref, out_ref):
    allowed = causal_mask(q_ref.shape[0], length_ref[0])
    width = q_ref.shape[1]
    items = list(zip(split(q_ref), split(k_ref), split(v_ref), split(grad_ref)))
    for p, grads in enumerate(pairs_backward(items, allowed)):
        for third in range(3):
            begin = pl.multiple_of(third * D + pl.program_id(0) * width + p * LANES, LANES)
            out_ref[:, pl.ds(begin, LANES)] = grads[third]


def self_attend_back(joint, grad, lengths):
    rows = joint.shape[0]
    return pl.pallas_call(
        self_attend_back_kernel,
        grid_spec=pltpu.PrefetchScalarGridSpec(
            num_scalar_prefetch=1,
            grid=(SELF_STEPS,),
            in_specs=self_specs(rows) + [pl.BlockSpec((rows, D // SELF_STEPS), lambda p, _: (0, p))],
            out_specs=pl.BlockSpec((rows, 3 * D), lambda p, _: (0, 0)),
        ),
        out_shape=jax.ShapeDtypeStruct((rows, 3 * D), BF16),
        cost_estimate=estimate(10 * rows * rows * D * 4, rows * D * 14, rows * rows * HEADS),
        name="self_attend_back",
    )(lengths, joint, joint, joint, grad)


def cross_items(asked_ref, first_ref, second_ref):
    return [
        (asked_ref[:, col(p)],)
        + tuple(
            jnp.concatenate([first_ref[0, :, col(p, third)], second_ref[0, :, col(p, third)]], axis=0) for third in range(2)
        )
        for p in range(PAIRS)
    ]


def cross_attend_kernel(order_ref, asked_ref, first_ref, second_ref, out_ref):
    for p, mixed in enumerate(pairs_forward(cross_items(asked_ref, first_ref, second_ref))):
        out_ref[:, col(p)] = mixed


def cross_attend(asked, memory, order):
    rows = asked.shape[0]
    count, places, _ = memory.shape
    return pl.pallas_call(
        cross_attend_kernel,
        grid_spec=pltpu.PrefetchScalarGridSpec(
            num_scalar_prefetch=1,
            grid=(rows // CH,),
            in_specs=[
                pl.BlockSpec((CH, D), lambda c, order: (c, 0)),
                pl.BlockSpec((1, places, 2 * D), lambda c, order: (order[2 * c], 0, 0)),
                pl.BlockSpec((1, places, 2 * D), lambda c, order: (order[2 * c + 1], 0, 0)),
            ],
            out_specs=pl.BlockSpec((CH, D), lambda c, order: (c, 0)),
        ),
        out_shape=jax.ShapeDtypeStruct((rows, D), BF16),
        cost_estimate=estimate(4 * rows * 2 * places * D * 4, rows * D * 4 + count * places * D * 4, rows * 2 * places * HEADS),
        name="cross_attend",
    )(order, asked, memory, memory)


def cross_attend_back_kernel(order_ref, asked_ref, first_ref, second_ref, grad_ref, dq_ref, dmem_ref):
    c = pl.program_id(0)
    first, second = order_ref[2 * c], order_ref[2 * c + 1]
    places = first_ref.shape[1]
    items = [
        item + (grad_ref[:, col(p)],) for p, item in enumerate(cross_items(asked_ref, first_ref, second_ref))
    ]
    for p, (dq, dk, dv) in enumerate(pairs_backward(items)):
        dq_ref[:, col(p)] = dq
        dmem_ref[first, :, col(p, 0)] = dk[:places]
        dmem_ref[second, :, col(p, 0)] = dk[places:]
        dmem_ref[first, :, col(p, 1)] = dv[:places]
        dmem_ref[second, :, col(p, 1)] = dv[places:]


def cross_attend_back(asked, memory, grad, order):
    rows = asked.shape[0]
    count, places, _ = memory.shape
    return pl.pallas_call(
        cross_attend_back_kernel,
        grid_spec=pltpu.PrefetchScalarGridSpec(
            num_scalar_prefetch=1,
            grid=(rows // CH,),
            in_specs=[
                pl.BlockSpec((CH, D), lambda c, order: (c, 0)),
                pl.BlockSpec((1, places, 2 * D), lambda c, order: (order[2 * c], 0, 0)),
                pl.BlockSpec((1, places, 2 * D), lambda c, order: (order[2 * c + 1], 0, 0)),
                pl.BlockSpec((CH, D), lambda c, order: (c, 0)),
            ],
            out_specs=[
                pl.BlockSpec((CH, D), lambda c, order: (c, 0)),
                pl.BlockSpec((count, places, 2 * D), lambda c, order: (0, 0, 0)),
            ],
        ),
        out_shape=[jax.ShapeDtypeStruct((rows, D), BF16), jax.ShapeDtypeStruct(memory.shape, BF16)],
        cost_estimate=estimate(10 * rows * 2 * places * D * 4, rows * D * 6 + count * places * D * 8, rows * 2 * places * HEADS),
        name="cross_attend_back",
    )(order, asked, memory, memory, grad)


def swap(value, axis, size, mask):
    return lax.ppermute(value, axis, [(i, i ^ mask) for i in range(size)])


def bit_of(axis, mask):
    return (lax.axis_index(axis) // mask) % 2


def pick(value, dim, index):
    return lax.dynamic_index_in_dim(value, index, dim, keepdims=False)


def halve(value, dim, axis, size, mask):
    bit = bit_of(axis, mask)
    arrived = swap(pick(value, dim, 1 - bit), axis, size, mask)
    return (pick(value, dim, bit).astype(F32) + arrived.astype(F32)).astype(BF16)


def join(value, dim, axis, size, mask):
    arrived = swap(value, axis, size, mask)
    bit = bit_of(axis, mask)
    return jnp.where(
        bit == 0, jnp.concatenate([value, arrived], axis=dim), jnp.concatenate([arrived, value], axis=dim)
    )


def masks(size):
    found, mask = [], 1
    while mask < size:
        found.append(mask)
        mask *= 2
    return found


def reduce_group(totals, sizes, rows_first):
    nseq, nnbr = sizes
    core = bit_of("seq", 1)
    parts = []
    for whole in totals:
        height, width = whole.shape
        parts.append(halve(whole.reshape(height, 2, width // 2), 1, "seq", nseq, 1))
    widths = [part.shape[1] for part in parts]
    total = parts[0] if len(parts) == 1 else jnp.concatenate(parts, axis=1)
    bits = masks(nnbr)
    rows = total.shape[0] // nnbr
    total = total.reshape((2,) * len(bits) + (rows, total.shape[1]))
    seq_bits = masks(nseq)[1:]

    def over_seq(total):
        for mask in seq_bits:
            shape = total.shape
            total = total.reshape(shape[:-2] + (2, shape[-2] // 2, shape[-1]))
            total = halve(total, total.ndim - 3, "seq", nseq, mask)
        return total

    def over_nbr(total):
        left = list(reversed(bits))
        for mask in bits:
            total = halve(total, left.index(mask), "nbr", nnbr, mask)
            left.remove(mask)
        return total

    if rows_first:
        total = over_nbr(over_seq(total))
        for mask in reversed(seq_bits):
            total = join(total, 0, "seq", nseq, mask)
    else:
        total = over_nbr(total)
        for mask in seq_bits:
            total = (total.astype(F32) + swap(total, "seq", nseq, mask).astype(F32)).astype(BF16)
    other = swap(total, "seq", nseq, 1)
    results, start = [], 0
    for width in widths:
        mine, theirs = total[:, start : start + width], other[:, start : start + width]
        results.append(
            jnp.where(
                core == 0, jnp.concatenate([mine, theirs], axis=1), jnp.concatenate([theirs, mine], axis=1)
            ).astype(F32)
        )
        start += width
    return results


MESH = pl.DeviceIdType.MESH
HALF = D // 2


def norm_back_tile(grad, normed, inverse, gain):
    scaled = grad * gain
    inner = jnp.mean(scaled * normed, axis=-1, keepdims=True)
    return inverse * (scaled - jnp.mean(scaled, axis=-1, keepdims=True) - normed * inner)


MATRICES = 11
DOWN = (0, 7)
UNITS = (
    ((0, 0), (0, 1)),
    ((0, 2), (0, 3)),
    ((1, 0), (1, 1)),
    ((1, 2), (1, 3)),
    ((2, 0), (3, 0)),
    ((4, 0), (4, 1)),
    ((5, 0), (6, 0)),
    ((6, 1), (6, 2)),
    ((7, 0), (7, 1)),
    ((7, 2), (7, 3)),
    ((8, 0), (8, 1)),
    ((8, 2), (8, 3)),
    ((9, 0), (10, 0)),
    ((10, 1), (10, 2)),
)
CARRIED = {
    0: (("rows", 0, None),),
    1: (("heads", 0, (0, 1)),),
    2: (("rows", 1, None),),
    3: (("heads", 1, (0, 1)),),
    4: (("rows", 2, None),),
    5: (("heads", 2, (0,)),),
    6: (("rows", 3, None),),
    7: (("heads", 2, (1,)), ("heads", 3, (0,))),
    9: (("heads", 3, (1,)),),
}
TILE = 256


def backward_kernel(blocks, *refs):
    refs = list(refs)

    def take(number):
        taken = refs[:number]
        del refs[:number]
        return taken

    returned = take(blocks)
    plain_c, inverse_c, slope, plain_b, inverse_b, joint = take(6)
    gain_c, gain_b = take(2)
    coderdown, coderup, codermerge = take(3)
    values = take(MATRICES)
    grads = take(7)
    outs = take(MATRICES)
    (
        stage, first, own, mid, low_a, end_a, tail_a, low_b, end_b, tail_b, low_d, end_d, tail_d, tail_x, result,
        down_w, wide, merge_w, rising_grad, down_in, merge_in, joint_grad, mixed_grad,
        y_in, plain_in, inverse_in, slope_in, plain_in_b, inverse_in_b, joint_in, upper,
        feed_a, some_a, some_b,
        send_sem, recv_sem, local_sem,
    ) = refs
    rows = D // 8
    part = rows // 2
    flat = blocks * TILE
    s, n = lax.axis_index("seq"), lax.axis_index("nbr")
    c, x = s % 2, s // 2
    y, z1, z2 = n % 2, (n // 2) % 2, n // 4
    at_core, at_x = (s + 1 - 2 * c, n), (s + 2 - 4 * x, n)
    at_y, at_z1, at_z2 = (s, n + 1 - 2 * y), (s, n + 2 - 4 * z1), (s, n + 4 - 8 * z2)
    mine = pl.ds(pl.multiple_of(c * HALF, 128), HALF)
    other = pl.ds(pl.multiple_of((1 - c) * HALF, 128), HALF)
    kept = pl.ds(pl.multiple_of(x * part, 16), part)
    given = pl.ds(pl.multiple_of((1 - x) * part, 16), part)

    barrier = pltpu.get_barrier_semaphore()
    for partner in (at_core, at_x, at_y, at_z1, at_z2):
        pl.semaphore_signal(barrier, inc=1, device_id=partner, device_id_type=MESH)
    pl.semaphore_wait(barrier, 5)

    pending = {}
    counts = {"local": 0, "remote": 0}

    def remote(key, src, dst, partner):
        index = counts["remote"]
        counts["remote"] += 1
        copy = pltpu.make_async_remote_copy(
            src_ref=src,
            dst_ref=dst,
            send_sem=send_sem.at[index],
            recv_sem=recv_sem.at[index],
            device_id=partner,
            device_id_type=MESH,
        )
        copy.start()
        pending[key] = copy

    def local(key, src, dst):
        copy = pltpu.make_async_copy(src, dst, local_sem.at[counts["local"]])
        counts["local"] += 1
        copy.start()
        pending.setdefault(key, []).append(copy)

    def arrived(key):
        for copy in pending.pop(key, []):
            copy.wait()


    def fetch(u):
        if u == 0:
            local(("unit", 0), values[0], feed_a)
            local(("unit", 0), grads[0], some_b.at[pl.ds(0, TILE), pl.ds(0, D)])
        elif u in (2, 3):
            if u == 2:
                local(("unit", u), values[1], some_a.at[pl.ds(0, TILE)])
            local(("unit", u), grads[1].at[:, pl.ds((u - 2) * 2 * D, 2 * D)], some_b.at[pl.ds(0, TILE)])
        elif u == 4:
            for k in range(2):
                local(("unit", u), values[2 + k], some_a.at[pl.ds(k * TILE, TILE)])
                local(("unit", u), grads[2 + k], some_b.at[pl.ds(0, TILE), pl.ds(k * D, D)])
        elif u == 5:
            local(("unit", u), values[4], some_a)
            local(("unit", u), grads[4], some_b)
        elif u == 6:
            for k in range(2):
                local(("unit", u), values[5 + k], some_a.at[pl.ds(k * TILE, TILE)])
            local(("unit", u), grads[5], some_b.at[pl.ds(0, TILE), pl.ds(0, D)])
            local(("unit", u), grads[6].at[:, pl.ds(0, D)], some_b.at[pl.ds(0, TILE), pl.ds(D, D)])
        elif u == 7:
            local(("unit", u), grads[6].at[:, pl.ds(D, 2 * D)], some_b.at[pl.ds(0, TILE)])
        elif u == 8:
            local(("unit", 8), values[7], wide)
            for k in range(3):
                local(("unit", 10), values[8 + k], down_w.at[pl.ds(k * flat, flat)])

    def operands(u, k):
        left = pl.ds(k * D, D)
        if u in (2, 3):
            return some_a.at[pl.ds(0, TILE)], some_b.at[pl.ds(0, TILE), left]
        if u in (4, 6):
            return some_a.at[pl.ds(k * TILE, TILE)], some_b.at[pl.ds(0, TILE), left]
        if u == 5:
            return some_a, some_b.at[:, left]
        if u == 7:
            return some_a.at[pl.ds(TILE, TILE)], some_b.at[pl.ds(0, TILE), left]
        if u in (10, 11):
            return down_w.at[pl.ds(0, flat)], rising_grad.at[:, pl.ds(((u - 10) * 2 + k) * D, D)]
        if u == 12:
            return down_w.at[pl.ds((1 + k) * flat, flat)], merge_in if k == 0 else joint_grad.at[:, pl.ds(0, D)]
        return down_w.at[pl.ds(2 * flat, flat)], joint_grad.at[:, pl.ds((1 + k) * D, D)]

    def product(u):
        if UNITS[u][0][0] in DOWN:
            left = feed_a if u < 2 else wide
            right = some_b.at[pl.ds(0, TILE), pl.ds(0, D)] if u < 2 else down_in
            begin = (u % 2) * 2 * rows

            def one(shard, carry):
                columns = left[:, pl.ds(pl.multiple_of(shard * 4 * rows, 128), 4 * rows)]
                tile = dot_tn(columns[:, begin : begin + 2 * rows], right[...]).astype(BF16)
                stage[0, shard] = tile[:rows]
                stage[1, shard] = tile[rows:]
                return carry

            lax.fori_loop(0, 8, one, 0)
            return
        for k in range(2):
            left, right = operands(u, k)
            stage[k] = dot_tn(left[...], right[...]).astype(BF16).reshape(8, rows, D)


    def slot(u):
        return u % 5, u % 4

    def straight(u):
        return u % 4 != 0

    def stage0(u):
        arrived(("unit", u))
        product(u)
        remote(("core", u), stage.at[:, :, :, other], first.at[u % 2], at_core)

    def stage1(u):
        five, four = slot(u)
        pending.pop(("core", u)).wait()

        def one(k, carry):
            k, a, b, d = k // 8, (k // 4) % 2, (k // 2) % 2, k % 2
            shard = 4 * a + 2 * b + d
            own[five, k, a, b, d] = stage[k, shard, :, mine] + first[u % 2, k, shard]
            return carry

        lax.fori_loop(0, 16, one, 0)
        remote(("a", u), own.at[five, 0, :, :, :, given], mid.at[four], at_x)
        if straight(u):
            remote(("b", u), own.at[five, 1, :, :, 1 - y], low_b.at[four], at_y)
        else:
            remote(("b", u), own.at[five, 1, :, 1 - z1], low_d, at_z1)

    def stage2(u):
        five, four = slot(u)
        pending.pop(("a", u)).wait()
        pending.pop(("b", u)).wait()
        for a in range(2):
            for b in range(2):
                for d in range(2):
                    own[five, 0, a, b, d, kept] = own[five, 0, a, b, d, kept] + mid[four, a, b, d]
        for a in range(2):
            for b in range(2):
                if straight(u):
                    own[five, 1, a, b, y] = own[five, 1, a, b, y] + low_b[four, a, b]
                else:
                    own[five, 1, a, z1, b] = own[five, 1, a, z1, b] + low_d[a, b]
        remote(("a", u), own.at[five, 0, :, :, 1 - y, kept], low_a.at[four], at_y)
        if straight(u):
            remote(("b", u), own.at[five, 1, :, 1 - z1, y], end_b.at[four], at_z1)
        else:
            remote(("b", u), own.at[five, 1, 1 - z2, z1], end_d, at_z2)

    def stage3(u):
        five, four = slot(u)
        pending.pop(("a", u)).wait()
        pending.pop(("b", u)).wait()
        for a in range(2):
            for b in range(2):
                own[five, 0, a, b, y, kept] = own[five, 0, a, b, y, kept] + low_a[four, a, b]
            if straight(u):
                own[five, 1, a, z1, y] = own[five, 1, a, z1, y] + end_b[four, a]
            else:
                own[five, 1, z2, z1, a] = own[five, 1, z2, z1, a] + end_d[a]
        remote(("a", u), own.at[five, 0, :, 1 - z1, y, kept], end_a.at[four], at_z1)
        if straight(u):
            remote(("b", u), own.at[five, 1, 1 - z2, z1, y], tail_b.at[four], at_z2)
        else:
            remote(("b", u), own.at[five, 1, z2, z1, 1 - y], tail_d, at_y)

    def stage4(u):
        five, four = slot(u)
        pending.pop(("a", u)).wait()
        pending.pop(("b", u)).wait()
        for a in range(2):
            own[five, 0, a, z1, y, kept] = own[five, 0, a, z1, y, kept] + end_a[four, a]
        own[five, 1, z2, z1, y] = own[five, 1, z2, z1, y] + (tail_b[four] if straight(u) else tail_d[...])
        remote(("a", u), own.at[five, 0, 1 - z2, z1, y, kept], tail_a.at[four], at_z2)
        remote(("b", u), own.at[five, 1, z2, z1, y], tail_x.at[four], at_x)

    def stage5(u):
        five, four = slot(u)
        pending.pop(("a", u)).wait()
        pending.pop(("b", u)).wait()
        result[u % 6, 0, kept, mine] = own[five, 0, z2, z1, y, kept] + tail_a[four]
        result[u % 6, 1, :, mine] = own[five, 1, z2, z1, y] + tail_x[four]
        piece = result.at[u % 6, 0, kept, mine]
        remote(("a", u), piece, piece, at_x)

    def stage6(u):
        pending.pop(("a", u)).wait()
        piece = result.at[u % 6, :, :, mine]
        remote(("a", u), piece, piece, at_core)

    def stage7(u):
        pending.pop(("a", u)).wait()
        for k, (matrix, block) in enumerate(UNITS[u]):
            if matrix in DOWN:
                target = outs[matrix].at[pl.ds(block * rows, rows)]
            else:
                target = outs[matrix].at[:, pl.ds(block * D, D)]
            local(("out", u), result.at[u % 6, k], target)

    def stage8(u):
        arrived(("out", u))

    stages = (stage0, stage1, stage2, stage3, stage4, stage5, stage6, stage7, stage8)


    def fetch_rows(block):
        window = pl.ds(block * TILE, TILE)
        local("rows", returned[block], y_in)
        local("rows", plain_c.at[window], plain_in)
        local("rows", inverse_c.at[window], inverse_in)
        local("rows", slope.at[window], slope_in)
        local("rows", plain_b.at[window], plain_in_b)
        local("rows", inverse_b.at[window], inverse_in_b)

    def fetch_heads(block):
        local("heads", joint.at[pl.ds(block * TILE, TILE)], joint_in)

    def carry_rows(block):
        window = pl.ds(block * TILE, TILE)
        arrived("rows")
        total = norm_back_tile(
            y_in[...].astype(F32), plain_in[...].astype(F32), inverse_in[:, :1], gain_c[...]
        )
        upper[...] = total
        down_in[window] = total.astype(BF16)
        if block == 0:
            arrived("weights")
        for f in range(4):
            lanes = pl.ds(f * D, D)
            slopes = slope_in[:, lanes].astype(F32)
            rounded = (dot_nt(down_in[window], down_w[lanes]) * slopes).astype(BF16)
            rising_grad[window, lanes] = rounded
            back = dot_nt(rounded, wide[pl.ds(0, D), lanes])
            if f == 0:
                total = back
            else:
                total = total + back
        total = upper[...] + norm_back_tile(total, plain_in_b[...].astype(F32), inverse_in_b[:, :1], gain_b[...])
        rounded = total.astype(BF16)
        merge_in[window] = rounded
        mixed_grad[block] = dot_nt(rounded, merge_w[...]).astype(BF16)
        if block + 1 < blocks:
            fetch_rows(block + 1)
        else:
            fetch(8)

    def carry_heads(block, which):
        if which[0] == 0:
            arrived("heads")
        places = TILE // 2

        def one(k, carry):
            inside = pl.ds(pl.multiple_of(k * places, 128), places)
            outside = pl.ds(pl.multiple_of(block * TILE + k * places, 128), places)
            items = [
                tuple(joint_in[inside, col(p, third)] for third in range(3)) + (mixed_grad[block, inside, col(p)],)
                for p in range(PAIRS)
            ]
            for p, pieces in enumerate(pairs_backward(items)):
                for third in range(3):
                    joint_grad[outside, col(p, third)] = pieces[third]
            return carry

        lax.fori_loop(which[0], which[-1] + 1, one, 0)
        if which[-1] == 1 and block + 1 < blocks:
            fetch_heads(block + 1)

    fetch(0)
    fetch_rows(0)
    local("weights", coderdown, down_w)
    local("weights", coderup, wide.at[pl.ds(0, D)])
    local("weights", codermerge, merge_w)
    fetch_heads(0)
    for tick in range(len(UNITS) + len(stages) - 1):
        for level in (1, 0) + tuple(range(2, len(stages))):
            if 0 <= tick - level < len(UNITS):
                stages[level](tick - level)
        if 1 <= tick < 7:
            fetch(tick + 1)
        for kind, block, which in CARRIED.get(tick, ()):
            if kind == "rows":
                carry_rows(block)
            else:
                carry_heads(block, which)


def backward(returned, kept, gains, weights, values, grads, heights):
    blocks = len(returned)
    rows = D // 8
    part = rows // 2
    flat = blocks * TILE
    flat = kept[0].shape[0]
    widths = [v.shape[1] if m in DOWN else 0 for m, v in enumerate(values)]
    anywhere = pl.BlockSpec(memory_space=pl.ANY)
    inside = pl.BlockSpec(memory_space=pltpu.VMEM)
    operands = list(returned) + list(kept) + list(gains) + list(weights) + list(values) + list(grads)
    specs = [anywhere] * len(operands)
    specs[blocks + 6] = specs[blocks + 7] = inside

    def room(*shape, dtype=BF16):
        return pltpu.VMEM(shape, dtype)

    return pl.pallas_call(
        partial(backward_kernel, blocks),
        in_specs=specs,
        out_specs=[anywhere] * MATRICES,
        out_shape=[jax.ShapeDtypeStruct(height, BF16) for height in heights],
        scratch_shapes=[
            room(2, 8, rows, D),
            room(2, 2, 8, rows, HALF),
            room(5, 2, 2, 2, 2, rows, HALF),
            room(4, 2, 2, 2, part, HALF),
            room(4, 2, 2, part, HALF),
            room(4, 2, part, HALF),
            room(4, part, HALF),
            room(4, 2, 2, rows, HALF),
            room(4, 2, rows, HALF),
            room(4, rows, HALF),
            room(2, 2, rows, HALF),
            room(2, rows, HALF),
            room(rows, HALF),
            room(4, rows, HALF),
            room(6, 2, rows, D),
            room(4 * D, D),
            room(flat, 4 * D),
            room(D, D),
            room(flat, 4 * D),
            room(flat, D),
            room(flat, D),
            room(flat, 3 * D),
            room(blocks, TILE, D),
            room(TILE, D),
            room(TILE, D),
            room(TILE, LANES, dtype=F32),
            room(TILE, 4 * D),
            room(TILE, D),
            room(TILE, LANES, dtype=F32),
            room(TILE, 3 * D),
            room(TILE, D, dtype=F32),
            room(TILE, 4 * D),
            room(flat, D),
            room(flat, 2 * D),
            pltpu.SemaphoreType.DMA((len(UNITS) * 12,)),
            pltpu.SemaphoreType.DMA((len(UNITS) * 12,)),
            pltpu.SemaphoreType.DMA((128,)),
        ],
        compiler_params=pltpu.CompilerParams(
            collective_id=0, has_side_effects=True, vmem_limit_bytes=62 * 2**20
        ),
        cost_estimate=estimate(45e9, 120e6),
        name="encoder_backward_and_sums",
    )(*operands)


GAINED = (6, 3, 1, 10, 8, 4)


def finish_kernel(nbr_ref, *refs):
    gains, sums, weights, outs, gain_outs = refs[:6], refs[6:17], refs[17:23], refs[23:34], refs[34:]
    for total, out in zip(sums, outs):
        out[...] = total[...].astype(F32)
    rows = gain_outs[0].shape[1]
    row = lax.broadcasted_iota(jnp.int32, (D, rows), 0)
    place = lax.broadcasted_iota(jnp.int32, (D, rows), 1) + nbr_ref[0] * rows
    own = lax.dot_general(
        jnp.concatenate([gain[...] for gain in gains], axis=0),
        (row == place).astype(F32),
        (((1,), (0,)), ((), ())),
        precision=lax.Precision.HIGHEST,
        preferred_element_type=F32,
    )
    for k, (matrix, weight, out) in enumerate(zip(GAINED, weights, gain_outs)):
        product = weight[...].astype(F32) * sums[matrix][...].astype(F32)
        summed = lax.dot_general(
            jnp.ones((8, product.shape[1]), F32),
            product,
            (((1,), (1,)), ((), ())),
            precision=lax.Precision.HIGHEST,
            preferred_element_type=F32,
        )
        out[...] = summed[:1] / own[k : k + 1]


def finish(sums, gains, weights, nnbr):
    rows = D // nnbr
    gains = [gain[None] for gain in gains]
    nbr = lax.axis_index("nbr").reshape(1).astype(jnp.int32)

    def whole(array):
        return pl.BlockSpec(array.shape, lambda i, nbr: (0, 0))

    results = pl.pallas_call(
        finish_kernel,
        grid_spec=pltpu.PrefetchScalarGridSpec(
            num_scalar_prefetch=1,
            grid=(1,),
            in_specs=[whole(array) for array in gains + list(sums)]
            + [pl.BlockSpec((rows, weight.shape[1]), lambda i, nbr: (nbr[0], 0)) for weight in weights],
            out_specs=[whole(total) for total in sums] + [pl.BlockSpec((1, rows), lambda i, nbr: (0, 0))] * len(weights),
        ),
        out_shape=[jax.ShapeDtypeStruct(total.shape, F32) for total in sums]
        + [jax.ShapeDtypeStruct((1, rows), F32)] * len(weights),
        compiler_params=pltpu.CompilerParams(vmem_limit_bytes=56 * 2**20),
        cost_estimate=estimate(1e7, 20e6),
        name="finish",
    )(nbr, *gains, *sums, *weights)
    return results[: len(sums)], [grad.reshape(rows) for grad in results[len(sums) :]]


def body(
    sizes,
    tokens,
    neighbours,
    out_grad,
    lengths,
    slot_order,
    selfgain,
    selfjoint,
    selfmerge,
    crossgain,
    crossquery,
    crossmerge,
    feedgain,
    feedup,
    feeddown,
    codergain,
    coderjoint,
    codermerge,
    codermid,
    coderup,
    coderdown,
    codertop,
    memorymap,
):
    nseq, nnbr = sizes
    me = lax.axis_index("seq")
    count, places, _ = neighbours.shape
    cap = count // nseq
    flat = count * places

    ordered = jnp.concatenate(
        [lax.dynamic_slice_in_dim(neighbours, (me ^ m) * cap, cap, 0) for m in range(nseq)], axis=0
    )
    embedded = ordered.reshape(flat, D).astype(F32)
    enc_normed, _, _ = norm_forward(embedded, codergain)
    enc_joint = times(enc_normed, coderjoint).astype(BF16).reshape(count, places, 3 * D)
    enc_mixed = enc_attend(enc_joint).reshape(flat, D)
    enc_middle = embedded + times(enc_mixed, codermerge)
    enc_normed_b, enc_plain_b, enc_inverse_b = norm_forward(enc_middle, codermid)
    enc_hidden, enc_slope = curve(times(enc_normed_b, coderup))
    enc_upper = enc_middle + times(enc_hidden, coderdown)
    enc_normed_c, enc_plain_c, enc_inverse_c = norm_forward(enc_upper, codertop)
    blocks = enc_normed_c.reshape(nseq, cap * places, D)
    received = jnp.concatenate(
        [blocks[m] if m == 0 else swap(blocks[m], "seq", nseq, m) for m in range(nseq)], axis=0
    )

    sequence = tokens[0].astype(F32)
    rows = sequence.shape[0]
    normed_a, plain_a, inverse_a = norm_forward(sequence, selfgain)
    joint = times(normed_a, selfjoint).astype(BF16)
    mixed = self_attend(joint, lengths)
    after_self = sequence + times(mixed, selfmerge)
    normed_b, plain_b, inverse_b = norm_forward(after_self, crossgain)
    asked = times(normed_b, crossquery).astype(BF16)

    memory = times(received, memorymap).astype(BF16).reshape(count, places, 2 * D)
    order = slot_order[0]
    order = ((order // cap) ^ me) * cap + order % cap
    crossed = cross_attend(asked, memory, order)
    live = (jnp.arange(rows, dtype=jnp.int32) // CH * CH < lengths[0]).astype(F32)[:, None]
    after_cross = after_self + times(crossed, crossmerge) * live
    normed_c, plain_c, inverse_c = norm_forward(after_cross, feedgain)
    hidden, slope = curve(times(normed_c, feedup))
    output = (after_cross + times(hidden, feeddown)).astype(BF16)[None]

    down_in = out_grad[0]
    rising_grad = (slope.astype(F32) * times_back(down_in, feeddown)).astype(BF16)
    cross_total = down_in.astype(F32) + norm_backward(times_back(rising_grad, feedup), plain_c, inverse_c, feedgain)
    cross_in = (cross_total * live).astype(BF16)
    crossed_grad = times_back(cross_in, crossmerge).astype(BF16)
    asked_grad, memory_grad = cross_attend_back(asked, memory, crossed_grad, order)
    memory_grad = memory_grad.reshape(flat, 2 * D)
    back = times_back(memory_grad, memorymap).astype(BF16).reshape(nseq, cap * places, D)
    returned = [back[m] if m == 0 else swap(back[m], "seq", nseq, m) for m in range(nseq)]
    self_total = cross_total + norm_backward(times_back(asked_grad, crossquery), plain_b, inverse_b, crossgain)
    self_in = self_total.astype(BF16)
    mixed_grad = times_back(self_in, selfmerge).astype(BF16)
    joint_grad = self_attend_back(joint, mixed_grad, lengths)
    input_grad = (self_total + norm_backward(times_back(joint_grad, selfjoint), plain_a, inverse_a, selfgain))[None]

    values = [
        hidden, normed_c, crossed, normed_b, received, mixed, normed_a, enc_hidden, enc_normed_b, enc_mixed, enc_normed
    ]
    grads = [down_in, rising_grad, cross_in, asked_grad, memory_grad, self_in, joint_grad]
    if nseq == 4 and nnbr == 8:
        heights = [
            (v.shape[1] // nnbr, w.shape[1])
            for v, w in zip(
                values,
                [feeddown, feedup, crossmerge, crossquery, memorymap, selfmerge, selfjoint, coderdown, coderup, codermerge, coderjoint],
            )
        ]
        sums = backward(
            returned,
            [
                enc_plain_c.astype(BF16),
                jnp.broadcast_to(enc_inverse_c, (flat, LANES)),
                enc_slope,
                enc_plain_b.astype(BF16),
                jnp.broadcast_to(enc_inverse_b, (flat, LANES)),
                enc_joint.reshape(flat, 3 * D),
            ],
            [codertop[None], codermid[None]],
            [coderdown, coderup, codermerge],
            values,
            grads,
            heights,
        )
    else:
        upper_total = norm_backward(
            jnp.concatenate(returned, axis=0).astype(F32), enc_plain_c, enc_inverse_c, codertop
        )
        enc_down_in = upper_total.astype(BF16)
        enc_rising_grad = (enc_slope.astype(F32) * times_back(enc_down_in, coderdown)).astype(BF16)
        middle_total = upper_total + norm_backward(
            times_back(enc_rising_grad, coderup), enc_plain_b, enc_inverse_b, codermid
        )
        enc_merge_in = middle_total.astype(BF16)
        enc_mixed_grad = times_back(enc_merge_in, codermerge).astype(BF16).reshape(count, places, D)
        enc_joint_grad = enc_attend_back(enc_joint, enc_mixed_grad).reshape(flat, 3 * D)
        grads += [enc_down_in, enc_rising_grad, enc_merge_in, enc_joint_grad]
        sums = [weight_grad(v, g).astype(BF16) for v, g in zip(values, grads)]
        ways = (False, True, False, False, False, False, False, True, False, True, True)
        sums = [reduce_group([total], sizes, way)[0] for total, way in zip(sums, ways)]
    sums, gain_grads = finish(
        sums,
        [selfgain, crossgain, feedgain, codergain, codermid, codertop],
        [selfjoint, crossquery, feedup, coderjoint, coderup, memorymap],
        nnbr,
    )
    (
        grad_feeddown,
        grad_feedup,
        grad_crossmerge,
        grad_crossquery,
        grad_memorymap,
        grad_selfmerge,
        grad_selfjoint,
        grad_coderdown,
        grad_coderup,
        grad_codermerge,
        grad_coderjoint,
    ) = sums
    grad_selfgain, grad_crossgain, grad_feedgain, grad_codergain, grad_codermid, grad_codertop = gain_grads
    return (
        output,
        input_grad,
        grad_selfgain,
        grad_selfjoint,
        grad_selfmerge,
        grad_crossgain,
        grad_crossquery,
        grad_crossmerge,
        grad_feedgain,
        grad_feedup,
        grad_feeddown,
        grad_codergain,
        grad_coderjoint,
        grad_codermerge,
        grad_codermid,
        grad_coderup,
        grad_coderdown,
        grad_codertop,
        grad_memorymap,
    )


def solution(mesh):
    spread = ("seq", "nbr")
    sizes = (mesh.shape["seq"], mesh.shape["nbr"])
    placed = (
        P(spread, None, None),
        P(spread, None, None),
        P(spread, None, None),
        P(spread),
        P(spread, None),
    ) + (P(),) * 17
    gain, weight = P("nbr"), P("nbr", None)
    return jax.shard_map(
        partial(body, sizes),
        mesh=mesh,
        in_specs=placed,
        out_specs=(
            P(spread, None, None),
            P(spread, None, None),
            gain,
            weight,
            weight,
            gain,
            weight,
            weight,
            gain,
            weight,
            weight,
            gain,
            weight,
            weight,
            gain,
            weight,
            weight,
            gain,
            weight,
        ),
        check_vma=False,
    )
```

```python
from functools import partial

import jax
import jax.numpy as jnp
from jax import lax
from jax.experimental import pallas as pl
from jax.experimental.pallas import tpu as pltpu
from jax.sharding import PartitionSpec as P

D = 768
HEADS = 12
HD = 64
CH = 64
PAIRS = HEADS // 2
LANES = 2 * HD
SCALE = HD ** (-0.5)
F32 = jnp.float32
BF16 = jnp.bfloat16
MESH = pl.DeviceIdType.MESH


def norm_backward(grad, normed, inverse, gain):
    scaled = grad * gain
    inner = jnp.mean(scaled * normed, axis=-1, keepdims=True)
    return inverse * (scaled - jnp.mean(scaled, axis=-1, keepdims=True) - normed * inner)


def times(values, weight):
    return lax.dot_general(values, weight, (((1,), (0,)), ((), ())), preferred_element_type=F32)


def times_back(grad, weight):
    return lax.dot_general(grad, weight, (((1,), (1,)), ((), ())), preferred_element_type=F32)


def weight_grad(values, grad):
    return lax.dot_general(values, grad, (((0,), (0,)), ((), ())), preferred_element_type=F32)


def curve(rising):
    square = rising * rising
    bend = jnp.tanh(rising * (0.7978845608028654 + 0.035677408136300125 * square))
    half = 0.5 * (1.0 + bend)
    slope = half + 0.5 * rising * (1.0 - bend * bend) * (0.7978845608028654 + 0.10703222440890037 * square)
    return (rising * half).astype(BF16), slope.astype(BF16)


def dot_nt(a, b):
    return lax.dot_general(a, b, (((1,), (1,)), ((), ())), preferred_element_type=F32)


def dot_nn(a, b):
    return lax.dot_general(a, b, (((1,), (0,)), ((), ())), preferred_element_type=F32)


def dot_tn(a, b):
    return lax.dot_general(a, b, (((0,), (0,)), ((), ())), preferred_element_type=F32)


def stack_pair(block):
    lane = lax.broadcasted_iota(jnp.int32, block.shape, 1)
    zero = jnp.zeros_like(block)
    return jnp.concatenate([jnp.where(lane < HD, block, zero), jnp.where(lane >= HD, block, zero)], axis=0)


def unstack_pair(stacked):
    half = stacked.shape[0] // 2
    lane = lax.broadcasted_iota(jnp.int32, (half, LANES), 1)
    return jnp.where(lane < HD, stacked[:half], stacked[half:])


def halves(block):
    width = block.shape[1] // 2
    return block[:, :width], block[:, width:]


def softmax_halves(products, allowed):
    parts = []
    for scores in halves(products):
        scores = scores * SCALE
        if allowed is not None:
            scores = jnp.where(allowed, scores, -1000000000.0)
        exponent = jnp.exp(scores - jnp.max(scores, axis=-1, keepdims=True))
        parts.append(exponent * (1.0 / jnp.sum(exponent, axis=-1, keepdims=True)))
    return parts


def rounded_halves(parts):
    return jnp.concatenate([part.astype(BF16) for part in parts], axis=1)


def pairs_forward(items, allowed=None):
    scores = [dot_nt(queries, stack_pair(keys)) for queries, keys, _ in items]
    probs = [rounded_halves(softmax_halves(block, allowed)) for block in scores]
    return [dot_nn(block, stack_pair(values)).astype(BF16) for block, (_, _, values) in zip(probs, items)]


def pairs_backward(items, allowed=None):
    stacked = [stack_pair(keys) for _, keys, _, _ in items]
    scores = [dot_nt(item[0], keys) for item, keys in zip(items, stacked)]
    prob_grads = [dot_nt(item[3], stack_pair(item[2])) for item in items]
    probs = [softmax_halves(block, allowed) for block in scores]
    value_grads = [unstack_pair(dot_tn(rounded_halves(block), item[3])) for block, item in zip(probs, items)]
    score_grads = []
    for block, grad in zip(probs, prob_grads):
        parts = []
        for prob, part in zip(block, halves(grad)):
            inner = jnp.sum(prob * part, axis=-1, keepdims=True)
            parts.append(prob * (part - inner) * SCALE)
        score_grads.append(rounded_halves(parts))
    query_grads = [dot_nn(grad, keys) for grad, keys in zip(score_grads, stacked)]
    key_grads = [unstack_pair(dot_tn(grad, item[0])) for grad, item in zip(score_grads, items)]
    return [tuple(g.astype(BF16) for g in grads) for grads in zip(query_grads, key_grads, value_grads)]


def col(pair, third=0):
    return slice(third * D + pair * LANES, third * D + (pair + 1) * LANES)


def estimate(flops, nbytes, exps=0):
    return pl.CostEstimate(flops=int(flops), bytes_accessed=int(nbytes), transcendentals=int(exps))


def enc_attend_back_kernel(joint_ref, grad_ref, out_ref):
    items = [
        tuple(joint_ref[0, :, col(p, third)] for third in range(3)) + (grad_ref[0, :, col(p)],) for p in range(PAIRS)
    ]
    for p, grads in enumerate(pairs_backward(items)):
        for third in range(3):
            out_ref[0, :, col(p, third)] = grads[third]


def enc_attend_back(joint, grad):
    count, rows, _ = joint.shape
    return pl.pallas_call(
        enc_attend_back_kernel,
        grid=(count,),
        in_specs=[
            pl.BlockSpec((1, rows, 3 * D), lambda i: (i, 0, 0)),
            pl.BlockSpec((1, rows, D), lambda i: (i, 0, 0)),
        ],
        out_specs=pl.BlockSpec((1, rows, 3 * D), lambda i: (i, 0, 0)),
        out_shape=jax.ShapeDtypeStruct((count, rows, 3 * D), BF16),
        cost_estimate=estimate(10 * count * rows * rows * D * 4, count * rows * D * 14, count * rows * rows * HEADS),
        name="enc_attend_back",
    )(joint, grad)


def causal_mask(rows, length):
    row = lax.broadcasted_iota(jnp.int32, (rows, rows), 0)
    column = lax.broadcasted_iota(jnp.int32, (rows, rows), 1)
    return (column <= row) & (column < length)


def norm_tile(values, gain):
    centred = values - jnp.mean(values, axis=-1, keepdims=True)
    inverse = lax.rsqrt(jnp.mean(centred * centred, axis=-1, keepdims=True) + 1e-05)
    plain = centred * inverse
    return (plain * gain).astype(BF16), plain, inverse


def norm_back_tile(grad, normed, inverse, gain):
    scaled = grad * gain
    inner = jnp.mean(scaled * normed, axis=-1, keepdims=True)
    return inverse * (scaled - jnp.mean(scaled, axis=-1, keepdims=True) - normed * inner)


class Loads:
    def __init__(self, sems, *pairs):
        self.copies = [pltpu.make_async_copy(src, dst, sems.at[k]) for k, (src, dst) in enumerate(pairs)]
        for copy in self.copies:
            copy.start()

    def wait(self, k):
        self.copies[k].wait()


def live_rows(rows, length):
    row = lax.broadcasted_iota(jnp.int32, (rows, 1), 0)
    return (row // CH * CH < length).astype(F32)


def decoder_kernel(nseq, length_ref, order_ref, tokens, out_grad, gain_a, gain_b, gain_c, *refs):
    received, selfjoint, selfmerge, crossquery, memorymap, crossmerge, feedup, feeddown = refs[:8]
    (
        output, normed_a, plain_a, inverse_a, joint, mixed, normed_b, plain_b, inverse_b, crossed, cross_in,
        asked_grad, memory_grad, normed_c, hidden, rising_grad, cross_total, back,
    ) = kept = refs[26:44]
    outs = refs[8:26]
    (
        received_in, joint_w, merge_w, query_w, map_w, cross_w, up_w, down_w, slope, memory, asked, crossed_grad, sems, store_sems
    ) = refs[44:]
    stores = []

    def store(*done):
        for k, (src, dst) in enumerate(zip(kept, outs)):
            if any(src is ref for ref in done):
                stores.append(pltpu.make_async_copy(src, dst, store_sems.at[k]))
                stores[-1].start()

    rows = tokens.shape[0]
    count, places, _ = memory.shape
    flat = count * places
    length = length_ref[0]
    loads = Loads(
        sems,
        (selfjoint, joint_w),
        (selfmerge, merge_w),
        (crossquery, query_w),
        (received, received_in),
        (memorymap, map_w),
        (crossmerge, cross_w),
        (feedup, up_w),
        (feeddown, down_w),
    )

    def keep_inverse(ref, inverse):
        ref[...] = jnp.broadcast_to(inverse, ref.shape)

    sequence = tokens[...].astype(F32)
    normed, plain, inverse = norm_tile(sequence, gain_a[...])
    normed_a[...] = normed
    plain_a[...] = plain.astype(BF16)
    keep_inverse(inverse_a, inverse)
    store(normed_a, plain_a, inverse_a)
    loads.wait(0)
    for third in range(3):
        lanes = slice(third * D, (third + 1) * D)
        joint[:, lanes] = dot_nn(normed_a[...], joint_w[:, lanes]).astype(BF16)
    store(joint)
    allowed = causal_mask(rows, length)
    for group in range(0, PAIRS, 3):
        chosen = range(group, group + 3)
        items = [tuple(joint[:, col(p, third)] for third in range(3)) for p in chosen]
        for p, block in zip(chosen, pairs_forward(items, allowed)):
            mixed[:, col(p)] = block
    loads.wait(1)
    after_self = sequence + dot_nn(mixed[...], merge_w[...])
    normed, plain, inverse = norm_tile(after_self, gain_b[...])
    normed_b[...] = normed
    plain_b[...] = plain.astype(BF16)
    keep_inverse(inverse_b, inverse)
    store(mixed, normed_b, plain_b, inverse_b)
    loads.wait(2)
    asked[...] = dot_nn(normed_b[...], query_w[...]).astype(BF16)

    loads.wait(3)
    loads.wait(4)

    def project(block, carry):
        window = pl.ds(pl.multiple_of(block * rows, rows), rows)
        nearby = pl.ds(block * (rows // places), rows // places)
        for half in range(2):
            lanes = slice(half * D, (half + 1) * D)
            tile = dot_nn(received_in[window], map_w[:, lanes]).astype(BF16)
            memory[nearby, :, lanes] = tile.reshape(rows // places, places, D)
        return carry

    lax.fori_loop(0, flat // rows, project, 0)

    cap = count // nseq
    me = lax.axis_index("seq")

    def span_items(span):
        first, second = (((slot // cap) ^ me) * cap + slot % cap for slot in (order_ref[0, 2 * span], order_ref[0, 2 * span + 1]))
        window = pl.ds(pl.multiple_of(span * CH, CH), CH)
        items = [
            (asked[window, col(p)],)
            + tuple(
                jnp.concatenate([memory[first, :, col(p, third)], memory[second, :, col(p, third)]], axis=0)
                for third in range(2)
            )
            for p in range(PAIRS)
        ]
        return window, first, second, items

    def cross_forward(span, carry):
        window, _, _, items = span_items(span)
        for p, block in enumerate(pairs_forward(items)):
            crossed[window, col(p)] = block
        return carry

    lax.fori_loop(0, rows // CH, cross_forward, 0)
    live = live_rows(rows, length)
    loads.wait(5)
    after_cross = after_self + dot_nn(crossed[...], cross_w[...]) * live
    normed, plain_c, inverse_c = norm_tile(after_cross, gain_c[...])
    normed_c[...] = normed
    store(crossed, normed_c)
    loads.wait(6)
    loads.wait(7)
    total = after_cross
    for f in range(hidden.shape[1] // D):
        lanes = slice(f * D, (f + 1) * D)
        bent, tilt = curve(dot_nn(normed_c[...], up_w[:, lanes]))
        hidden[:, lanes] = bent
        slope[:, lanes] = tilt
        total = total + dot_nn(bent, down_w[lanes])
    output[...] = total.astype(BF16)
    store(output, hidden)

    total = None
    for f in range(hidden.shape[1] // D):
        lanes = slice(f * D, (f + 1) * D)
        rounded = (dot_nt(out_grad[...], down_w[lanes]) * slope[:, lanes].astype(F32)).astype(BF16)
        rising_grad[:, lanes] = rounded
        part = dot_nt(rounded, up_w[:, lanes])
        total = part if total is None else total + part
    total = out_grad[...].astype(F32) + norm_back_tile(total, plain_c, inverse_c, gain_c[...])
    cross_total[...] = total
    cross_in[...] = (total * live).astype(BF16)
    store(rising_grad, cross_total, cross_in)
    crossed_grad[...] = dot_nt(cross_in[...], cross_w[...]).astype(BF16)

    def cross_back(span, carry):
        window, first, second, items = span_items(span)
        items = [item + (crossed_grad[window, col(p)],) for p, item in enumerate(items)]
        for p, (dq, dk, dv) in enumerate(pairs_backward(items)):
            asked_grad[window, col(p)] = dq
            memory_grad[first, :, col(p, 0)] = dk[:places]
            memory_grad[second, :, col(p, 0)] = dk[places:]
            memory_grad[first, :, col(p, 1)] = dv[:places]
            memory_grad[second, :, col(p, 1)] = dv[places:]
        return carry

    lax.fori_loop(0, rows // CH, cross_back, 0)
    store(asked_grad, memory_grad)

    def project_back(block, carry):
        window = pl.ds(pl.multiple_of(block * rows, rows), rows)
        nearby = pl.ds(block * (rows // places), rows // places)
        back[window] = dot_nt(memory_grad[nearby].reshape(rows, 2 * D), map_w[...]).astype(BF16)
        return carry

    lax.fori_loop(0, flat // rows, project_back, 0)
    store(back)
    for copy in stores:
        copy.wait()


def decoder(tokens, out_grad, lengths, order, received, gains, weights, count, nseq):
    rows = tokens.shape[0]
    places = received.shape[0] // count
    hidden = weights[5].shape[1]
    inside = pl.BlockSpec(memory_space=pltpu.VMEM)
    scalar = pl.BlockSpec(memory_space=pltpu.SMEM)
    anywhere = pl.BlockSpec(memory_space=pl.ANY)
    narrow = jax.ShapeDtypeStruct((rows, D), BF16)
    wide = jax.ShapeDtypeStruct((rows, hidden), BF16)
    inverse = jax.ShapeDtypeStruct((rows, LANES), F32)
    outs = [
        narrow, narrow, narrow, inverse, jax.ShapeDtypeStruct((rows, 3 * D), BF16), narrow, narrow, narrow, inverse, narrow, narrow,
        narrow, jax.ShapeDtypeStruct((count, places, 2 * D), BF16), narrow, wide, wide,
        jax.ShapeDtypeStruct((rows, D), F32), jax.ShapeDtypeStruct((count * places, D), BF16),
    ]
    return pl.pallas_call(
        partial(decoder_kernel, nseq),
        in_specs=[scalar] * 2 + [inside] * 5 + [anywhere] * 8,
        out_specs=[pl.BlockSpec(memory_space=pltpu.HBM)] * len(outs),
        out_shape=outs,
        scratch_shapes=[pltpu.VMEM(out.shape, out.dtype) for out in outs]
        + [pltpu.VMEM(received.shape, BF16)]
        + [pltpu.VMEM(weight.shape, BF16) for weight in weights]
        + [
            pltpu.VMEM((rows, hidden), BF16),
            pltpu.VMEM((count, places, 2 * D), BF16),
            pltpu.VMEM((rows, D), BF16),
            pltpu.VMEM((rows, D), BF16),
            pltpu.SemaphoreType.DMA((8,)),
            pltpu.SemaphoreType.DMA((len(outs),)),
        ],
        compiler_params=pltpu.CompilerParams(vmem_limit_bytes=60 * 2**20),
        cost_estimate=estimate(22e9, 40e6),
        name="decoder",
    )(lengths, order, tokens, out_grad, *gains, received, *weights)


def self_back_kernel(length_ref, *refs):
    asked_grad, cross_total, plain_b, inverse_b, gain_b, joint, plain_a, inverse_a, gain_a = refs[:9]
    crossquery, selfmerge, selfjoint = refs[9:12]
    self_in, joint_grad, input_grad = refs[12:15]
    query_w, merge_w, joint_w, mixed_grad, sems = refs[15:]
    rows = joint.shape[0]
    loads = Loads(sems, (crossquery, query_w), (selfmerge, merge_w), (selfjoint, joint_w))
    loads.wait(0)
    total = cross_total[...] + norm_back_tile(
        dot_nt(asked_grad[...], query_w[...]), plain_b[...].astype(F32), inverse_b[:, :1], gain_b[...]
    )
    self_in[...] = total.astype(BF16)
    loads.wait(1)
    mixed_grad[...] = dot_nt(self_in[...], merge_w[...]).astype(BF16)
    allowed = causal_mask(rows, length_ref[0])
    for group in range(0, PAIRS, 3):
        chosen = range(group, group + 3)
        items = [tuple(joint[:, col(p, third)] for third in range(3)) + (mixed_grad[:, col(p)],) for p in chosen]
        for p, grads in zip(chosen, pairs_backward(items, allowed)):
            for third in range(3):
                joint_grad[:, col(p, third)] = grads[third]
    loads.wait(2)
    back = dot_nt(joint_grad[...], joint_w[...])
    input_grad[...] = total + norm_back_tile(back, plain_a[...].astype(F32), inverse_a[:, :1], gain_a[...])


def self_back(lengths, asked_grad, cross_total, plain_b, inverse_b, gain_b, joint, plain_a, inverse_a, gain_a, weights):
    rows = joint.shape[0]
    inside = pl.BlockSpec(memory_space=pltpu.VMEM)
    return pl.pallas_call(
        self_back_kernel,
        in_specs=[pl.BlockSpec(memory_space=pltpu.SMEM)] + [inside] * 9 + [pl.BlockSpec(memory_space=pl.ANY)] * 3,
        out_specs=[inside] * 3,
        out_shape=[
            jax.ShapeDtypeStruct((rows, D), BF16),
            jax.ShapeDtypeStruct((rows, 3 * D), BF16),
            jax.ShapeDtypeStruct((rows, D), F32),
        ],
        scratch_shapes=[pltpu.VMEM(weight.shape, BF16) for weight in weights]
        + [pltpu.VMEM((rows, D), BF16), pltpu.SemaphoreType.DMA((3,))],
        compiler_params=pltpu.CompilerParams(vmem_limit_bytes=40 * 2**20),
        cost_estimate=estimate(8e9, 15e6),
        name="self_back",
    )(lengths, asked_grad, cross_total, plain_b, inverse_b, gain_b, joint, plain_a, inverse_a, gain_a, *weights)


def swap(value, axis, size, mask):
    return lax.ppermute(value, axis, [(i, i ^ mask) for i in range(size)])


def bit_of(axis, mask):
    return (lax.axis_index(axis) // mask) % 2


def pick(value, dim, index):
    return lax.dynamic_index_in_dim(value, index, dim, keepdims=False)


def halve(value, dim, axis, size, mask):
    bit = bit_of(axis, mask)
    arrived = swap(pick(value, dim, 1 - bit), axis, size, mask)
    return (pick(value, dim, bit).astype(F32) + arrived.astype(F32)).astype(BF16)


def join(value, dim, axis, size, mask):
    arrived = swap(value, axis, size, mask)
    bit = bit_of(axis, mask)
    return jnp.where(
        bit == 0, jnp.concatenate([value, arrived], axis=dim), jnp.concatenate([arrived, value], axis=dim)
    )


def masks(size):
    found, mask = [], 1
    while mask < size:
        found.append(mask)
        mask *= 2
    return found


def reduce_group(totals, sizes, rows_first):
    nseq, nnbr = sizes
    core = bit_of("seq", 1)
    parts = []
    for whole in totals:
        height, width = whole.shape
        parts.append(halve(whole.reshape(height, 2, width // 2), 1, "seq", nseq, 1))
    widths = [part.shape[1] for part in parts]
    total = parts[0] if len(parts) == 1 else jnp.concatenate(parts, axis=1)
    bits = masks(nnbr)
    rows = total.shape[0] // nnbr
    total = total.reshape((2,) * len(bits) + (rows, total.shape[1]))
    seq_bits = masks(nseq)[1:]

    def over_seq(total):
        for mask in seq_bits:
            shape = total.shape
            total = total.reshape(shape[:-2] + (2, shape[-2] // 2, shape[-1]))
            total = halve(total, total.ndim - 3, "seq", nseq, mask)
        return total

    def over_nbr(total):
        left = list(reversed(bits))
        for mask in bits:
            total = halve(total, left.index(mask), "nbr", nnbr, mask)
            left.remove(mask)
        return total

    if rows_first:
        total = over_nbr(over_seq(total))
        for mask in reversed(seq_bits):
            total = join(total, 0, "seq", nseq, mask)
    else:
        total = over_nbr(total)
        for mask in seq_bits:
            total = (total.astype(F32) + swap(total, "seq", nseq, mask).astype(F32)).astype(BF16)
    other = swap(total, "seq", nseq, 1)
    results, start = [], 0
    for width in widths:
        mine, theirs = total[:, start : start + width], other[:, start : start + width]
        results.append(
            jnp.where(
                core == 0, jnp.concatenate([mine, theirs], axis=1), jnp.concatenate([theirs, mine], axis=1)
            ).astype(F32)
        )
        start += width
    return results


def flip(index, mask):
    for bit in masks(mask + 1):
        if mask & bit:
            index = index + bit * (1 - 2 * ((lax.axis_index("seq") // bit) % 2))
    return index


def encoder_kernel(nseq, count, *refs):
    neighbours, gain_a, gain_b, gain_c, coderjoint, codermerge, coderup, coderdown = refs[:8]
    outs, received = refs[8:18], refs[18]
    entering, joint_w, merge_w, up_w, down_w = refs[19:24]
    kept, normed_c = refs[24:34], refs[34]
    load_sem, weight_sem, store_sem, send_sem, recv_sem = refs[35:]
    normed, joint, mixed, plain_b, inverse_b, normed_b, slope, hidden, plain_c, inverse_c = kept
    flat = entering.shape[0]
    rows, places = flat // nseq, flat // count
    s, n = lax.axis_index("seq"), lax.axis_index("nbr")

    barrier = pltpu.get_barrier_semaphore()
    for m in range(1, nseq):
        pl.semaphore_signal(barrier, inc=1, device_id=(flip(s, m), n), device_id_type=MESH)
    order = list(reversed(range(nseq)))
    loads = {}
    for m in order:
        source = pl.ds(pl.multiple_of(flip(s, m) * rows, rows), rows)
        loads[m] = pltpu.make_async_copy(neighbours.at[source], entering.at[pl.ds(m * rows, rows)], load_sem.at[m])
        loads[m].start()
    weights = Loads(weight_sem, (coderjoint, joint_w), (codermerge, merge_w), (coderup, up_w), (coderdown, down_w))
    pl.semaphore_wait(barrier, nseq - 1)

    stores, sends = [], []
    for turn, m in enumerate(order):
        window = pl.ds(m * rows, rows)
        loads[m].wait()
        embedded = entering[window].astype(F32)
        normed[window] = norm_tile(embedded, gain_a[...])[0]
        if turn == 0:
            weights.wait(0)
        for third in range(3):
            lanes = slice(third * D, (third + 1) * D)
            joint[window, lanes] = dot_nn(normed[window], joint_w[:, lanes]).astype(BF16)

        def attend(k, carry, m=m):
            inside = pl.ds(pl.multiple_of(m * rows + k * places, places), places)
            items = [tuple(joint[inside, col(p, third)] for third in range(3)) for p in range(PAIRS)]
            for p, block in enumerate(pairs_forward(items)):
                mixed[inside, col(p)] = block
            return carry

        lax.fori_loop(0, rows // places, attend, 0)
        if turn == 0:
            weights.wait(1)
        middle = embedded + dot_nn(mixed[window], merge_w[...])
        rounded, plain, inverse = norm_tile(middle, gain_b[...])
        normed_b[window] = rounded
        plain_b[window] = plain.astype(BF16)
        inverse_b[window] = jnp.broadcast_to(inverse, (rows, LANES))
        if turn == 0:
            weights.wait(2)
            weights.wait(3)
        total = middle
        for f in range(hidden.shape[1] // D):
            lanes = slice(f * D, (f + 1) * D)
            bent, tilt = curve(dot_nn(rounded, up_w[:, lanes]))
            hidden[window, lanes] = bent
            slope[window, lanes] = tilt
            total = total + dot_nn(bent, down_w[lanes])
        rounded, plain, inverse = norm_tile(total, gain_c[...])
        normed_c[window] = rounded
        plain_c[window] = plain.astype(BF16)
        inverse_c[window] = jnp.broadcast_to(inverse, (rows, LANES))
        if m == 0:
            stores.append(pltpu.make_async_copy(normed_c.at[window], received.at[window], store_sem.at[len(outs), m]))
            stores[-1].start()
        else:
            copy = pltpu.make_async_remote_copy(
                src_ref=normed_c.at[window],
                dst_ref=received.at[window],
                send_sem=send_sem.at[m],
                recv_sem=recv_sem.at[m],
                device_id=(flip(s, m), n),
                device_id_type=MESH,
            )
            copy.start()
            sends.append(copy)
        for k, (src, dst) in enumerate(zip(kept, outs)):
            stores.append(pltpu.make_async_copy(src.at[window], dst.at[window], store_sem.at[k, m]))
            stores[-1].start()
    for copy in stores + sends:
        copy.wait()


def encoder(neighbours, gains, weights, nseq):
    count, places, _ = neighbours.shape
    flat = count * places
    hidden = weights[2].shape[1]
    widths = (D, 3 * D, D, D, LANES, D, hidden, hidden, D, LANES)
    kinds = (BF16, BF16, BF16, BF16, F32, BF16, BF16, BF16, BF16, F32)
    anywhere = pl.BlockSpec(memory_space=pl.ANY)
    inside = pl.BlockSpec(memory_space=pltpu.VMEM)
    return pl.pallas_call(
        partial(encoder_kernel, nseq, count),
        in_specs=[anywhere] + [inside] * 3 + [anywhere] * 4,
        out_specs=[anywhere] * 11,
        out_shape=[jax.ShapeDtypeStruct((flat, w), k) for w, k in zip(widths, kinds)]
        + [jax.ShapeDtypeStruct((flat, D), BF16)],
        scratch_shapes=[pltpu.VMEM((flat, D), BF16)]
        + [pltpu.VMEM(weight.shape, BF16) for weight in weights]
        + [pltpu.VMEM((flat, w), k) for w, k in zip(widths, kinds)]
        + [
            pltpu.VMEM((flat, D), BF16),
            pltpu.SemaphoreType.DMA((nseq,)),
            pltpu.SemaphoreType.DMA((4,)),
            pltpu.SemaphoreType.DMA((11, nseq)),
            pltpu.SemaphoreType.DMA((nseq,)),
            pltpu.SemaphoreType.DMA((nseq,)),
        ],
        compiler_params=pltpu.CompilerParams(collective_id=1, has_side_effects=True, vmem_limit_bytes=60 * 2**20),
        cost_estimate=estimate(18e9, 50e6),
        name="encoder",
    )(neighbours.reshape(flat, D), *gains, *weights)


HALF = D // 2


MATRICES = 11
DOWN = (0, 7)
UNITS = (
    ((0, 0), (0, 1)),
    ((0, 2), (0, 3)),
    ((1, 0), (1, 1)),
    ((1, 2), (1, 3)),
    ((2, 0), (3, 0)),
    ((4, 0), (4, 1)),
    ((5, 0), (6, 0)),
    ((6, 1), (6, 2)),
    ((7, 0), (7, 1)),
    ((7, 2), (7, 3)),
    ((8, 0), (8, 1)),
    ((8, 2), (8, 3)),
    ((9, 0), (10, 0)),
    ((10, 1), (10, 2)),
)
CARRIED = {
    0: (("rows", 0, None),),
    1: (("heads", 0, (0, 1)),),
    2: (("rows", 1, None),),
    3: (("heads", 1, (0, 1)),),
    4: (("rows", 2, None),),
    5: (("heads", 2, (0,)),),
    6: (("rows", 3, None),),
    7: (("heads", 2, (1,)), ("heads", 3, (0,))),
    9: (("heads", 3, (1,)),),
}
TILE = 256


def backward_kernel(blocks, *refs):
    refs = list(refs)

    def take(number):
        taken = refs[:number]
        del refs[:number]
        return taken

    returned = take(blocks)
    plain_c, inverse_c, slope, plain_b, inverse_b, joint = take(6)
    gain_c, gain_b = take(2)
    coderdown, coderup, codermerge = take(3)
    values = take(MATRICES)
    grads = take(7)
    outs = take(MATRICES)
    (
        stage, first, own, mid, low_a, end_a, tail_a, low_b, end_b, tail_b, low_d, end_d, tail_d, tail_x, result,
        down_w, wide, merge_w, rising_grad, down_in, merge_in, joint_grad, mixed_grad,
        y_in, plain_in, inverse_in, slope_in, plain_in_b, inverse_in_b, joint_in, upper,
        feed_a, some_a, some_b,
        send_sem, recv_sem, local_sem,
    ) = refs
    rows = D // 8
    part = rows // 2
    flat = blocks * TILE
    s, n = lax.axis_index("seq"), lax.axis_index("nbr")
    c, x = s % 2, s // 2
    y, z1, z2 = n % 2, (n // 2) % 2, n // 4
    at_core, at_x = (s + 1 - 2 * c, n), (s + 2 - 4 * x, n)
    at_y, at_z1, at_z2 = (s, n + 1 - 2 * y), (s, n + 2 - 4 * z1), (s, n + 4 - 8 * z2)
    mine = pl.ds(pl.multiple_of(c * HALF, 128), HALF)
    other = pl.ds(pl.multiple_of((1 - c) * HALF, 128), HALF)
    kept = pl.ds(pl.multiple_of(x * part, 16), part)
    given = pl.ds(pl.multiple_of((1 - x) * part, 16), part)

    barrier = pltpu.get_barrier_semaphore()
    for partner in (at_core, at_x, at_y, at_z1, at_z2):
        pl.semaphore_signal(barrier, inc=1, device_id=partner, device_id_type=MESH)
    pl.semaphore_wait(barrier, 5)

    pending = {}
    counts = {"local": 0, "remote": 0}

    def remote(key, src, dst, partner):
        index = counts["remote"]
        counts["remote"] += 1
        copy = pltpu.make_async_remote_copy(
            src_ref=src,
            dst_ref=dst,
            send_sem=send_sem.at[index],
            recv_sem=recv_sem.at[index],
            device_id=partner,
            device_id_type=MESH,
        )
        copy.start()
        pending[key] = copy

    def local(key, src, dst):
        copy = pltpu.make_async_copy(src, dst, local_sem.at[counts["local"]])
        counts["local"] += 1
        copy.start()
        pending.setdefault(key, []).append(copy)

    def arrived(key):
        for copy in pending.pop(key, []):
            copy.wait()


    def fetch(u):
        if u == 0:
            local(("unit", 0), values[0], feed_a)
            local(("unit", 0), grads[0], some_b.at[pl.ds(0, TILE), pl.ds(0, D)])
        elif u in (2, 3):
            if u == 2:
                local(("unit", u), values[1], some_a.at[pl.ds(0, TILE)])
            local(("unit", u), grads[1].at[:, pl.ds((u - 2) * 2 * D, 2 * D)], some_b.at[pl.ds(0, TILE)])
        elif u == 4:
            for k in range(2):
                local(("unit", u), values[2 + k], some_a.at[pl.ds(k * TILE, TILE)])
                local(("unit", u), grads[2 + k], some_b.at[pl.ds(0, TILE), pl.ds(k * D, D)])
        elif u == 5:
            local(("unit", u), values[4], some_a)
            local(("unit", u), grads[4], some_b)
        elif u == 6:
            for k in range(2):
                local(("unit", u), values[5 + k], some_a.at[pl.ds(k * TILE, TILE)])
            local(("unit", u), grads[5], some_b.at[pl.ds(0, TILE), pl.ds(0, D)])
            local(("unit", u), grads[6].at[:, pl.ds(0, D)], some_b.at[pl.ds(0, TILE), pl.ds(D, D)])
        elif u == 7:
            local(("unit", u), grads[6].at[:, pl.ds(D, 2 * D)], some_b.at[pl.ds(0, TILE)])
        elif u == 8:
            local(("unit", 8), values[7], wide)
            for k in range(3):
                local(("unit", 10), values[8 + k], down_w.at[pl.ds(k * flat, flat)])

    def operands(u, k):
        left = pl.ds(k * D, D)
        if u in (2, 3):
            return some_a.at[pl.ds(0, TILE)], some_b.at[pl.ds(0, TILE), left]
        if u in (4, 6):
            return some_a.at[pl.ds(k * TILE, TILE)], some_b.at[pl.ds(0, TILE), left]
        if u == 5:
            return some_a, some_b.at[:, left]
        if u == 7:
            return some_a.at[pl.ds(TILE, TILE)], some_b.at[pl.ds(0, TILE), left]
        if u in (10, 11):
            return down_w.at[pl.ds(0, flat)], rising_grad.at[:, pl.ds(((u - 10) * 2 + k) * D, D)]
        if u == 12:
            return down_w.at[pl.ds((1 + k) * flat, flat)], merge_in if k == 0 else joint_grad.at[:, pl.ds(0, D)]
        return down_w.at[pl.ds(2 * flat, flat)], joint_grad.at[:, pl.ds((1 + k) * D, D)]

    def product(u):
        if UNITS[u][0][0] in DOWN:
            left = feed_a if u < 2 else wide
            right = some_b.at[pl.ds(0, TILE), pl.ds(0, D)] if u < 2 else down_in
            begin = (u % 2) * 2 * rows

            def one(shard, carry):
                columns = left[:, pl.ds(pl.multiple_of(shard * 4 * rows, 128), 4 * rows)]
                tile = dot_tn(columns[:, begin : begin + 2 * rows], right[...]).astype(BF16)
                stage[0, shard] = tile[:rows]
                stage[1, shard] = tile[rows:]
                return carry

            lax.fori_loop(0, 8, one, 0)
            return
        for k in range(2):
            left, right = operands(u, k)
            stage[k] = dot_tn(left[...], right[...]).astype(BF16).reshape(8, rows, D)


    def slot(u):
        return u % 5, u % 4

    def straight(u):
        return u % 4 != 0

    def stage0(u):
        arrived(("unit", u))
        product(u)
        remote(("core", u), stage.at[:, :, :, other], first.at[u % 2], at_core)

    def stage1(u):
        five, four = slot(u)
        pending.pop(("core", u)).wait()

        def one(k, carry):
            k, a, b, d = k // 8, (k // 4) % 2, (k // 2) % 2, k % 2
            shard = 4 * a + 2 * b + d
            own[five, k, a, b, d] = stage[k, shard, :, mine] + first[u % 2, k, shard]
            return carry

        lax.fori_loop(0, 16, one, 0)
        remote(("a", u), own.at[five, 0, :, :, :, given], mid.at[four], at_x)
        if straight(u):
            remote(("b", u), own.at[five, 1, :, :, 1 - y], low_b.at[four], at_y)
        else:
            remote(("b", u), own.at[five, 1, :, 1 - z1], low_d, at_z1)

    def stage2(u):
        five, four = slot(u)
        pending.pop(("a", u)).wait()
        pending.pop(("b", u)).wait()
        for a in range(2):
            for b in range(2):
                for d in range(2):
                    own[five, 0, a, b, d, kept] = own[five, 0, a, b, d, kept] + mid[four, a, b, d]
        for a in range(2):
            for b in range(2):
                if straight(u):
                    own[five, 1, a, b, y] = own[five, 1, a, b, y] + low_b[four, a, b]
                else:
                    own[five, 1, a, z1, b] = own[five, 1, a, z1, b] + low_d[a, b]
        remote(("a", u), own.at[five, 0, :, :, 1 - y, kept], low_a.at[four], at_y)
        if straight(u):
            remote(("b", u), own.at[five, 1, :, 1 - z1, y], end_b.at[four], at_z1)
        else:
            remote(("b", u), own.at[five, 1, 1 - z2, z1], end_d, at_z2)

    def stage3(u):
        five, four = slot(u)
        pending.pop(("a", u)).wait()
        pending.pop(("b", u)).wait()
        for a in range(2):
            for b in range(2):
                own[five, 0, a, b, y, kept] = own[five, 0, a, b, y, kept] + low_a[four, a, b]
            if straight(u):
                own[five, 1, a, z1, y] = own[five, 1, a, z1, y] + end_b[four, a]
            else:
                own[five, 1, z2, z1, a] = own[five, 1, z2, z1, a] + end_d[a]
        remote(("a", u), own.at[five, 0, :, 1 - z1, y, kept], end_a.at[four], at_z1)
        if straight(u):
            remote(("b", u), own.at[five, 1, 1 - z2, z1, y], tail_b.at[four], at_z2)
        else:
            remote(("b", u), own.at[five, 1, z2, z1, 1 - y], tail_d, at_y)

    def stage4(u):
        five, four = slot(u)
        pending.pop(("a", u)).wait()
        pending.pop(("b", u)).wait()
        for a in range(2):
            own[five, 0, a, z1, y, kept] = own[five, 0, a, z1, y, kept] + end_a[four, a]
        own[five, 1, z2, z1, y] = own[five, 1, z2, z1, y] + (tail_b[four] if straight(u) else tail_d[...])
        remote(("a", u), own.at[five, 0, 1 - z2, z1, y, kept], tail_a.at[four], at_z2)
        remote(("b", u), own.at[five, 1, z2, z1, y], tail_x.at[four], at_x)

    def stage5(u):
        five, four = slot(u)
        pending.pop(("a", u)).wait()
        pending.pop(("b", u)).wait()
        result[u % 6, 0, kept, mine] = own[five, 0, z2, z1, y, kept] + tail_a[four]
        result[u % 6, 1, :, mine] = own[five, 1, z2, z1, y] + tail_x[four]
        piece = result.at[u % 6, 0, kept, mine]
        remote(("a", u), piece, piece, at_x)

    def stage6(u):
        pending.pop(("a", u)).wait()
        piece = result.at[u % 6, :, :, mine]
        remote(("a", u), piece, piece, at_core)

    def stage7(u):
        pending.pop(("a", u)).wait()
        for k, (matrix, block) in enumerate(UNITS[u]):
            if matrix in DOWN:
                target = outs[matrix].at[pl.ds(block * rows, rows)]
            else:
                target = outs[matrix].at[:, pl.ds(block * D, D)]
            local(("out", u), result.at[u % 6, k], target)

    def stage8(u):
        arrived(("out", u))

    stages = (stage0, stage1, stage2, stage3, stage4, stage5, stage6, stage7, stage8)


    def fetch_rows(block):
        window = pl.ds(block * TILE, TILE)
        local("rows", returned[block], y_in)
        local("rows", plain_c.at[window], plain_in)
        local("rows", inverse_c.at[window], inverse_in)
        local("rows", slope.at[window], slope_in)
        local("rows", plain_b.at[window], plain_in_b)
        local("rows", inverse_b.at[window], inverse_in_b)

    def fetch_heads(block):
        local("heads", joint.at[pl.ds(block * TILE, TILE)], joint_in)

    def carry_rows(block):
        window = pl.ds(block * TILE, TILE)
        arrived("rows")
        total = norm_back_tile(
            y_in[...].astype(F32), plain_in[...].astype(F32), inverse_in[:, :1], gain_c[...]
        )
        upper[...] = total
        down_in[window] = total.astype(BF16)
        if block == 0:
            arrived("weights")
        for f in range(4):
            lanes = pl.ds(f * D, D)
            slopes = slope_in[:, lanes].astype(F32)
            rounded = (dot_nt(down_in[window], down_w[lanes]) * slopes).astype(BF16)
            rising_grad[window, lanes] = rounded
            back = dot_nt(rounded, wide[pl.ds(0, D), lanes])
            if f == 0:
                total = back
            else:
                total = total + back
        total = upper[...] + norm_back_tile(total, plain_in_b[...].astype(F32), inverse_in_b[:, :1], gain_b[...])
        rounded = total.astype(BF16)
        merge_in[window] = rounded
        mixed_grad[block] = dot_nt(rounded, merge_w[...]).astype(BF16)
        if block + 1 < blocks:
            fetch_rows(block + 1)
        else:
            fetch(8)

    def carry_heads(block, which):
        if which[0] == 0:
            arrived("heads")
        places = TILE // 2

        def one(k, carry):
            inside = pl.ds(pl.multiple_of(k * places, 128), places)
            outside = pl.ds(pl.multiple_of(block * TILE + k * places, 128), places)
            items = [
                tuple(joint_in[inside, col(p, third)] for third in range(3)) + (mixed_grad[block, inside, col(p)],)
                for p in range(PAIRS)
            ]
            for p, pieces in enumerate(pairs_backward(items)):
                for third in range(3):
                    joint_grad[outside, col(p, third)] = pieces[third]
            return carry

        lax.fori_loop(which[0], which[-1] + 1, one, 0)
        if which[-1] == 1 and block + 1 < blocks:
            fetch_heads(block + 1)

    fetch(0)
    fetch_rows(0)
    local("weights", coderdown, down_w)
    local("weights", coderup, wide.at[pl.ds(0, D)])
    local("weights", codermerge, merge_w)
    fetch_heads(0)
    for tick in range(len(UNITS) + len(stages) - 1):
        for level in (1, 0) + tuple(range(2, len(stages))):
            if 0 <= tick - level < len(UNITS):
                stages[level](tick - level)
        if 1 <= tick < 7:
            fetch(tick + 1)
        for kind, block, which in CARRIED.get(tick, ()):
            if kind == "rows":
                carry_rows(block)
            else:
                carry_heads(block, which)


def backward(returned, kept, gains, weights, values, grads, heights):
    blocks = len(returned)
    rows = D // 8
    part = rows // 2
    flat = blocks * TILE
    flat = kept[0].shape[0]
    widths = [v.shape[1] if m in DOWN else 0 for m, v in enumerate(values)]
    anywhere = pl.BlockSpec(memory_space=pl.ANY)
    inside = pl.BlockSpec(memory_space=pltpu.VMEM)
    operands = list(returned) + list(kept) + list(gains) + list(weights) + list(values) + list(grads)
    specs = [anywhere] * len(operands)
    specs[blocks + 6] = specs[blocks + 7] = inside

    def room(*shape, dtype=BF16):
        return pltpu.VMEM(shape, dtype)

    return pl.pallas_call(
        partial(backward_kernel, blocks),
        in_specs=specs,
        out_specs=[anywhere] * MATRICES,
        out_shape=[jax.ShapeDtypeStruct(height, BF16) for height in heights],
        scratch_shapes=[
            room(2, 8, rows, D),
            room(2, 2, 8, rows, HALF),
            room(5, 2, 2, 2, 2, rows, HALF),
            room(4, 2, 2, 2, part, HALF),
            room(4, 2, 2, part, HALF),
            room(4, 2, part, HALF),
            room(4, part, HALF),
            room(4, 2, 2, rows, HALF),
            room(4, 2, rows, HALF),
            room(4, rows, HALF),
            room(2, 2, rows, HALF),
            room(2, rows, HALF),
            room(rows, HALF),
            room(4, rows, HALF),
            room(6, 2, rows, D),
            room(4 * D, D),
            room(flat, 4 * D),
            room(D, D),
            room(flat, 4 * D),
            room(flat, D),
            room(flat, D),
            room(flat, 3 * D),
            room(blocks, TILE, D),
            room(TILE, D),
            room(TILE, D),
            room(TILE, LANES, dtype=F32),
            room(TILE, 4 * D),
            room(TILE, D),
            room(TILE, LANES, dtype=F32),
            room(TILE, 3 * D),
            room(TILE, D, dtype=F32),
            room(TILE, 4 * D),
            room(flat, D),
            room(flat, 2 * D),
            pltpu.SemaphoreType.DMA((len(UNITS) * 12,)),
            pltpu.SemaphoreType.DMA((len(UNITS) * 12,)),
            pltpu.SemaphoreType.DMA((128,)),
        ],
        compiler_params=pltpu.CompilerParams(
            collective_id=0, has_side_effects=True, vmem_limit_bytes=62 * 2**20
        ),
        cost_estimate=estimate(45e9, 120e6),
        name="encoder_backward_and_sums",
    )(*operands)


GAINED = (6, 3, 1, 10, 8, 4)


def finish_kernel(nbr_ref, *refs):
    gains, sums, weights, outs, gain_outs = refs[:6], refs[6:17], refs[17:23], refs[23:34], refs[34:]
    for total, out in zip(sums, outs):
        out[...] = total[...].astype(F32)
    rows = gain_outs[0].shape[1]
    row = lax.broadcasted_iota(jnp.int32, (D, rows), 0)
    place = lax.broadcasted_iota(jnp.int32, (D, rows), 1) + nbr_ref[0] * rows
    own = lax.dot_general(
        jnp.concatenate([gain[...][None] for gain in gains], axis=0),
        (row == place).astype(F32),
        (((1,), (0,)), ((), ())),
        precision=lax.Precision.HIGHEST,
        preferred_element_type=F32,
    )
    for k, (matrix, weight, out) in enumerate(zip(GAINED, weights, gain_outs)):
        product = weight[...].astype(F32) * sums[matrix][...].astype(F32)
        summed = lax.dot_general(
            jnp.ones((8, product.shape[1]), F32),
            product,
            (((1,), (1,)), ((), ())),
            precision=lax.Precision.HIGHEST,
            preferred_element_type=F32,
        )
        out[...] = summed[:1] / own[k : k + 1]


def finish(sums, gains, weights, nnbr):
    rows = D // nnbr
    nbr = lax.axis_index("nbr").reshape(1).astype(jnp.int32)

    def whole(array):
        return pl.BlockSpec(array.shape, lambda i, nbr: (0,) * array.ndim)

    results = pl.pallas_call(
        finish_kernel,
        grid_spec=pltpu.PrefetchScalarGridSpec(
            num_scalar_prefetch=1,
            grid=(1,),
            in_specs=[whole(array) for array in gains + list(sums)]
            + [pl.BlockSpec((rows, weight.shape[1]), lambda i, nbr: (nbr[0], 0)) for weight in weights],
            out_specs=[whole(total) for total in sums] + [pl.BlockSpec((1, rows), lambda i, nbr: (0, 0))] * len(weights),
        ),
        out_shape=[jax.ShapeDtypeStruct(total.shape, F32) for total in sums]
        + [jax.ShapeDtypeStruct((1, rows), F32)] * len(weights),
        compiler_params=pltpu.CompilerParams(vmem_limit_bytes=56 * 2**20),
        cost_estimate=estimate(1e7, 20e6),
        name="finish",
    )(nbr, *gains, *sums, *weights)
    return results[: len(sums)], [grad.reshape(rows) for grad in results[len(sums) :]]


def body(
    sizes,
    tokens,
    neighbours,
    out_grad,
    lengths,
    slot_order,
    selfgain,
    selfjoint,
    selfmerge,
    crossgain,
    crossquery,
    crossmerge,
    feedgain,
    feedup,
    feeddown,
    codergain,
    coderjoint,
    codermerge,
    codermid,
    coderup,
    coderdown,
    codertop,
    memorymap,
):
    nseq, nnbr = sizes
    count, places, _ = neighbours.shape
    flat = count * places

    (
        enc_normed, enc_joint, enc_mixed, enc_plain_b, enc_inverse_b, enc_normed_b, enc_slope, enc_hidden, enc_plain_c, enc_inverse_c,
        received,
    ) = encoder(
        neighbours,
        [codergain, codermid, codertop],
        [coderjoint, codermerge, coderup, coderdown],
        nseq,
    )

    down_in = out_grad[0]
    (
        output, normed_a, plain_a, inverse_a, joint, mixed, normed_b, plain_b, inverse_b, crossed, cross_in,
        asked_grad, memory_grad, normed_c, hidden, rising_grad, cross_total, back,
    ) = decoder(
        tokens[0],
        down_in,
        lengths,
        slot_order,
        received,
        [selfgain, crossgain, feedgain],
        [selfjoint, selfmerge, crossquery, memorymap, crossmerge, feedup, feeddown],
        count,
        nseq,
    )
    memory_grad = memory_grad.reshape(flat, 2 * D)
    back = back.reshape(nseq, flat // nseq, D)
    returned = [back[m] if m == 0 else swap(back[m], "seq", nseq, m) for m in range(nseq)]
    self_in, joint_grad, input_grad = self_back(
        lengths,
        asked_grad,
        cross_total,
        plain_b,
        inverse_b,
        crossgain,
        joint,
        plain_a,
        inverse_a,
        selfgain,
        [crossquery, selfmerge, selfjoint],
    )
    output, input_grad = output[None], input_grad[None]

    values = [
        hidden, normed_c, crossed, normed_b, received, mixed, normed_a, enc_hidden, enc_normed_b, enc_mixed, enc_normed
    ]
    grads = [down_in, rising_grad, cross_in, asked_grad, memory_grad, self_in, joint_grad]
    if nseq == 4 and nnbr == 8:
        heights = [
            (v.shape[1] // nnbr, w.shape[1])
            for v, w in zip(
                values,
                [feeddown, feedup, crossmerge, crossquery, memorymap, selfmerge, selfjoint, coderdown, coderup, codermerge, coderjoint],
            )
        ]
        sums = backward(
            returned,
            [enc_plain_c, enc_inverse_c, enc_slope, enc_plain_b, enc_inverse_b, enc_joint],
            [codertop, codermid],
            [coderdown, coderup, codermerge],
            values,
            grads,
            heights,
        )
    else:
        upper_total = norm_backward(
            jnp.concatenate(returned, axis=0).astype(F32), enc_plain_c.astype(F32), enc_inverse_c[:, :1], codertop
        )
        enc_down_in = upper_total.astype(BF16)
        enc_rising_grad = (enc_slope.astype(F32) * times_back(enc_down_in, coderdown)).astype(BF16)
        middle_total = upper_total + norm_backward(
            times_back(enc_rising_grad, coderup), enc_plain_b.astype(F32), enc_inverse_b[:, :1], codermid
        )
        enc_merge_in = middle_total.astype(BF16)
        enc_mixed_grad = times_back(enc_merge_in, codermerge).astype(BF16).reshape(count, places, D)
        enc_joint_grad = enc_attend_back(enc_joint.reshape(count, places, 3 * D), enc_mixed_grad).reshape(flat, 3 * D)
        grads += [enc_down_in, enc_rising_grad, enc_merge_in, enc_joint_grad]
        sums = [weight_grad(v, g).astype(BF16) for v, g in zip(values, grads)]
        ways = (False, True, False, False, False, False, False, True, False, True, True)
        sums = [reduce_group([total], sizes, way)[0] for total, way in zip(sums, ways)]
    sums, gain_grads = finish(
        sums,
        [selfgain, crossgain, feedgain, codergain, codermid, codertop],
        [selfjoint, crossquery, feedup, coderjoint, coderup, memorymap],
        nnbr,
    )
    (
        grad_feeddown,
        grad_feedup,
        grad_crossmerge,
        grad_crossquery,
        grad_memorymap,
        grad_selfmerge,
        grad_selfjoint,
        grad_coderdown,
        grad_coderup,
        grad_codermerge,
        grad_coderjoint,
    ) = sums
    grad_selfgain, grad_crossgain, grad_feedgain, grad_codergain, grad_codermid, grad_codertop = gain_grads
    return (
        output,
        input_grad,
        grad_selfgain,
        grad_selfjoint,
        grad_selfmerge,
        grad_crossgain,
        grad_crossquery,
        grad_crossmerge,
        grad_feedgain,
        grad_feedup,
        grad_feeddown,
        grad_codergain,
        grad_coderjoint,
        grad_codermerge,
        grad_codermid,
        grad_coderup,
        grad_coderdown,
        grad_codertop,
        grad_memorymap,
    )


def solution(mesh):
    spread = ("seq", "nbr")
    sizes = (mesh.shape["seq"], mesh.shape["nbr"])
    placed = (
        P(spread, None, None),
        P(spread, None, None),
        P(spread, None, None),
        P(spread),
        P(spread, None),
    ) + (P(),) * 17
    gain, weight = P("nbr"), P("nbr", None)
    return jax.shard_map(
        partial(body, sizes),
        mesh=mesh,
        in_specs=placed,
        out_specs=(
            P(spread, None, None),
            P(spread, None, None),
            gain,
            weight,
            weight,
            gain,
            weight,
            weight,
            gain,
            weight,
            weight,
            gain,
            weight,
            weight,
            gain,
            weight,
            weight,
            gain,
            weight,
        ),
        check_vma=False,
    )
```

```python
from functools import partial

import jax
import jax.numpy as jnp
from jax import lax
from jax.experimental import pallas as pl
from jax.experimental.pallas import tpu as pltpu
from jax.sharding import PartitionSpec as P

D = 768
HEADS = 12
HD = 64
CH = 64
PAIRS = HEADS // 2
LANES = 2 * HD
SCALE = HD ** (-0.5)
F32 = jnp.float32
BF16 = jnp.bfloat16
MESH = pl.DeviceIdType.MESH


def norm_backward(grad, normed, inverse, gain):
    scaled = grad * gain
    inner = jnp.mean(scaled * normed, axis=-1, keepdims=True)
    return inverse * (scaled - jnp.mean(scaled, axis=-1, keepdims=True) - normed * inner)


def times(values, weight):
    return lax.dot_general(values, weight, (((1,), (0,)), ((), ())), preferred_element_type=F32)


def times_back(grad, weight):
    return lax.dot_general(grad, weight, (((1,), (1,)), ((), ())), preferred_element_type=F32)


def weight_grad(values, grad):
    return lax.dot_general(values, grad, (((0,), (0,)), ((), ())), preferred_element_type=F32)


def curve(rising):
    square = rising * rising
    bend = jnp.tanh(rising * (0.7978845608028654 + 0.035677408136300125 * square))
    half = 0.5 * (1.0 + bend)
    slope = half + 0.5 * rising * (1.0 - bend * bend) * (0.7978845608028654 + 0.10703222440890037 * square)
    return (rising * half).astype(BF16), slope.astype(BF16)


def dot_nt(a, b):
    return lax.dot_general(a, b, (((1,), (1,)), ((), ())), preferred_element_type=F32)


def dot_nn(a, b):
    return lax.dot_general(a, b, (((1,), (0,)), ((), ())), preferred_element_type=F32)


def dot_tn(a, b):
    return lax.dot_general(a, b, (((0,), (0,)), ((), ())), preferred_element_type=F32)


def stack_pair(block):
    lane = lax.broadcasted_iota(jnp.int32, block.shape, 1)
    zero = jnp.zeros_like(block)
    return jnp.concatenate([jnp.where(lane < HD, block, zero), jnp.where(lane >= HD, block, zero)], axis=0)


def unstack_pair(stacked):
    half = stacked.shape[0] // 2
    lane = lax.broadcasted_iota(jnp.int32, (half, LANES), 1)
    return jnp.where(lane < HD, stacked[:half], stacked[half:])


def halves(block):
    width = block.shape[1] // 2
    return block[:, :width], block[:, width:]


def softmax_halves(products, allowed):
    parts = []
    for scores in halves(products):
        scores = scores * SCALE
        if allowed is not None:
            scores = jnp.where(allowed, scores, -1000000000.0)
        exponent = jnp.exp(scores - jnp.max(scores, axis=-1, keepdims=True))
        parts.append(exponent * (1.0 / jnp.sum(exponent, axis=-1, keepdims=True)))
    return parts


def rounded_halves(parts):
    return jnp.concatenate([part.astype(BF16) for part in parts], axis=1)


def pairs_forward(items, allowed=None):
    scores = [dot_nt(queries, stack_pair(keys)) for queries, keys, _ in items]
    probs = [rounded_halves(softmax_halves(block, allowed)) for block in scores]
    return [dot_nn(block, stack_pair(values)).astype(BF16) for block, (_, _, values) in zip(probs, items)]


def pairs_backward(items, allowed=None):
    stacked = [stack_pair(keys) for _, keys, _, _ in items]
    scores = [dot_nt(item[0], keys) for item, keys in zip(items, stacked)]
    prob_grads = [dot_nt(item[3], stack_pair(item[2])) for item in items]
    probs = [softmax_halves(block, allowed) for block in scores]
    value_grads = [unstack_pair(dot_tn(rounded_halves(block), item[3])) for block, item in zip(probs, items)]
    score_grads = []
    for block, grad in zip(probs, prob_grads):
        parts = []
        for prob, part in zip(block, halves(grad)):
            inner = jnp.sum(prob * part, axis=-1, keepdims=True)
            parts.append(prob * (part - inner) * SCALE)
        score_grads.append(rounded_halves(parts))
    query_grads = [dot_nn(grad, keys) for grad, keys in zip(score_grads, stacked)]
    key_grads = [unstack_pair(dot_tn(grad, item[0])) for grad, item in zip(score_grads, items)]
    return [tuple(g.astype(BF16) for g in grads) for grads in zip(query_grads, key_grads, value_grads)]


def col(pair, third=0):
    return slice(third * D + pair * LANES, third * D + (pair + 1) * LANES)


def estimate(flops, nbytes, exps=0):
    return pl.CostEstimate(flops=int(flops), bytes_accessed=int(nbytes), transcendentals=int(exps))


def spans_backward(asked, memory, outgoing):
    spans = asked.shape[0] // CH
    queries, grads = (block.reshape(spans, CH, HEADS, HD) for block in (asked, outgoing))
    keys, values = (memory[:, k * D : (k + 1) * D].reshape(spans, -1, HEADS, HD) for k in range(2))

    def product(form, left, right):
        return jnp.einsum(form, left, right, preferred_element_type=F32)

    probs = jax.nn.softmax(product("brhd,bshd->bhrs", queries, keys) * SCALE, axis=-1)
    value_grad = product("bhrs,brhd->bshd", probs.astype(BF16), grads)
    prob_grad = product("brhd,bshd->bhrs", grads, values)
    inner = jnp.sum(probs * prob_grad, axis=-1, keepdims=True)
    score_grad = (probs * (prob_grad - inner) * SCALE).astype(BF16)
    query_grad = product("bhrs,bshd->brhd", score_grad, keys)
    key_grad = product("bhrs,brhd->bshd", score_grad, queries)
    memory_grad = jnp.concatenate([block.reshape(-1, D) for block in (key_grad, value_grad)], axis=1)
    return query_grad.reshape(-1, D).astype(BF16), memory_grad.astype(BF16)


def enc_attend_back_kernel(joint_ref, grad_ref, out_ref):
    items = [
        tuple(joint_ref[0, :, col(p, third)] for third in range(3)) + (grad_ref[0, :, col(p)],) for p in range(PAIRS)
    ]
    for p, grads in enumerate(pairs_backward(items)):
        for third in range(3):
            out_ref[0, :, col(p, third)] = grads[third]


def enc_attend_back(joint, grad):
    count, rows, _ = joint.shape
    return pl.pallas_call(
        enc_attend_back_kernel,
        grid=(count,),
        in_specs=[
            pl.BlockSpec((1, rows, 3 * D), lambda i: (i, 0, 0)),
            pl.BlockSpec((1, rows, D), lambda i: (i, 0, 0)),
        ],
        out_specs=pl.BlockSpec((1, rows, 3 * D), lambda i: (i, 0, 0)),
        out_shape=jax.ShapeDtypeStruct((count, rows, 3 * D), BF16),
        cost_estimate=estimate(10 * count * rows * rows * D * 4, count * rows * D * 14, count * rows * rows * HEADS),
        name="enc_attend_back",
    )(joint, grad)


def causal_mask(rows, length):
    row = lax.broadcasted_iota(jnp.int32, (rows, rows), 0)
    column = lax.broadcasted_iota(jnp.int32, (rows, rows), 1)
    return (column <= row) & (column < length)


def norm_tile(values, gain):
    centred = values - jnp.mean(values, axis=-1, keepdims=True)
    inverse = lax.rsqrt(jnp.mean(centred * centred, axis=-1, keepdims=True) + 1e-05)
    plain = centred * inverse
    return (plain * gain).astype(BF16), plain, inverse


def norm_back_tile(grad, normed, inverse, gain):
    scaled = grad * gain
    inner = jnp.mean(scaled * normed, axis=-1, keepdims=True)
    return inverse * (scaled - jnp.mean(scaled, axis=-1, keepdims=True) - normed * inner)


class Loads:
    def __init__(self, sems, *pairs):
        self.copies = [pltpu.make_async_copy(src, dst, sems.at[k]) for k, (src, dst) in enumerate(pairs)]
        for copy in self.copies:
            copy.start()

    def wait(self, k):
        self.copies[k].wait()


def live_rows(rows, length):
    row = lax.broadcasted_iota(jnp.int32, (rows, 1), 0)
    return (row // CH * CH < length).astype(F32)


def decoder_kernel(nseq, length_ref, order_ref, tokens, gain_a, gain_b, gain_c, *refs):
    received, selfjoint, selfmerge, crossquery, memorymap, crossmerge, feedup, feeddown = refs[:8]
    outs, place_of = refs[8:25], refs[25]
    (
        output, normed_a, plain_a, inverse_a, joint, mixed, normed_b, plain_b, inverse_b, asked, chosen, memory, crossed, normed_c,
        plain_c, inverse_c, hidden_slope,
    ) = kept = refs[26:43]
    joint_w, merge_w, query_w, map_w, cross_w, up_w, down_w, sems, gather_sems, store_sems = refs[43:]
    rows = tokens.shape[0]
    count = order_ref.shape[1]
    flat = chosen.shape[0]
    places = flat // count
    cap = count // nseq
    length = length_ref[0]
    me = lax.axis_index("seq")
    stores = []

    def store(*done):
        for k, (src, dst) in enumerate(zip(kept, outs)):
            if any(src is ref for ref in done):
                stores.append(pltpu.make_async_copy(src, dst, store_sems.at[k]))
                stores[-1].start()

    gathers = []
    for k in range(count):
        slot = order_ref[0, k]
        source = ((slot // cap) ^ me) * cap + slot % cap
        place_of[source] = k
        gathers.append(
            pltpu.make_async_copy(
                received.at[pl.ds(pl.multiple_of(source * places, places), places)],
                chosen.at[pl.ds(k * places, places)],
                gather_sems.at[k],
            )
        )
    loads = Loads(
        sems,
        (selfjoint, joint_w),
        (selfmerge, merge_w),
        (crossquery, query_w),
        (memorymap, map_w),
        (crossmerge, cross_w),
        (feedup, up_w),
        (feeddown, down_w),
    )
    for copy in gathers:
        copy.start()

    def keep_inverse(ref, inverse):
        ref[...] = jnp.broadcast_to(inverse, ref.shape)

    sequence = tokens[...].astype(F32)
    normed, plain, inverse = norm_tile(sequence, gain_a[...])
    normed_a[...] = normed
    plain_a[...] = plain.astype(BF16)
    keep_inverse(inverse_a, inverse)
    store(normed_a, plain_a, inverse_a)
    loads.wait(0)
    for third in range(3):
        lanes = slice(third * D, (third + 1) * D)
        joint[:, lanes] = dot_nn(normed_a[...], joint_w[:, lanes]).astype(BF16)
    store(joint)
    allowed = causal_mask(rows, length)
    for group in range(0, PAIRS, 3):
        chosen_pairs = range(group, group + 3)
        items = [tuple(joint[:, col(p, third)] for third in range(3)) for p in chosen_pairs]
        for p, block in zip(chosen_pairs, pairs_forward(items, allowed)):
            mixed[:, col(p)] = block
    loads.wait(1)
    after_self = sequence + dot_nn(mixed[...], merge_w[...])
    normed, plain, inverse = norm_tile(after_self, gain_b[...])
    normed_b[...] = normed
    plain_b[...] = plain.astype(BF16)
    keep_inverse(inverse_b, inverse)
    store(mixed, normed_b, plain_b, inverse_b)
    loads.wait(2)
    asked[...] = dot_nn(normed_b[...], query_w[...]).astype(BF16)
    store(asked)

    for copy in gathers:
        copy.wait()
    store(chosen)
    loads.wait(3)

    def project(block, carry):
        window = pl.ds(pl.multiple_of(block * rows, rows), rows)
        for half in range(2):
            lanes = slice(half * D, (half + 1) * D)
            memory[window, lanes] = dot_nn(chosen[window], map_w[:, lanes]).astype(BF16)
        return carry

    lax.fori_loop(0, flat // rows, project, 0)
    store(memory)

    def cross_forward(span, carry):
        window = pl.ds(pl.multiple_of(span * CH, CH), CH)
        around = pl.ds(pl.multiple_of(span * 2 * places, places), 2 * places)
        items = [(asked[window, col(p)], memory[around, col(p, 0)], memory[around, col(p, 1)]) for p in range(PAIRS)]
        for p, block in enumerate(pairs_forward(items)):
            crossed[window, col(p)] = block
        return carry

    lax.fori_loop(0, rows // CH, cross_forward, 0)
    loads.wait(4)
    after_cross = after_self + dot_nn(crossed[...], cross_w[...]) * live_rows(rows, length)
    normed, plain, inverse = norm_tile(after_cross, gain_c[...])
    normed_c[...] = normed
    plain_c[...] = plain.astype(BF16)
    keep_inverse(inverse_c, inverse)
    store(crossed, normed_c, plain_c, inverse_c)
    loads.wait(5)
    loads.wait(6)
    total = after_cross
    for f in range(hidden_slope.shape[2] // D):
        lanes = slice(f * D, (f + 1) * D)
        bent, tilt = curve(dot_nn(normed_c[...], up_w[:, lanes]))
        hidden_slope[0, :, lanes] = bent
        hidden_slope[1, :, lanes] = tilt
        total = total + dot_nn(bent, down_w[lanes])
    output[...] = total.astype(BF16)
    store(output, hidden_slope)
    for copy in stores:
        copy.wait()


def decoder(tokens, lengths, order, received, gains, weights, nseq):
    rows = tokens.shape[0]
    flat = received.shape[0]
    count = order.shape[1]
    inside = pl.BlockSpec(memory_space=pltpu.VMEM)
    scalar = pl.BlockSpec(memory_space=pltpu.SMEM)
    anywhere = pl.BlockSpec(memory_space=pl.ANY)
    narrow = jax.ShapeDtypeStruct((rows, D), BF16)
    inverse = jax.ShapeDtypeStruct((rows, LANES), F32)
    outs = [
        narrow, narrow, narrow, inverse, jax.ShapeDtypeStruct((rows, 3 * D), BF16), narrow, narrow, narrow, inverse, narrow,
        jax.ShapeDtypeStruct((flat, D), BF16), jax.ShapeDtypeStruct((flat, 2 * D), BF16), narrow, narrow, narrow, inverse,
        jax.ShapeDtypeStruct((2, rows, weights[5].shape[1]), BF16),
    ]
    return pl.pallas_call(
        partial(decoder_kernel, nseq),
        in_specs=[scalar] * 2 + [inside] * 4 + [anywhere] * 8,
        out_specs=[pl.BlockSpec(memory_space=pltpu.HBM)] * len(outs) + [scalar],
        out_shape=outs + [jax.ShapeDtypeStruct((count,), jnp.int32)],
        scratch_shapes=[pltpu.VMEM(out.shape, out.dtype) for out in outs]
        + [pltpu.VMEM(weight.shape, BF16) for weight in weights]
        + [
            pltpu.SemaphoreType.DMA((7,)),
            pltpu.SemaphoreType.DMA((count,)),
            pltpu.SemaphoreType.DMA((len(outs),)),
        ],
        compiler_params=pltpu.CompilerParams(vmem_limit_bytes=60 * 2**20),
        cost_estimate=estimate(10e9, 40e6),
        name="decoder",
    )(lengths, order, tokens, *gains, received, *weights)


def self_back_kernel(length_ref, *refs):
    asked_grad, cross_total, plain_b, inverse_b, gain_b, joint, plain_a, inverse_a, gain_a = refs[:9]
    crossquery, selfmerge, selfjoint = refs[9:12]
    self_in, joint_grad, input_grad = refs[12:15]
    query_w, merge_w, joint_w, mixed_grad, sems = refs[15:]
    rows = joint.shape[0]
    loads = Loads(sems, (crossquery, query_w), (selfmerge, merge_w), (selfjoint, joint_w))
    loads.wait(0)
    total = cross_total[...] + norm_back_tile(
        dot_nt(asked_grad[...], query_w[...]), plain_b[...].astype(F32), inverse_b[:, :1], gain_b[...]
    )
    self_in[...] = total.astype(BF16)
    loads.wait(1)
    mixed_grad[...] = dot_nt(self_in[...], merge_w[...]).astype(BF16)
    allowed = causal_mask(rows, length_ref[0])
    for group in range(0, PAIRS, 3):
        chosen = range(group, group + 3)
        items = [tuple(joint[:, col(p, third)] for third in range(3)) + (mixed_grad[:, col(p)],) for p in chosen]
        for p, grads in zip(chosen, pairs_backward(items, allowed)):
            for third in range(3):
                joint_grad[:, col(p, third)] = grads[third]
    loads.wait(2)
    back = dot_nt(joint_grad[...], joint_w[...])
    input_grad[...] = total + norm_back_tile(back, plain_a[...].astype(F32), inverse_a[:, :1], gain_a[...])


def self_back(lengths, asked_grad, cross_total, plain_b, inverse_b, gain_b, joint, plain_a, inverse_a, gain_a, weights):
    rows = joint.shape[0]
    inside = pl.BlockSpec(memory_space=pltpu.VMEM)
    return pl.pallas_call(
        self_back_kernel,
        in_specs=[pl.BlockSpec(memory_space=pltpu.SMEM)] + [inside] * 9 + [pl.BlockSpec(memory_space=pl.ANY)] * 3,
        out_specs=[inside] * 3,
        out_shape=[
            jax.ShapeDtypeStruct((rows, D), BF16),
            jax.ShapeDtypeStruct((rows, 3 * D), BF16),
            jax.ShapeDtypeStruct((rows, D), F32),
        ],
        scratch_shapes=[pltpu.VMEM(weight.shape, BF16) for weight in weights]
        + [pltpu.VMEM((rows, D), BF16), pltpu.SemaphoreType.DMA((3,))],
        compiler_params=pltpu.CompilerParams(vmem_limit_bytes=40 * 2**20),
        cost_estimate=estimate(8e9, 15e6),
        name="self_back",
    )(lengths, asked_grad, cross_total, plain_b, inverse_b, gain_b, joint, plain_a, inverse_a, gain_a, *weights)


def swap(value, axis, size, mask):
    return lax.ppermute(value, axis, [(i, i ^ mask) for i in range(size)])


def bit_of(axis, mask):
    return (lax.axis_index(axis) // mask) % 2


def pick(value, dim, index):
    return lax.dynamic_index_in_dim(value, index, dim, keepdims=False)


def halve(value, dim, axis, size, mask):
    bit = bit_of(axis, mask)
    arrived = swap(pick(value, dim, 1 - bit), axis, size, mask)
    return (pick(value, dim, bit).astype(F32) + arrived.astype(F32)).astype(BF16)


def join(value, dim, axis, size, mask):
    arrived = swap(value, axis, size, mask)
    bit = bit_of(axis, mask)
    return jnp.where(
        bit == 0, jnp.concatenate([value, arrived], axis=dim), jnp.concatenate([arrived, value], axis=dim)
    )


def masks(size):
    found, mask = [], 1
    while mask < size:
        found.append(mask)
        mask *= 2
    return found


def reduce_group(totals, sizes, rows_first):
    nseq, nnbr = sizes
    core = bit_of("seq", 1)
    parts = []
    for whole in totals:
        height, width = whole.shape
        parts.append(halve(whole.reshape(height, 2, width // 2), 1, "seq", nseq, 1))
    widths = [part.shape[1] for part in parts]
    total = parts[0] if len(parts) == 1 else jnp.concatenate(parts, axis=1)
    bits = masks(nnbr)
    rows = total.shape[0] // nnbr
    total = total.reshape((2,) * len(bits) + (rows, total.shape[1]))
    seq_bits = masks(nseq)[1:]

    def over_seq(total):
        for mask in seq_bits:
            shape = total.shape
            total = total.reshape(shape[:-2] + (2, shape[-2] // 2, shape[-1]))
            total = halve(total, total.ndim - 3, "seq", nseq, mask)
        return total

    def over_nbr(total):
        left = list(reversed(bits))
        for mask in bits:
            total = halve(total, left.index(mask), "nbr", nnbr, mask)
            left.remove(mask)
        return total

    if rows_first:
        total = over_nbr(over_seq(total))
        for mask in reversed(seq_bits):
            total = join(total, 0, "seq", nseq, mask)
    else:
        total = over_nbr(total)
        for mask in seq_bits:
            total = (total.astype(F32) + swap(total, "seq", nseq, mask).astype(F32)).astype(BF16)
    other = swap(total, "seq", nseq, 1)
    results, start = [], 0
    for width in widths:
        mine, theirs = total[:, start : start + width], other[:, start : start + width]
        results.append(
            jnp.where(
                core == 0, jnp.concatenate([mine, theirs], axis=1), jnp.concatenate([theirs, mine], axis=1)
            ).astype(F32)
        )
        start += width
    return results


def flip(index, mask):
    for bit in masks(mask + 1):
        if mask & bit:
            index = index + bit * (1 - 2 * ((lax.axis_index("seq") // bit) % 2))
    return index


def encoder_kernel(nseq, count, *refs):
    neighbours, gain_a, gain_b, gain_c, coderjoint, codermerge, coderup, coderdown = refs[:8]
    outs, received = refs[8:18], refs[18]
    entering, joint_w, merge_w, up_w, down_w = refs[19:24]
    kept, normed_c = refs[24:34], refs[34]
    load_sem, weight_sem, store_sem, send_sem, recv_sem = refs[35:]
    normed, joint, mixed, plain_b, inverse_b, normed_b, slope, hidden, plain_c, inverse_c = kept
    flat = entering.shape[0]
    rows, places = flat // nseq, flat // count
    s, n = lax.axis_index("seq"), lax.axis_index("nbr")

    barrier = pltpu.get_barrier_semaphore()
    for m in range(1, nseq):
        pl.semaphore_signal(barrier, inc=1, device_id=(flip(s, m), n), device_id_type=MESH)
    order = list(reversed(range(nseq)))
    loads = {}
    for m in order:
        source = pl.ds(pl.multiple_of(flip(s, m) * rows, rows), rows)
        loads[m] = pltpu.make_async_copy(neighbours.at[source], entering.at[pl.ds(m * rows, rows)], load_sem.at[m])
        loads[m].start()
    weights = Loads(weight_sem, (coderjoint, joint_w), (codermerge, merge_w), (coderup, up_w), (coderdown, down_w))
    pl.semaphore_wait(barrier, nseq - 1)

    stores, sends = [], []
    for turn, m in enumerate(order):
        window = pl.ds(m * rows, rows)
        loads[m].wait()
        embedded = entering[window].astype(F32)
        normed[window] = norm_tile(embedded, gain_a[...])[0]
        if turn == 0:
            weights.wait(0)
        for third in range(3):
            lanes = slice(third * D, (third + 1) * D)
            joint[window, lanes] = dot_nn(normed[window], joint_w[:, lanes]).astype(BF16)

        def attend(k, carry, m=m):
            inside = pl.ds(pl.multiple_of(m * rows + k * places, places), places)
            items = [tuple(joint[inside, col(p, third)] for third in range(3)) for p in range(PAIRS)]
            for p, block in enumerate(pairs_forward(items)):
                mixed[inside, col(p)] = block
            return carry

        lax.fori_loop(0, rows // places, attend, 0)
        if turn == 0:
            weights.wait(1)
        middle = embedded + dot_nn(mixed[window], merge_w[...])
        rounded, plain, inverse = norm_tile(middle, gain_b[...])
        normed_b[window] = rounded
        plain_b[window] = plain.astype(BF16)
        inverse_b[window] = jnp.broadcast_to(inverse, (rows, LANES))
        if turn == 0:
            weights.wait(2)
            weights.wait(3)
        total = middle
        for f in range(hidden.shape[1] // D):
            lanes = slice(f * D, (f + 1) * D)
            bent, tilt = curve(dot_nn(rounded, up_w[:, lanes]))
            hidden[window, lanes] = bent
            slope[window, lanes] = tilt
            total = total + dot_nn(bent, down_w[lanes])
        rounded, plain, inverse = norm_tile(total, gain_c[...])
        normed_c[window] = rounded
        plain_c[window] = plain.astype(BF16)
        inverse_c[window] = jnp.broadcast_to(inverse, (rows, LANES))
        if m == 0:
            stores.append(pltpu.make_async_copy(normed_c.at[window], received.at[window], store_sem.at[len(outs), m]))
            stores[-1].start()
        else:
            copy = pltpu.make_async_remote_copy(
                src_ref=normed_c.at[window],
                dst_ref=received.at[window],
                send_sem=send_sem.at[m],
                recv_sem=recv_sem.at[m],
                device_id=(flip(s, m), n),
                device_id_type=MESH,
            )
            copy.start()
            sends.append(copy)
        for k, (src, dst) in enumerate(zip(kept, outs)):
            stores.append(pltpu.make_async_copy(src.at[window], dst.at[window], store_sem.at[k, m]))
            stores[-1].start()
    for copy in stores + sends:
        copy.wait()


def encoder(neighbours, gains, weights, nseq):
    count, places, _ = neighbours.shape
    flat = count * places
    hidden = weights[2].shape[1]
    widths = (D, 3 * D, D, D, LANES, D, hidden, hidden, D, LANES)
    kinds = (BF16, BF16, BF16, BF16, F32, BF16, BF16, BF16, BF16, F32)
    anywhere = pl.BlockSpec(memory_space=pl.ANY)
    inside = pl.BlockSpec(memory_space=pltpu.VMEM)
    return pl.pallas_call(
        partial(encoder_kernel, nseq, count),
        in_specs=[anywhere] + [inside] * 3 + [anywhere] * 4,
        out_specs=[anywhere] * 11,
        out_shape=[jax.ShapeDtypeStruct((flat, w), k) for w, k in zip(widths, kinds)]
        + [jax.ShapeDtypeStruct((flat, D), BF16)],
        scratch_shapes=[pltpu.VMEM((flat, D), BF16)]
        + [pltpu.VMEM(weight.shape, BF16) for weight in weights]
        + [pltpu.VMEM((flat, w), k) for w, k in zip(widths, kinds)]
        + [
            pltpu.VMEM((flat, D), BF16),
            pltpu.SemaphoreType.DMA((nseq,)),
            pltpu.SemaphoreType.DMA((4,)),
            pltpu.SemaphoreType.DMA((11, nseq)),
            pltpu.SemaphoreType.DMA((nseq,)),
            pltpu.SemaphoreType.DMA((nseq,)),
        ],
        compiler_params=pltpu.CompilerParams(collective_id=1, has_side_effects=True, vmem_limit_bytes=60 * 2**20),
        cost_estimate=estimate(18e9, 50e6),
        name="encoder",
    )(neighbours.reshape(flat, D), *gains, *weights)


HALF = D // 2


MATRICES = 11
DOWN = (0, 7)
UNITS = (
    ((0, 0), (0, 1)),
    ((0, 2), (0, 3)),
    ((1, 0), (1, 1)),
    ((1, 2), (1, 3)),
    ((2, 0), (3, 0)),
    ((4, 0), (4, 1)),
    ((5, 0), (6, 0)),
    ((6, 1), (6, 2)),
    ((7, 0), (7, 1)),
    ((7, 2), (7, 3)),
    ((8, 0), (8, 1)),
    ((8, 2), (8, 3)),
    ((9, 0), (10, 0)),
    ((10, 1), (10, 2)),
)
CARRIED = {
    0: (("feed",),),
    1: (("spans", 0, 2),),
    2: (("spans", 2, 4), ("back",)),
    3: (("self",),),
    4: (("enter",), ("rows", 0)),
    5: (("rows", 1),),
    6: (("rows", 2),),
    7: (("rows", 3),),
    8: (("heads", 0, (0, 1)),),
    9: (("heads", 1, (0, 1)),),
    10: (("heads", 2, (0, 1)),),
    11: (("heads", 3, (0, 1)),),
}
TILE = 256
BACK_IN = (
    "length", "place_of", "feed_gain", "cross_gain", "self_gain", "gain_c", "gain_b",
    "out_grad", "dec_plain_a", "dec_inverse_a", "dec_plain_b", "dec_inverse_b", "dec_plain_c", "dec_inverse_c", "hidden_slope",
    "dec_joint", "asked", "memory",
    "plain_c", "inverse_c", "slope", "plain_b", "inverse_b", "joint",
    "feeddown", "feedup", "crossmerge", "memorymap", "crossquery", "selfmerge", "selfjoint", "coderdown", "coderup", "codermerge",
)


def backward_kernel(blocks, *refs):
    refs = list(refs)

    def take(number):
        taken = refs[:number]
        del refs[:number]
        return taken

    given_refs = dict(zip(BACK_IN, take(len(BACK_IN))))
    values = take(MATRICES)
    outs = take(MATRICES)
    (input_grad,) = take(1)
    (
        stage, first, own, mid, low_a, end_a, tail_a, low_b, end_b, tail_b, low_d, end_d, tail_d, tail_x, result,
        down_w, wide, merge_w, rising_grad, down_in, merge_in, joint_grad,
        y_in, plain_in, inverse_in, slope_in, plain_in_b, inverse_in_b, upper,
        feed_a, some_a, some_b, grad_in, self_in, dec_joint_grad,
        send_sem, recv_sem, local_sem,
    ) = refs
    rows = D // 8
    part = rows // 2
    flat = blocks * TILE
    places = TILE // 2
    s, n = lax.axis_index("seq"), lax.axis_index("nbr")
    c, x = s % 2, s // 2
    y, z1, z2 = n % 2, (n // 2) % 2, n // 4
    at_core, at_x = (s + 1 - 2 * c, n), (s + 2 - 4 * x, n)
    at_y, at_z1, at_z2 = (s, n + 1 - 2 * y), (s, n + 2 - 4 * z1), (s, n + 4 - 8 * z2)
    at_seq = (None, at_core, at_x, (3 - s, n))
    mine = pl.ds(pl.multiple_of(c * HALF, 128), HALF)
    other = pl.ds(pl.multiple_of((1 - c) * HALF, 128), HALF)
    kept = pl.ds(pl.multiple_of(x * part, 16), part)
    given = pl.ds(pl.multiple_of((1 - x) * part, 16), part)

    barrier = pltpu.get_barrier_semaphore()
    for partner in at_seq[1:] + (at_y, at_z1, at_z2):
        pl.semaphore_signal(barrier, inc=1, device_id=partner, device_id_type=MESH)

    pending = {}
    counts = {"local": 0, "remote": 0}

    def remote(key, src, dst, partner):
        index = counts["remote"]
        counts["remote"] += 1
        copy = pltpu.make_async_remote_copy(
            src_ref=src,
            dst_ref=dst,
            send_sem=send_sem.at[index],
            recv_sem=recv_sem.at[index],
            device_id=partner,
            device_id_type=MESH,
        )
        copy.start()
        pending[key] = copy

    def local(key, src, dst):
        copy = pltpu.make_async_copy(src, dst, local_sem.at[counts["local"]])
        counts["local"] += 1
        copy.start()
        pending.setdefault(key, []).append(copy)

    def load(key, name, dst):
        local(key, given_refs[name], dst)

    def arrived(key):
        for copy in pending.pop(key, []):
            copy.wait()

    def tile(block, number=1):
        return pl.ds(block * TILE, number * TILE)


    def fetch(u):
        if u == 0:
            local(("unit", 0), given_refs["hidden_slope"].at[0], feed_a)
        elif u == 2:
            local(("unit", u), values[1], some_a.at[tile(0)])
        elif u in (4, 6):
            for k in range(2):
                local(("unit", u), values[u - 2 + k if u == 4 else u - 1 + k], some_a.at[tile(k)])
        elif u == 5:
            local(("unit", u), values[4], some_a)
        elif u == 8:
            local(("unit", 8), values[7], wide)
            for k in range(3):
                local(("unit", 10), values[8 + k], down_w.at[pl.ds(k * flat, flat)])

    def operands(u, k):
        left = pl.ds(k * D, D)
        if u in (2, 3):
            return some_a.at[tile(0)], rising_grad.at[tile(u - 2), pl.ds((2 + k) * D, D)]
        if u == 4:
            return some_a.at[tile(k)], some_a.at[tile(2 + k)]
        if u == 5:
            return some_a, some_b.at[:, left]
        if u == 6:
            return some_a.at[tile(k)], self_in if k == 0 else dec_joint_grad.at[:, pl.ds(0, D)]
        if u == 7:
            return some_a.at[tile(1)], dec_joint_grad.at[:, pl.ds((1 + k) * D, D)]
        if u in (10, 11):
            return down_w.at[pl.ds(0, flat)], rising_grad.at[:, pl.ds(((u - 10) * 2 + k) * D, D)]
        if u == 12:
            return down_w.at[pl.ds((1 + k) * flat, flat)], merge_in if k == 0 else joint_grad.at[:, pl.ds(0, D)]
        return down_w.at[pl.ds(2 * flat, flat)], joint_grad.at[:, pl.ds((1 + k) * D, D)]

    def product(u):
        if UNITS[u][0][0] in DOWN:
            left, right = (feed_a, grad_in) if u < 2 else (wide, down_in)
            begin = (u % 2) * 2 * rows

            def one(shard, carry):
                columns = left[:, pl.ds(pl.multiple_of(shard * 4 * rows, 128), 4 * rows)]
                block = dot_tn(columns[:, begin : begin + 2 * rows], right[...]).astype(BF16)
                stage[0, shard] = block[:rows]
                stage[1, shard] = block[rows:]
                return carry

            lax.fori_loop(0, 8, one, 0)
            return
        for k in range(2):
            left, right = operands(u, k)
            stage[k] = dot_tn(left[...], right[...]).astype(BF16).reshape(8, rows, D)


    def slot(u):
        return u % 5, u % 4

    def straight(u):
        return u % 4 != 2

    def wide_slot(u):
        return (u // 4 * 3 + (0, 1, None, 2)[u % 4]) % 4

    def stage0(u):
        arrived(("unit", u))
        product(u)
        remote(("core", u), stage.at[:, :, :, other], first.at[u % 2], at_core)

    def stage1(u):
        five, four = slot(u)
        pending.pop(("core", u)).wait()

        def one(k, carry):
            k, a, b, d = k // 8, (k // 4) % 2, (k // 2) % 2, k % 2
            shard = 4 * a + 2 * b + d
            own[five, k, a, b, d] = stage[k, shard, :, mine] + first[u % 2, k, shard]
            return carry

        lax.fori_loop(0, 16, one, 0)
        if straight(u):
            remote(("a", u), own.at[five, 0, :, :, :, given], mid.at[wide_slot(u)], at_x)
            remote(("b", u), own.at[five, 1, :, :, 1 - y], low_b.at[four], at_y)
        else:
            remote(("a", u), own.at[five, 0, :, :, 1 - y], low_b.at[four], at_y)
            remote(("b", u), own.at[five, 1, :, 1 - z1], low_d, at_z1)

    def stage2(u):
        five, four = slot(u)
        pending.pop(("a", u)).wait()
        pending.pop(("b", u)).wait()
        for a in range(2):
            for b in range(2):
                if straight(u):
                    for d in range(2):
                        own[five, 0, a, b, d, kept] = own[five, 0, a, b, d, kept] + mid[wide_slot(u), a, b, d]
                    own[five, 1, a, b, y] = own[five, 1, a, b, y] + low_b[four, a, b]
                else:
                    own[five, 0, a, b, y] = own[five, 0, a, b, y] + low_b[four, a, b]
                    own[five, 1, a, z1, b] = own[five, 1, a, z1, b] + low_d[a, b]
        if straight(u):
            remote(("a", u), own.at[five, 0, :, :, 1 - y, kept], low_a.at[four], at_y)
        else:
            remote(("a", u), own.at[five, 0, :, :, y, given], low_a.at[four], at_x)
        if straight(u):
            remote(("b", u), own.at[five, 1, :, 1 - z1, y], end_b.at[four], at_z1)
        else:
            remote(("b", u), own.at[five, 1, 1 - z2, z1], end_d, at_z2)

    def stage3(u):
        five, four = slot(u)
        pending.pop(("a", u)).wait()
        pending.pop(("b", u)).wait()
        for a in range(2):
            for b in range(2):
                own[five, 0, a, b, y, kept] = own[five, 0, a, b, y, kept] + low_a[four, a, b]
            if straight(u):
                own[five, 1, a, z1, y] = own[five, 1, a, z1, y] + end_b[four, a]
            else:
                own[five, 1, z2, z1, a] = own[five, 1, z2, z1, a] + end_d[a]
        remote(("a", u), own.at[five, 0, :, 1 - z1, y, kept], end_a.at[four], at_z1)
        if straight(u):
            remote(("b", u), own.at[five, 1, 1 - z2, z1, y], tail_b.at[four], at_z2)
        else:
            remote(("b", u), own.at[five, 1, z2, z1, 1 - y], tail_d, at_y)

    def stage4(u):
        five, four = slot(u)
        pending.pop(("a", u)).wait()
        pending.pop(("b", u)).wait()
        for a in range(2):
            own[five, 0, a, z1, y, kept] = own[five, 0, a, z1, y, kept] + end_a[four, a]
        own[five, 1, z2, z1, y] = own[five, 1, z2, z1, y] + (tail_b[four] if straight(u) else tail_d[...])
        remote(("a", u), own.at[five, 0, 1 - z2, z1, y, kept], tail_a.at[four], at_z2)
        remote(("b", u), own.at[five, 1, z2, z1, y], tail_x.at[four], at_x)

    def stage5(u):
        five, four = slot(u)
        pending.pop(("a", u)).wait()
        pending.pop(("b", u)).wait()
        result[u % 6, 0, kept, mine] = own[five, 0, z2, z1, y, kept] + tail_a[four]
        result[u % 6, 1, :, mine] = own[five, 1, z2, z1, y] + tail_x[four]
        piece = result.at[u % 6, 0, kept, mine]
        remote(("a", u), piece, piece, at_x)

    def stage6(u):
        pending.pop(("a", u)).wait()
        piece = result.at[u % 6, :, :, mine]
        remote(("a", u), piece, piece, at_core)

    def stage7(u):
        pending.pop(("a", u)).wait()
        for k, (matrix, block) in enumerate(UNITS[u]):
            if matrix in DOWN:
                target = outs[matrix].at[pl.ds(block * rows, rows)]
            else:
                target = outs[matrix].at[:, pl.ds(block * D, D)]
            local(("out", u), result.at[u % 6, k], target)

    def stage8(u):
        arrived(("out", u))

    stages = (stage0, stage1, stage2, stage3, stage4, stage5, stage6, stage7, stage8)


    def carry_feed():
        arrived("feed")
        total = None
        for f in range(4):
            lanes = pl.ds(f * D, D)
            rounded = (dot_nt(grad_in[...], down_w[lanes]) * slope_in[:, lanes].astype(F32)).astype(BF16)
            rising_grad[tile(f // 2), pl.ds((2 + f % 2) * D, D)] = rounded
            back = dot_nt(rounded, wide[pl.ds(0, D), lanes])
            total = back if total is None else total + back
        total = grad_in[...].astype(F32) + norm_back_tile(
            total, plain_in[...].astype(F32), inverse_in[:, :1], given_refs["feed_gain"][...]
        )
        upper[...] = total
        cross_in = (total * live_rows(TILE, given_refs["length"][0])).astype(BF16)
        some_a[tile(2)] = cross_in
        arrived("cross")
        down_in[tile(1)] = dot_nt(cross_in, merge_w[0]).astype(BF16)
        load("weights", "coderdown", down_w)
        load("weights", "coderup", wide.at[pl.ds(0, D)])
        load("self", "selfmerge", merge_w.at[0])
        load("enter", "dec_plain_a", plain_in)
        load("enter", "dec_inverse_a", inverse_in)

    def carry_spans(begin, end):
        def one(span, carry):
            window = pl.ds(pl.multiple_of(span * CH, CH), CH)
            shifted = pl.ds(pl.multiple_of(TILE + span * CH, CH), CH)
            around = pl.ds(pl.multiple_of(span * TILE, TILE), TILE)
            items = [
                (down_in[window, col(p)], rising_grad[around, col(p, 0)], rising_grad[around, col(p, 1)], down_in[shifted, col(p)])
                for p in range(PAIRS)
            ]
            for p, (dq, dk, dv) in enumerate(pairs_backward(items)):
                some_a[pl.ds(pl.multiple_of(3 * TILE + span * CH, CH), CH), col(p)] = dq
                some_b[around, col(p, 0)] = dk
                some_b[around, col(p, 1)] = dv
            return carry

        lax.fori_loop(begin, end, one, 0)

    def carry_back():
        arrived("map")

        def one(block, carry):
            window = pl.ds(pl.multiple_of(block * TILE, TILE), TILE)
            down_in[window] = dot_nt(some_b[window], joint_grad[pl.ds(0, D), pl.ds(0, 2 * D)]).astype(BF16)
            return carry

        lax.fori_loop(0, blocks, one, 0)
        load("enter", "selfjoint", joint_grad.at[pl.ds(0, D)])
        for k in range(2 * blocks):
            place = given_refs["place_of"][k]
            total = None
            for span in range(2 * blocks):
                weight = (place == span).astype(F32)
                part_of = down_in[pl.ds(span * places, places)].astype(F32) * weight
                total = part_of if total is None else total + part_of
            merge_in[pl.ds(k * places, places)] = total.astype(BF16)
        for m in range(1, blocks):
            remote(("y", m), merge_in.at[tile(m)], y_in.at[m - 1], at_seq[m])

    def carry_self():
        arrived("self")
        total = upper[...] + norm_back_tile(
            dot_nt(some_a[tile(3)], merge_w[1]), plain_in_b[...].astype(F32), inverse_in_b[:, :1], given_refs["cross_gain"][...]
        )
        upper[...] = total
        self_in[...] = total.astype(BF16)
        load("weights", "codermerge", merge_w.at[1])
        feed_a[:, pl.ds(3 * D, D)] = dot_nt(self_in[...], merge_w[0]).astype(BF16)
        allowed = causal_mask(TILE, given_refs["length"][0])
        for group in range(0, PAIRS, 3):
            pairs = range(group, group + 3)
            items = [tuple(joint_grad[tile(3), col(p, third)] for third in range(3)) + (feed_a[:, pl.ds(3 * D + p * LANES, LANES)],) for p in pairs]
            for p, pieces in zip(pairs, pairs_backward(items, allowed)):
                for third in range(3):
                    dec_joint_grad[:, col(p, third)] = pieces[third]

    def carry_enter():
        arrived("enter")
        back = dot_nt(dec_joint_grad[...], joint_grad[pl.ds(0, D)])
        upper[...] = upper[...] + norm_back_tile(
            back, plain_in[...].astype(F32), inverse_in[:, :1], given_refs["self_gain"][...]
        )
        local("input", upper, input_grad)
        fetch_rows(0)


    def fetch_rows(block):
        window = tile(block)
        local("rows", given_refs["plain_c"].at[window], plain_in)
        local("rows", given_refs["inverse_c"].at[window], inverse_in)
        local("rows", given_refs["slope"].at[window], slope_in)
        local("rows", given_refs["plain_b"].at[window], plain_in_b)
        local("rows", given_refs["inverse_b"].at[window], inverse_in_b)

    def fetch_heads(block):
        local("heads", given_refs["joint"].at[tile(block)], dec_joint_grad)

    def carry_rows(block):
        window = tile(block)
        arrived("rows")
        if block == 0:
            arrived("weights")
            arrived("input")
            came = merge_in[window]
        else:
            pending.pop(("y", block)).wait()
            came = y_in[block - 1]
        total = norm_back_tile(
            came.astype(F32), plain_in[...].astype(F32), inverse_in[:, :1], given_refs["gain_c"][...]
        )
        upper[...] = total
        down_in[window] = total.astype(BF16)
        for f in range(4):
            lanes = pl.ds(f * D, D)
            rounded = (dot_nt(down_in[window], down_w[lanes]) * slope_in[:, lanes].astype(F32)).astype(BF16)
            rising_grad[window, lanes] = rounded
            back = dot_nt(rounded, wide[pl.ds(0, D), lanes])
            total = back if f == 0 else total + back
        total = upper[...] + norm_back_tile(
            total, plain_in_b[...].astype(F32), inverse_in_b[:, :1], given_refs["gain_b"][...]
        )
        rounded = total.astype(BF16)
        merge_in[window] = rounded
        feed_a[:, pl.ds(block * D, D)] = dot_nt(rounded, merge_w[1]).astype(BF16)
        if block + 1 < blocks:
            fetch_rows(block + 1)
        else:
            fetch(8)
            fetch_heads(0)

    def carry_heads(block, which):
        if which[0] == 0:
            arrived("heads")

        def one(k, carry):
            inside = pl.ds(pl.multiple_of(k * places, 128), places)
            outside = pl.ds(pl.multiple_of(block * TILE + k * places, 128), places)
            items = [
                tuple(dec_joint_grad[inside, col(p, third)] for third in range(3)) + (feed_a[inside, pl.ds(block * D + p * LANES, LANES)],)
                for p in range(PAIRS)
            ]
            for p, pieces in enumerate(pairs_backward(items)):
                for third in range(3):
                    joint_grad[outside, col(p, third)] = pieces[third]
            return carry

        lax.fori_loop(which[0], which[-1] + 1, one, 0)
        if which[-1] == 1 and block + 1 < blocks:
            fetch_heads(block + 1)

    carried = {
        "feed": carry_feed,
        "spans": carry_spans,
        "back": carry_back,
        "self": carry_self,
        "enter": carry_enter,
        "rows": carry_rows,
        "heads": carry_heads,
    }
    load(("unit", 0), "out_grad", grad_in)
    fetch(0)
    load("feed", "feeddown", down_w)
    local("feed", given_refs["hidden_slope"].at[1], slope_in)
    load("feed", "feedup", wide.at[pl.ds(0, D)])
    load("feed", "dec_plain_c", plain_in)
    load("feed", "dec_inverse_c", inverse_in)
    load("cross", "crossmerge", merge_w.at[0])
    load("cross", "asked", down_in.at[tile(0)])
    load("cross", "memory", rising_grad.at[:, pl.ds(0, 2 * D)])
    load("map", "memorymap", joint_grad.at[pl.ds(0, D), pl.ds(0, 2 * D)])
    load("self", "crossquery", merge_w.at[1])
    load("self", "dec_plain_b", plain_in_b)
    load("self", "dec_inverse_b", inverse_in_b)
    load("self", "dec_joint", joint_grad.at[tile(3)])
    pl.semaphore_wait(barrier, 6)
    for tick in range(len(UNITS) + len(stages) - 1):
        for level in (1, 0) + tuple(range(2, len(stages))):
            if 0 <= tick - level < len(UNITS):
                stages[level](tick - level)
        if 1 <= tick < 7:
            fetch(tick + 1)
        for kind, *details in CARRIED.get(tick, ()):
            carried[kind](*details)


def backward(blocks, given, values, heights):
    rows = D // 8
    part = rows // 2
    flat = blocks * TILE
    anywhere = pl.BlockSpec(memory_space=pl.ANY)
    spaces = [pltpu.SMEM] * 2 + [pltpu.VMEM] * 5 + [pl.ANY] * (len(BACK_IN) - 7 + MATRICES)

    def room(*shape, dtype=BF16):
        return pltpu.VMEM(shape, dtype)

    return pl.pallas_call(
        partial(backward_kernel, blocks),
        in_specs=[pl.BlockSpec(memory_space=space) for space in spaces],
        out_specs=[anywhere] * (MATRICES + 1),
        out_shape=[jax.ShapeDtypeStruct(height, BF16) for height in heights] + [jax.ShapeDtypeStruct((TILE, D), F32)],
        scratch_shapes=[
            room(2, 8, rows, D),
            room(2, 2, 8, rows, HALF),
            room(5, 2, 2, 2, 2, rows, HALF),
            room(4, 2, 2, 2, part, HALF),
            room(4, 2, 2, part, HALF),
            room(4, 2, part, HALF),
            room(4, part, HALF),
            room(4, 2, 2, rows, HALF),
            room(4, 2, rows, HALF),
            room(4, rows, HALF),
            room(2, 2, rows, HALF),
            room(2, rows, HALF),
            room(rows, HALF),
            room(4, rows, HALF),
            room(6, 2, rows, D),
            room(4 * D, D),
            room(flat, 4 * D),
            room(2, D, D),
            room(flat, 4 * D),
            room(flat, D),
            room(flat, D),
            room(flat, 3 * D),
            room(blocks - 1, TILE, D),
            room(TILE, D),
            room(TILE, LANES, dtype=F32),
            room(TILE, 4 * D),
            room(TILE, D),
            room(TILE, LANES, dtype=F32),
            room(TILE, D, dtype=F32),
            room(TILE, 4 * D),
            room(flat, D),
            room(flat, 2 * D),
            room(TILE, D),
            room(TILE, D),
            room(TILE, 3 * D),
            pltpu.SemaphoreType.DMA((len(UNITS) * 12,)),
            pltpu.SemaphoreType.DMA((len(UNITS) * 12,)),
            pltpu.SemaphoreType.DMA((128,)),
        ],
        compiler_params=pltpu.CompilerParams(
            collective_id=0, has_side_effects=True, vmem_limit_bytes=62 * 2**20
        ),
        cost_estimate=estimate(55e9, 120e6),
        name="backward_and_sums",
    )(*[given[name] for name in BACK_IN], *values)


GAINED = (6, 3, 1, 10, 8, 4)


def finish_kernel(nbr_ref, *refs):
    gains, sums, weights, outs, gain_outs = refs[:6], refs[6:17], refs[17:23], refs[23:34], refs[34:]
    for total, out in zip(sums, outs):
        out[...] = total[...].astype(F32)
    rows = gain_outs[0].shape[1]
    row = lax.broadcasted_iota(jnp.int32, (D, rows), 0)
    place = lax.broadcasted_iota(jnp.int32, (D, rows), 1) + nbr_ref[0] * rows
    own = lax.dot_general(
        jnp.concatenate([gain[...][None] for gain in gains], axis=0),
        (row == place).astype(F32),
        (((1,), (0,)), ((), ())),
        precision=lax.Precision.HIGHEST,
        preferred_element_type=F32,
    )
    for k, (matrix, weight, out) in enumerate(zip(GAINED, weights, gain_outs)):
        product = weight[...].astype(F32) * sums[matrix][...].astype(F32)
        summed = lax.dot_general(
            jnp.ones((8, product.shape[1]), F32),
            product,
            (((1,), (1,)), ((), ())),
            precision=lax.Precision.HIGHEST,
            preferred_element_type=F32,
        )
        out[...] = summed[:1] / own[k : k + 1]


def finish(sums, gains, weights, nnbr):
    rows = D // nnbr
    nbr = lax.axis_index("nbr").reshape(1).astype(jnp.int32)

    def whole(array):
        return pl.BlockSpec(array.shape, lambda i, nbr: (0,) * array.ndim)

    results = pl.pallas_call(
        finish_kernel,
        grid_spec=pltpu.PrefetchScalarGridSpec(
            num_scalar_prefetch=1,
            grid=(1,),
            in_specs=[whole(array) for array in gains + list(sums)]
            + [pl.BlockSpec((rows, weight.shape[1]), lambda i, nbr: (nbr[0], 0)) for weight in weights],
            out_specs=[whole(total) for total in sums] + [pl.BlockSpec((1, rows), lambda i, nbr: (0, 0))] * len(weights),
        ),
        out_shape=[jax.ShapeDtypeStruct(total.shape, F32) for total in sums]
        + [jax.ShapeDtypeStruct((1, rows), F32)] * len(weights),
        compiler_params=pltpu.CompilerParams(vmem_limit_bytes=56 * 2**20),
        cost_estimate=estimate(1e7, 20e6),
        name="finish",
    )(nbr, *gains, *sums, *weights)
    return results[: len(sums)], [grad.reshape(rows) for grad in results[len(sums) :]]


def body(
    sizes,
    tokens,
    neighbours,
    out_grad,
    lengths,
    slot_order,
    selfgain,
    selfjoint,
    selfmerge,
    crossgain,
    crossquery,
    crossmerge,
    feedgain,
    feedup,
    feeddown,
    codergain,
    coderjoint,
    codermerge,
    codermid,
    coderup,
    coderdown,
    codertop,
    memorymap,
):
    nseq, nnbr = sizes
    count, places, _ = neighbours.shape
    flat = count * places

    (
        enc_normed, enc_joint, enc_mixed, enc_plain_b, enc_inverse_b, enc_normed_b, enc_slope, enc_hidden, enc_plain_c, enc_inverse_c,
        received,
    ) = encoder(
        neighbours,
        [codergain, codermid, codertop],
        [coderjoint, codermerge, coderup, coderdown],
        nseq,
    )

    (
        output, normed_a, plain_a, inverse_a, joint, mixed, normed_b, plain_b, inverse_b, asked, chosen, memory, crossed, normed_c,
        plain_c, inverse_c, hidden_slope, place_of,
    ) = decoder(
        tokens[0],
        lengths,
        slot_order,
        received,
        [selfgain, crossgain, feedgain],
        [selfjoint, selfmerge, crossquery, memorymap, crossmerge, feedup, feeddown],
        nseq,
    )
    values = [
        hidden_slope[0], normed_c, crossed, normed_b, chosen, mixed, normed_a, enc_hidden, enc_normed_b, enc_mixed, enc_normed,
    ]
    if nseq == 4 and nnbr == 8:
        weights = [
            feeddown, feedup, crossmerge, crossquery, memorymap, selfmerge, selfjoint, coderdown, coderup, codermerge, coderjoint
        ]
        given = dict(
            length=lengths, place_of=place_of, feed_gain=feedgain, cross_gain=crossgain, self_gain=selfgain, gain_c=codertop,
            gain_b=codermid, out_grad=out_grad[0], dec_plain_a=plain_a, dec_inverse_a=inverse_a, dec_plain_b=plain_b,
            dec_inverse_b=inverse_b, dec_plain_c=plain_c, dec_inverse_c=inverse_c, hidden_slope=hidden_slope, dec_joint=joint,
            asked=asked, memory=memory, plain_c=enc_plain_c, inverse_c=enc_inverse_c, slope=enc_slope, plain_b=enc_plain_b,
            inverse_b=enc_inverse_b, joint=enc_joint, feeddown=feeddown, feedup=feedup, crossmerge=crossmerge,
            memorymap=memorymap, crossquery=crossquery, selfmerge=selfmerge, selfjoint=selfjoint, coderdown=coderdown,
            coderup=coderup, codermerge=codermerge,
        )
        *sums, input_grad = backward(nseq, given, [normed_c] + values[1:], [(w.shape[0] // nnbr, w.shape[1]) for w in weights])
    else:
        down_in = out_grad[0]
        rising_grad = (hidden_slope[1].astype(F32) * times_back(down_in, feeddown)).astype(BF16)
        cross_total = down_in.astype(F32) + norm_backward(
            times_back(rising_grad, feedup), plain_c.astype(F32), inverse_c[:, :1], feedgain
        )
        live = (jnp.arange(tokens.shape[1], dtype=jnp.int32) // CH * CH < lengths[0]).astype(F32)[:, None]
        cross_in = (cross_total * live).astype(BF16)
        asked_grad, memory_grad = spans_backward(asked, memory, times_back(cross_in, crossmerge).astype(BF16))
        back = times_back(memory_grad, memorymap).astype(BF16).reshape(count, places, D)[place_of]
        back = back.reshape(nseq, flat // nseq, D)
        returned = [back[m] if m == 0 else swap(back[m], "seq", nseq, m) for m in range(nseq)]
        self_in, joint_grad, input_grad = self_back(
            lengths, asked_grad, cross_total, plain_b, inverse_b, crossgain, joint, plain_a, inverse_a, selfgain,
            [crossquery, selfmerge, selfjoint],
        )
        upper_total = norm_backward(
            jnp.concatenate(returned, axis=0).astype(F32), enc_plain_c.astype(F32), enc_inverse_c[:, :1], codertop
        )
        enc_down_in = upper_total.astype(BF16)
        enc_rising_grad = (enc_slope.astype(F32) * times_back(enc_down_in, coderdown)).astype(BF16)
        middle_total = upper_total + norm_backward(
            times_back(enc_rising_grad, coderup), enc_plain_b.astype(F32), enc_inverse_b[:, :1], codermid
        )
        enc_merge_in = middle_total.astype(BF16)
        enc_mixed_grad = times_back(enc_merge_in, codermerge).astype(BF16).reshape(count, places, D)
        enc_joint_grad = enc_attend_back(enc_joint.reshape(count, places, 3 * D), enc_mixed_grad).reshape(flat, 3 * D)
        grads = [
            down_in, rising_grad, cross_in, asked_grad, memory_grad, self_in, joint_grad, enc_down_in, enc_rising_grad, enc_merge_in,
            enc_joint_grad,
        ]
        sums = [weight_grad(v, g).astype(BF16) for v, g in zip(values, grads)]
        ways = (False, True, False, False, False, False, False, True, False, True, True)
        sums = [reduce_group([total], sizes, way)[0] for total, way in zip(sums, ways)]
    output, input_grad = output[None], input_grad[None]
    sums, gain_grads = finish(
        sums,
        [selfgain, crossgain, feedgain, codergain, codermid, codertop],
        [selfjoint, crossquery, feedup, coderjoint, coderup, memorymap],
        nnbr,
    )
    (
        grad_feeddown,
        grad_feedup,
        grad_crossmerge,
        grad_crossquery,
        grad_memorymap,
        grad_selfmerge,
        grad_selfjoint,
        grad_coderdown,
        grad_coderup,
        grad_codermerge,
        grad_coderjoint,
    ) = sums
    grad_selfgain, grad_crossgain, grad_feedgain, grad_codergain, grad_codermid, grad_codertop = gain_grads
    return (
        output,
        input_grad,
        grad_selfgain,
        grad_selfjoint,
        grad_selfmerge,
        grad_crossgain,
        grad_crossquery,
        grad_crossmerge,
        grad_feedgain,
        grad_feedup,
        grad_feeddown,
        grad_codergain,
        grad_coderjoint,
        grad_codermerge,
        grad_codermid,
        grad_coderup,
        grad_coderdown,
        grad_codertop,
        grad_memorymap,
    )


def solution(mesh):
    spread = ("seq", "nbr")
    sizes = (mesh.shape["seq"], mesh.shape["nbr"])
    placed = (
        P(spread, None, None),
        P(spread, None, None),
        P(spread, None, None),
        P(spread),
        P(spread, None),
    ) + (P(),) * 17
    gain, weight = P("nbr"), P("nbr", None)
    return jax.shard_map(
        partial(body, sizes),
        mesh=mesh,
        in_specs=placed,
        out_specs=(
            P(spread, None, None),
            P(spread, None, None),
            gain,
            weight,
            weight,
            gain,
            weight,
            weight,
            gain,
            weight,
            weight,
            gain,
            weight,
            weight,
            gain,
            weight,
            weight,
            gain,
            weight,
        ),
        check_vma=False,
    )
```

```python
from functools import partial

import jax
import jax.numpy as jnp
from jax import lax
from jax.experimental import pallas as pl
from jax.experimental.pallas import tpu as pltpu
from jax.sharding import PartitionSpec as P

D = 768
HEADS = 12
HD = 64
CH = 64
PAIRS = HEADS // 2
LANES = 2 * HD
SCALE = HD ** (-0.5)
F32 = jnp.float32
BF16 = jnp.bfloat16
MESH = pl.DeviceIdType.MESH


def norm_backward(grad, normed, inverse, gain):
    scaled = grad * gain
    inner = jnp.mean(scaled * normed, axis=-1, keepdims=True)
    return inverse * (scaled - jnp.mean(scaled, axis=-1, keepdims=True) - normed * inner)


def times(values, weight):
    return lax.dot_general(values, weight, (((1,), (0,)), ((), ())), preferred_element_type=F32)


def times_back(grad, weight):
    return lax.dot_general(grad, weight, (((1,), (1,)), ((), ())), preferred_element_type=F32)


def weight_grad(values, grad):
    return lax.dot_general(values, grad, (((0,), (0,)), ((), ())), preferred_element_type=F32)


def curve(rising):
    square = rising * rising
    bend = jnp.tanh(rising * (0.7978845608028654 + 0.035677408136300125 * square))
    half = 0.5 * (1.0 + bend)
    slope = half + 0.5 * rising * (1.0 - bend * bend) * (0.7978845608028654 + 0.10703222440890037 * square)
    return (rising * half).astype(BF16), slope.astype(BF16)


def dot_nt(a, b):
    return lax.dot_general(a, b, (((1,), (1,)), ((), ())), preferred_element_type=F32)


def dot_nn(a, b):
    return lax.dot_general(a, b, (((1,), (0,)), ((), ())), preferred_element_type=F32)


def dot_tn(a, b):
    return lax.dot_general(a, b, (((0,), (0,)), ((), ())), preferred_element_type=F32)


def stack_pair(block):
    lane = lax.broadcasted_iota(jnp.int32, block.shape, 1)
    zero = jnp.zeros_like(block)
    return jnp.concatenate([jnp.where(lane < HD, block, zero), jnp.where(lane >= HD, block, zero)], axis=0)


def unstack_pair(stacked):
    half = stacked.shape[0] // 2
    lane = lax.broadcasted_iota(jnp.int32, (half, LANES), 1)
    return jnp.where(lane < HD, stacked[:half], stacked[half:])


def halves(block):
    width = block.shape[1] // 2
    return block[:, :width], block[:, width:]


def exponents(products, allowed):
    parts = []
    for scores in halves(products):
        if allowed is not None:
            scores = jnp.where(allowed, scores, -1000000000.0)
        parts.append(jnp.exp((scores - jnp.max(scores, axis=-1, keepdims=True)) * SCALE).astype(BF16))
    return jnp.concatenate(parts, axis=1)


def summing(width, lanes):
    row = lax.broadcasted_iota(jnp.int32, (2 * width, lanes), 0)
    lane = lax.broadcasted_iota(jnp.int32, (2 * width, lanes), 1)
    return ((row < width) == (lane < lanes // 2)).astype(BF16)


def pairs_forward(items, allowed=None):
    ones = summing(items[0][1].shape[0], LANES)
    scores = [dot_nt(queries, stack_pair(keys)) for queries, keys, _ in items]
    raised = [exponents(block, allowed) for block in scores]
    mixed = [
        dot_nn(block, jnp.concatenate([stack_pair(values), ones], axis=1)) for block, (_, _, values) in zip(raised, items)
    ]
    return [(block[:, :LANES] / block[:, LANES:]).astype(BF16) for block in mixed]


def pairs_backward(items, allowed=None):
    width = items[0][1].shape[0]
    ones = summing(width, 2 * width)
    stacked = [stack_pair(keys) for _, keys, _, _ in items]
    scores = [dot_nt(item[0], keys) for item, keys in zip(items, stacked)]
    prob_grads = [dot_nt(item[3], stack_pair(item[2])) for item in items]
    raised = [exponents(block, allowed) for block in scores]
    totals = [dot_nn(block, ones) for block in raised]
    probs = [block.astype(F32) * (1.0 / total) for block, total in zip(raised, totals)]
    value_grads = [unstack_pair(dot_tn(block.astype(BF16), item[3])) for block, item in zip(probs, items)]
    score_grads = []
    for block, grad in zip(probs, prob_grads):
        parts = []
        for prob, part in zip(halves(block), halves(block * grad)):
            parts.append(((part - prob * jnp.sum(part, axis=-1, keepdims=True)) * SCALE).astype(BF16))
        score_grads.append(jnp.concatenate(parts, axis=1))
    query_grads = [dot_nn(grad, keys) for grad, keys in zip(score_grads, stacked)]
    key_grads = [unstack_pair(dot_tn(grad, item[0])) for grad, item in zip(score_grads, items)]
    return [tuple(g.astype(BF16) for g in grads) for grads in zip(query_grads, key_grads, value_grads)]


def col(pair, third=0):
    return slice(third * D + pair * LANES, third * D + (pair + 1) * LANES)


def estimate(flops, nbytes, exps=0):
    return pl.CostEstimate(flops=int(flops), bytes_accessed=int(nbytes), transcendentals=int(exps))


def spans_backward(asked, memory, outgoing):
    spans = asked.shape[0] // CH
    queries, grads = (block.reshape(spans, CH, HEADS, HD) for block in (asked, outgoing))
    keys, values = (memory[:, k * D : (k + 1) * D].reshape(spans, -1, HEADS, HD) for k in range(2))

    def product(form, left, right):
        return jnp.einsum(form, left, right, preferred_element_type=F32)

    probs = jax.nn.softmax(product("brhd,bshd->bhrs", queries, keys) * SCALE, axis=-1)
    value_grad = product("bhrs,brhd->bshd", probs.astype(BF16), grads)
    prob_grad = product("brhd,bshd->bhrs", grads, values)
    inner = jnp.sum(probs * prob_grad, axis=-1, keepdims=True)
    score_grad = (probs * (prob_grad - inner) * SCALE).astype(BF16)
    query_grad = product("bhrs,bshd->brhd", score_grad, keys)
    key_grad = product("bhrs,brhd->bshd", score_grad, queries)
    memory_grad = jnp.concatenate([block.reshape(-1, D) for block in (key_grad, value_grad)], axis=1)
    return query_grad.reshape(-1, D).astype(BF16), memory_grad.astype(BF16)


def enc_attend_back_kernel(joint_ref, grad_ref, out_ref):
    items = [
        tuple(joint_ref[0, :, col(p, third)] for third in range(3)) + (grad_ref[0, :, col(p)],) for p in range(PAIRS)
    ]
    for p, grads in enumerate(pairs_backward(items)):
        for third in range(3):
            out_ref[0, :, col(p, third)] = grads[third]


def enc_attend_back(joint, grad):
    count, rows, _ = joint.shape
    return pl.pallas_call(
        enc_attend_back_kernel,
        grid=(count,),
        in_specs=[
            pl.BlockSpec((1, rows, 3 * D), lambda i: (i, 0, 0)),
            pl.BlockSpec((1, rows, D), lambda i: (i, 0, 0)),
        ],
        out_specs=pl.BlockSpec((1, rows, 3 * D), lambda i: (i, 0, 0)),
        out_shape=jax.ShapeDtypeStruct((count, rows, 3 * D), BF16),
        cost_estimate=estimate(10 * count * rows * rows * D * 4, count * rows * D * 14, count * rows * rows * HEADS),
        name="enc_attend_back",
    )(joint, grad)


def causal_mask(rows, length):
    row = lax.broadcasted_iota(jnp.int32, (rows, rows), 0)
    column = lax.broadcasted_iota(jnp.int32, (rows, rows), 1)
    return (column <= row) & (column < length)


def norm_tile(values, gain):
    centred = values - jnp.mean(values, axis=-1, keepdims=True)
    inverse = lax.rsqrt(jnp.mean(centred * centred, axis=-1, keepdims=True) + 1e-05)
    plain = centred * inverse
    return (plain * gain).astype(BF16), plain, inverse


def norm_back_tile(grad, normed, inverse, gain):
    scaled = grad * gain
    inner = jnp.mean(scaled * normed, axis=-1, keepdims=True)
    return inverse * (scaled - jnp.mean(scaled, axis=-1, keepdims=True) - normed * inner)


class Loads:
    def __init__(self, sems, *pairs):
        self.copies = [pltpu.make_async_copy(src, dst, sems.at[k]) for k, (src, dst) in enumerate(pairs)]
        for copy in self.copies:
            copy.start()

    def wait(self, k):
        self.copies[k].wait()


def live_rows(rows, length):
    row = lax.broadcasted_iota(jnp.int32, (rows, 1), 0)
    return (row // CH * CH < length).astype(F32)


def decoder_kernel(nseq, length_ref, order_ref, tokens, gain_a, gain_b, gain_c, *refs):
    received, selfjoint, selfmerge, crossquery, memorymap, crossmerge, feedup, feeddown = refs[:8]
    outs, place_of = refs[8:25], refs[25]
    (
        output, normed_a, plain_a, inverse_a, joint, mixed, normed_b, plain_b, inverse_b, asked, chosen, memory, crossed, normed_c,
        plain_c, inverse_c, hidden_slope,
    ) = kept = refs[26:43]
    joint_w, merge_w, query_w, map_w, cross_w, up_w, down_w, sems, gather_sems, store_sems = refs[43:]
    rows = tokens.shape[0]
    count = order_ref.shape[1]
    flat = chosen.shape[0]
    places = flat // count
    cap = count // nseq
    length = length_ref[0]
    me = lax.axis_index("seq")
    stores = []

    def store(*done):
        for k, (src, dst) in enumerate(zip(kept, outs)):
            if any(src is ref for ref in done):
                stores.append(pltpu.make_async_copy(src, dst, store_sems.at[k]))
                stores[-1].start()

    gathers = []
    for k in range(count):
        slot = order_ref[0, k]
        source = ((slot // cap) ^ me) * cap + slot % cap
        place_of[source] = k
        gathers.append(
            pltpu.make_async_copy(
                received.at[pl.ds(pl.multiple_of(source * places, places), places)],
                chosen.at[pl.ds(k * places, places)],
                gather_sems.at[k],
            )
        )
    loads = Loads(
        sems,
        (selfjoint, joint_w),
        (selfmerge, merge_w),
        (crossquery, query_w),
        (memorymap, map_w),
        (crossmerge, cross_w),
        (feedup, up_w),
        (feeddown, down_w),
    )
    for copy in gathers:
        copy.start()

    def keep_inverse(ref, inverse):
        ref[...] = jnp.broadcast_to(inverse, ref.shape)

    sequence = tokens[...].astype(F32)
    normed, plain, inverse = norm_tile(sequence, gain_a[...])
    normed_a[...] = normed
    plain_a[...] = plain.astype(BF16)
    keep_inverse(inverse_a, inverse)
    store(normed_a, plain_a, inverse_a)
    loads.wait(0)
    for third in range(3):
        lanes = slice(third * D, (third + 1) * D)
        joint[:, lanes] = dot_nn(normed_a[...], joint_w[:, lanes]).astype(BF16)
    store(joint)
    allowed = causal_mask(rows, length)
    for group in range(0, PAIRS, 3):
        chosen_pairs = range(group, group + 3)
        items = [tuple(joint[:, col(p, third)] for third in range(3)) for p in chosen_pairs]
        for p, block in zip(chosen_pairs, pairs_forward(items, allowed)):
            mixed[:, col(p)] = block
    loads.wait(1)
    after_self = sequence + dot_nn(mixed[...], merge_w[...])
    normed, plain, inverse = norm_tile(after_self, gain_b[...])
    normed_b[...] = normed
    plain_b[...] = plain.astype(BF16)
    keep_inverse(inverse_b, inverse)
    store(mixed, normed_b, plain_b, inverse_b)
    loads.wait(2)
    asked[...] = dot_nn(normed_b[...], query_w[...]).astype(BF16)
    store(asked)

    for copy in gathers:
        copy.wait()
    store(chosen)
    loads.wait(3)

    def project(block, carry):
        window = pl.ds(pl.multiple_of(block * rows, rows), rows)
        for half in range(2):
            lanes = slice(half * D, (half + 1) * D)
            memory[window, lanes] = dot_nn(chosen[window], map_w[:, lanes]).astype(BF16)
        return carry

    lax.fori_loop(0, flat // rows, project, 0)
    store(memory)

    def cross_forward(span, carry):
        window = pl.ds(pl.multiple_of(span * CH, CH), CH)
        around = pl.ds(pl.multiple_of(span * 2 * places, places), 2 * places)
        items = [(asked[window, col(p)], memory[around, col(p, 0)], memory[around, col(p, 1)]) for p in range(PAIRS)]
        for p, block in enumerate(pairs_forward(items)):
            crossed[window, col(p)] = block
        return carry

    lax.fori_loop(0, rows // CH, cross_forward, 0)
    loads.wait(4)
    after_cross = after_self + dot_nn(crossed[...], cross_w[...]) * live_rows(rows, length)
    normed, plain, inverse = norm_tile(after_cross, gain_c[...])
    normed_c[...] = normed
    plain_c[...] = plain.astype(BF16)
    keep_inverse(inverse_c, inverse)
    store(crossed, normed_c, plain_c, inverse_c)
    loads.wait(5)
    loads.wait(6)
    total = after_cross
    for f in range(hidden_slope.shape[2] // D):
        lanes = slice(f * D, (f + 1) * D)
        bent, tilt = curve(dot_nn(normed_c[...], up_w[:, lanes]))
        hidden_slope[0, :, lanes] = bent
        hidden_slope[1, :, lanes] = tilt
        total = total + dot_nn(bent, down_w[lanes])
    output[...] = total.astype(BF16)
    store(output, hidden_slope)
    for copy in stores:
        copy.wait()


def decoder(tokens, lengths, order, received, gains, weights, nseq):
    rows = tokens.shape[0]
    flat = received.shape[0]
    count = order.shape[1]
    inside = pl.BlockSpec(memory_space=pltpu.VMEM)
    scalar = pl.BlockSpec(memory_space=pltpu.SMEM)
    anywhere = pl.BlockSpec(memory_space=pl.ANY)
    narrow = jax.ShapeDtypeStruct((rows, D), BF16)
    inverse = jax.ShapeDtypeStruct((rows, LANES), F32)
    outs = [
        narrow, narrow, narrow, inverse, jax.ShapeDtypeStruct((rows, 3 * D), BF16), narrow, narrow, narrow, inverse, narrow,
        jax.ShapeDtypeStruct((flat, D), BF16), jax.ShapeDtypeStruct((flat, 2 * D), BF16), narrow, narrow, narrow, inverse,
        jax.ShapeDtypeStruct((2, rows, weights[5].shape[1]), BF16),
    ]
    return pl.pallas_call(
        partial(decoder_kernel, nseq),
        in_specs=[scalar] * 2 + [inside] * 4 + [anywhere] * 8,
        out_specs=[pl.BlockSpec(memory_space=pltpu.HBM)] * len(outs) + [scalar],
        out_shape=outs + [jax.ShapeDtypeStruct((count,), jnp.int32)],
        scratch_shapes=[pltpu.VMEM(out.shape, out.dtype) for out in outs]
        + [pltpu.VMEM(weight.shape, BF16) for weight in weights]
        + [
            pltpu.SemaphoreType.DMA((7,)),
            pltpu.SemaphoreType.DMA((count,)),
            pltpu.SemaphoreType.DMA((len(outs),)),
        ],
        compiler_params=pltpu.CompilerParams(vmem_limit_bytes=60 * 2**20),
        cost_estimate=estimate(10e9, 40e6),
        name="decoder",
    )(lengths, order, tokens, *gains, received, *weights)


def self_back_kernel(length_ref, *refs):
    asked_grad, cross_total, plain_b, inverse_b, gain_b, joint, plain_a, inverse_a, gain_a = refs[:9]
    crossquery, selfmerge, selfjoint = refs[9:12]
    self_in, joint_grad, input_grad = refs[12:15]
    query_w, merge_w, joint_w, mixed_grad, sems = refs[15:]
    rows = joint.shape[0]
    loads = Loads(sems, (crossquery, query_w), (selfmerge, merge_w), (selfjoint, joint_w))
    loads.wait(0)
    total = cross_total[...] + norm_back_tile(
        dot_nt(asked_grad[...], query_w[...]), plain_b[...].astype(F32), inverse_b[:, :1], gain_b[...]
    )
    self_in[...] = total.astype(BF16)
    loads.wait(1)
    mixed_grad[...] = dot_nt(self_in[...], merge_w[...]).astype(BF16)
    allowed = causal_mask(rows, length_ref[0])
    for group in range(0, PAIRS, 3):
        chosen = range(group, group + 3)
        items = [tuple(joint[:, col(p, third)] for third in range(3)) + (mixed_grad[:, col(p)],) for p in chosen]
        for p, grads in zip(chosen, pairs_backward(items, allowed)):
            for third in range(3):
                joint_grad[:, col(p, third)] = grads[third]
    loads.wait(2)
    back = dot_nt(joint_grad[...], joint_w[...])
    input_grad[...] = total + norm_back_tile(back, plain_a[...].astype(F32), inverse_a[:, :1], gain_a[...])


def self_back(lengths, asked_grad, cross_total, plain_b, inverse_b, gain_b, joint, plain_a, inverse_a, gain_a, weights):
    rows = joint.shape[0]
    inside = pl.BlockSpec(memory_space=pltpu.VMEM)
    return pl.pallas_call(
        self_back_kernel,
        in_specs=[pl.BlockSpec(memory_space=pltpu.SMEM)] + [inside] * 9 + [pl.BlockSpec(memory_space=pl.ANY)] * 3,
        out_specs=[inside] * 3,
        out_shape=[
            jax.ShapeDtypeStruct((rows, D), BF16),
            jax.ShapeDtypeStruct((rows, 3 * D), BF16),
            jax.ShapeDtypeStruct((rows, D), F32),
        ],
        scratch_shapes=[pltpu.VMEM(weight.shape, BF16) for weight in weights]
        + [pltpu.VMEM((rows, D), BF16), pltpu.SemaphoreType.DMA((3,))],
        compiler_params=pltpu.CompilerParams(vmem_limit_bytes=40 * 2**20),
        cost_estimate=estimate(8e9, 15e6),
        name="self_back",
    )(lengths, asked_grad, cross_total, plain_b, inverse_b, gain_b, joint, plain_a, inverse_a, gain_a, *weights)


def swap(value, axis, size, mask):
    return lax.ppermute(value, axis, [(i, i ^ mask) for i in range(size)])


def bit_of(axis, mask):
    return (lax.axis_index(axis) // mask) % 2


def pick(value, dim, index):
    return lax.dynamic_index_in_dim(value, index, dim, keepdims=False)


def halve(value, dim, axis, size, mask):
    bit = bit_of(axis, mask)
    arrived = swap(pick(value, dim, 1 - bit), axis, size, mask)
    return (pick(value, dim, bit).astype(F32) + arrived.astype(F32)).astype(BF16)


def join(value, dim, axis, size, mask):
    arrived = swap(value, axis, size, mask)
    bit = bit_of(axis, mask)
    return jnp.where(
        bit == 0, jnp.concatenate([value, arrived], axis=dim), jnp.concatenate([arrived, value], axis=dim)
    )


def masks(size):
    found, mask = [], 1
    while mask < size:
        found.append(mask)
        mask *= 2
    return found


def reduce_group(totals, sizes, rows_first):
    nseq, nnbr = sizes
    core = bit_of("seq", 1)
    parts = []
    for whole in totals:
        height, width = whole.shape
        parts.append(halve(whole.reshape(height, 2, width // 2), 1, "seq", nseq, 1))
    widths = [part.shape[1] for part in parts]
    total = parts[0] if len(parts) == 1 else jnp.concatenate(parts, axis=1)
    bits = masks(nnbr)
    rows = total.shape[0] // nnbr
    total = total.reshape((2,) * len(bits) + (rows, total.shape[1]))
    seq_bits = masks(nseq)[1:]

    def over_seq(total):
        for mask in seq_bits:
            shape = total.shape
            total = total.reshape(shape[:-2] + (2, shape[-2] // 2, shape[-1]))
            total = halve(total, total.ndim - 3, "seq", nseq, mask)
        return total

    def over_nbr(total):
        left = list(reversed(bits))
        for mask in bits:
            total = halve(total, left.index(mask), "nbr", nnbr, mask)
            left.remove(mask)
        return total

    if rows_first:
        total = over_nbr(over_seq(total))
        for mask in reversed(seq_bits):
            total = join(total, 0, "seq", nseq, mask)
    else:
        total = over_nbr(total)
        for mask in seq_bits:
            total = (total.astype(F32) + swap(total, "seq", nseq, mask).astype(F32)).astype(BF16)
    other = swap(total, "seq", nseq, 1)
    results, start = [], 0
    for width in widths:
        mine, theirs = total[:, start : start + width], other[:, start : start + width]
        results.append(
            jnp.where(
                core == 0, jnp.concatenate([mine, theirs], axis=1), jnp.concatenate([theirs, mine], axis=1)
            ).astype(F32)
        )
        start += width
    return results


def flip(index, mask):
    for bit in masks(mask + 1):
        if mask & bit:
            index = index + bit * (1 - 2 * ((lax.axis_index("seq") // bit) % 2))
    return index


def encoder_kernel(nseq, count, *refs):
    neighbours, gain_a, gain_b, gain_c, coderjoint, codermerge, coderup, coderdown = refs[:8]
    outs, received = refs[8:18], refs[18]
    entering, joint_w, merge_w, up_w, down_w = refs[19:24]
    kept, normed_c = refs[24:34], refs[34]
    load_sem, weight_sem, store_sem, send_sem, recv_sem = refs[35:]
    normed, joint, mixed, plain_b, inverse_b, normed_b, slope, hidden, plain_c, inverse_c = kept
    flat = entering.shape[0]
    rows, places = flat // nseq, flat // count
    s, n = lax.axis_index("seq"), lax.axis_index("nbr")

    barrier = pltpu.get_barrier_semaphore()
    for m in range(1, nseq):
        pl.semaphore_signal(barrier, inc=1, device_id=(flip(s, m), n), device_id_type=MESH)
    order = list(reversed(range(nseq)))
    loads = {}
    for m in order:
        source = pl.ds(pl.multiple_of(flip(s, m) * rows, rows), rows)
        loads[m] = pltpu.make_async_copy(neighbours.at[source], entering.at[pl.ds(m * rows, rows)], load_sem.at[m])
        loads[m].start()
    weights = Loads(weight_sem, (coderjoint, joint_w), (codermerge, merge_w), (coderup, up_w), (coderdown, down_w))
    pl.semaphore_wait(barrier, nseq - 1)

    stores, sends = [], []

    def store(src, dst):
        stores.append(pltpu.make_async_copy(src, dst, store_sem.at[len(stores)]))
        stores[-1].start()

    for turn, group in enumerate([(m,) for m in order[: nseq - 2]] + [(0, 1)]):
        begin, size = group[0] * rows, len(group) * rows
        window = pl.ds(begin, size)

        def put(*numbers, window=window):
            for k in numbers:
                store(kept[k].at[window], outs[k].at[window])

        for m in group:
            loads[m].wait()
        embedded = entering[window].astype(F32)
        normed[window] = norm_tile(embedded, gain_a[...])[0]
        if turn == 0:
            weights.wait(0)
        for third in range(3):
            lanes = slice(third * D, (third + 1) * D)
            joint[window, lanes] = dot_nn(normed[window], joint_w[:, lanes]).astype(BF16)
        put(0, 1)

        def attend(k, carry, begin=begin):
            inside = pl.ds(pl.multiple_of(begin + k * places, places), places)
            items = [tuple(joint[inside, col(p, third)] for third in range(3)) for p in range(PAIRS)]
            for p, block in enumerate(pairs_forward(items)):
                mixed[inside, col(p)] = block
            return carry

        lax.fori_loop(0, size // places, attend, 0)
        if turn == 0:
            weights.wait(1)
        middle = embedded + dot_nn(mixed[window], merge_w[...])
        rounded, plain, inverse = norm_tile(middle, gain_b[...])
        normed_b[window] = rounded
        plain_b[window] = plain.astype(BF16)
        inverse_b[window] = jnp.broadcast_to(inverse, (size, LANES))
        put(2, 3, 4, 5)
        if turn == 0:
            weights.wait(2)
            weights.wait(3)
        total = middle
        for f in range(hidden.shape[1] // D):
            lanes = slice(f * D, (f + 1) * D)
            bent, tilt = curve(dot_nn(rounded, up_w[:, lanes]))
            hidden[window, lanes] = bent
            slope[window, lanes] = tilt
            store(hidden.at[window, lanes], outs[7].at[window, lanes])
            store(slope.at[window, lanes], outs[6].at[window, lanes])
            total = total + dot_nn(bent, down_w[lanes])
        rounded, plain, inverse = norm_tile(total, gain_c[...])
        normed_c[window] = rounded
        plain_c[window] = plain.astype(BF16)
        inverse_c[window] = jnp.broadcast_to(inverse, (size, LANES))
        for m in reversed(group):
            part = pl.ds(m * rows, rows)
            if m == 0:
                store(normed_c.at[part], received.at[part])
            else:
                copy = pltpu.make_async_remote_copy(
                    src_ref=normed_c.at[part],
                    dst_ref=received.at[part],
                    send_sem=send_sem.at[m],
                    recv_sem=recv_sem.at[m],
                    device_id=(flip(s, m), n),
                    device_id_type=MESH,
                )
                copy.start()
                sends.append(copy)
        put(8, 9)
    for copy in stores + sends:
        copy.wait()


def encoder(neighbours, gains, weights, nseq):
    count, places, _ = neighbours.shape
    flat = count * places
    hidden = weights[2].shape[1]
    widths = (D, 3 * D, D, D, LANES, D, hidden, hidden, D, LANES)
    kinds = (BF16, BF16, BF16, BF16, F32, BF16, BF16, BF16, BF16, F32)
    anywhere = pl.BlockSpec(memory_space=pl.ANY)
    inside = pl.BlockSpec(memory_space=pltpu.VMEM)
    return pl.pallas_call(
        partial(encoder_kernel, nseq, count),
        in_specs=[anywhere] + [inside] * 3 + [anywhere] * 4,
        out_specs=[anywhere] * 11,
        out_shape=[jax.ShapeDtypeStruct((flat, w), k) for w, k in zip(widths, kinds)]
        + [jax.ShapeDtypeStruct((flat, D), BF16)],
        scratch_shapes=[pltpu.VMEM((flat, D), BF16)]
        + [pltpu.VMEM(weight.shape, BF16) for weight in weights]
        + [pltpu.VMEM((flat, w), k) for w, k in zip(widths, kinds)]
        + [
            pltpu.VMEM((flat, D), BF16),
            pltpu.SemaphoreType.DMA((nseq,)),
            pltpu.SemaphoreType.DMA((4,)),
            pltpu.SemaphoreType.DMA((20 * nseq,)),
            pltpu.SemaphoreType.DMA((nseq,)),
            pltpu.SemaphoreType.DMA((nseq,)),
        ],
        compiler_params=pltpu.CompilerParams(collective_id=1, has_side_effects=True, vmem_limit_bytes=60 * 2**20),
        cost_estimate=estimate(18e9, 50e6),
        name="encoder",
    )(neighbours.reshape(flat, D), *gains, *weights)


HALF = D // 2


MATRICES = 11
DOWN = (0, 7)
UNITS = (
    ((0, 0), (0, 1)),
    ((0, 2), (0, 3)),
    ((1, 0), (1, 1)),
    ((1, 2), (1, 3)),
    ((2, 0), (3, 0)),
    ((4, 0), (4, 1)),
    ((5, 0), (6, 0)),
    ((6, 1), (6, 2)),
    ((7, 0), (7, 1)),
    ((7, 2), (7, 3)),
    ((8, 0), (8, 1)),
    ((8, 2), (8, 3)),
    ((9, 0), (10, 0)),
    ((10, 1), (10, 2)),
)
CARRIED = {
    0: (("feed",),),
    1: (("spans", 0, 2),),
    2: (("spans", 2, 4), ("back",)),
    3: (("self",),),
    4: (("enter",), ("rows", 0)),
    5: (("rows", 1),),
    6: (("rows", 2),),
    7: (("rows", 3),),
    8: (("heads", 0, (0, 1)),),
    9: (("heads", 1, (0, 1)),),
    10: (("heads", 2, (0, 1)),),
    11: (("heads", 3, (0, 1)),),
}
TILE = 256
BACK_IN = (
    "length", "place_of", "feed_gain", "cross_gain", "self_gain", "gain_c", "gain_b",
    "out_grad", "dec_plain_a", "dec_inverse_a", "dec_plain_b", "dec_inverse_b", "dec_plain_c", "dec_inverse_c", "hidden_slope",
    "dec_joint", "asked", "memory",
    "plain_c", "inverse_c", "slope", "plain_b", "inverse_b", "joint",
    "feeddown", "feedup", "crossmerge", "memorymap", "crossquery", "selfmerge", "selfjoint", "coderdown", "coderup", "codermerge",
)


def backward_kernel(blocks, *refs):
    refs = list(refs)

    def take(number):
        taken = refs[:number]
        del refs[:number]
        return taken

    given_refs = dict(zip(BACK_IN, take(len(BACK_IN))))
    values = take(MATRICES)
    outs = take(MATRICES)
    (input_grad,) = take(1)
    (
        stage, first, own, mid, low_a, end_a, tail_a, low_b, end_b, tail_b, low_d, end_d, tail_d, tail_x, result,
        down_w, wide, merge_w, rising_grad, down_in, merge_in, joint_grad,
        y_in, plain_in, inverse_in, slope_in, plain_in_b, inverse_in_b, upper,
        feed_a, some_a, some_b, grad_in, self_in, dec_joint_grad,
        send_sem, recv_sem, local_sem,
    ) = refs
    rows = D // 8
    part = rows // 2
    flat = blocks * TILE
    places = TILE // 2
    s, n = lax.axis_index("seq"), lax.axis_index("nbr")
    c, x = s % 2, s // 2
    y, z1, z2 = n % 2, (n // 2) % 2, n // 4
    at_core, at_x = (s + 1 - 2 * c, n), (s + 2 - 4 * x, n)
    at_y, at_z1, at_z2 = (s, n + 1 - 2 * y), (s, n + 2 - 4 * z1), (s, n + 4 - 8 * z2)
    at_seq = (None, at_core, at_x, (3 - s, n))
    mine = pl.ds(pl.multiple_of(c * HALF, 128), HALF)
    other = pl.ds(pl.multiple_of((1 - c) * HALF, 128), HALF)
    kept = pl.ds(pl.multiple_of(x * part, 16), part)
    given = pl.ds(pl.multiple_of((1 - x) * part, 16), part)

    barrier = pltpu.get_barrier_semaphore()
    for partner in at_seq[1:] + (at_y, at_z1, at_z2):
        pl.semaphore_signal(barrier, inc=1, device_id=partner, device_id_type=MESH)

    pending = {}
    counts = {"local": 0, "remote": 0}

    def remote(key, src, dst, partner):
        index = counts["remote"]
        counts["remote"] += 1
        copy = pltpu.make_async_remote_copy(
            src_ref=src,
            dst_ref=dst,
            send_sem=send_sem.at[index],
            recv_sem=recv_sem.at[index],
            device_id=partner,
            device_id_type=MESH,
        )
        copy.start()
        pending[key] = copy

    def local(key, src, dst):
        copy = pltpu.make_async_copy(src, dst, local_sem.at[counts["local"]])
        counts["local"] += 1
        copy.start()
        pending.setdefault(key, []).append(copy)

    def load(key, name, dst):
        local(key, given_refs[name], dst)

    def arrived(key):
        for copy in pending.pop(key, []):
            copy.wait()

    def tile(block, number=1):
        return pl.ds(block * TILE, number * TILE)


    def fetch(u):
        if u == 0:
            local(("unit", 0), given_refs["hidden_slope"].at[0], feed_a)
        elif u == 2:
            local(("unit", u), values[1], some_a.at[tile(0)])
        elif u in (4, 6):
            for k in range(2):
                local(("unit", u), values[u - 2 + k if u == 4 else u - 1 + k], some_a.at[tile(k)])
        elif u == 5:
            local(("unit", u), values[4], some_a)
        elif u == 8:
            local(("unit", 8), values[7], wide)
            for k in range(3):
                local(("unit", 10), values[8 + k], down_w.at[pl.ds(k * flat, flat)])

    def operands(u, k):
        left = pl.ds(k * D, D)
        if u in (2, 3):
            return some_a.at[tile(0)], rising_grad.at[tile(u - 2), pl.ds((2 + k) * D, D)]
        if u == 4:
            return some_a.at[tile(k)], some_a.at[tile(2 + k)]
        if u == 5:
            return some_a, some_b.at[:, left]
        if u == 6:
            return some_a.at[tile(k)], self_in if k == 0 else dec_joint_grad.at[:, pl.ds(0, D)]
        if u == 7:
            return some_a.at[tile(1)], dec_joint_grad.at[:, pl.ds((1 + k) * D, D)]
        if u in (10, 11):
            return down_w.at[pl.ds(0, flat)], rising_grad.at[:, pl.ds(((u - 10) * 2 + k) * D, D)]
        if u == 12:
            return down_w.at[pl.ds((1 + k) * flat, flat)], merge_in if k == 0 else joint_grad.at[:, pl.ds(0, D)]
        return down_w.at[pl.ds(2 * flat, flat)], joint_grad.at[:, pl.ds((1 + k) * D, D)]

    def product(u):
        if UNITS[u][0][0] in DOWN:
            left, right = (feed_a, grad_in) if u < 2 else (wide, down_in)
            begin = (u % 2) * 2 * rows

            def one(shard, carry):
                columns = left[:, pl.ds(pl.multiple_of(shard * 4 * rows, 128), 4 * rows)]
                block = dot_tn(columns[:, begin : begin + 2 * rows], right[...]).astype(BF16)
                stage[0, shard] = block[:rows]
                stage[1, shard] = block[rows:]
                return carry

            lax.fori_loop(0, 8, one, 0)
            return
        for k in range(2):
            left, right = operands(u, k)
            stage[k] = dot_tn(left[...], right[...]).astype(BF16).reshape(8, rows, D)


    def slot(u):
        return u % 5, u % 4

    def straight(u):
        return u % 4 != 2

    def wide_slot(u):
        return (u // 4 * 3 + (0, 1, None, 2)[u % 4]) % 4

    def stage0(u):
        arrived(("unit", u))
        product(u)
        remote(("core", u), stage.at[:, :, :, other], first.at[u % 2], at_core)

    def stage1(u):
        five, four = slot(u)
        pending.pop(("core", u)).wait()

        def one(k, carry):
            k, a, b, d = k // 8, (k // 4) % 2, (k // 2) % 2, k % 2
            shard = 4 * a + 2 * b + d
            own[five, k, a, b, d] = stage[k, shard, :, mine] + first[u % 2, k, shard]
            return carry

        lax.fori_loop(0, 16, one, 0)
        if straight(u):
            remote(("a", u), own.at[five, 0, :, :, :, given], mid.at[wide_slot(u)], at_x)
            remote(("b", u), own.at[five, 1, :, :, 1 - y], low_b.at[four], at_y)
        else:
            remote(("a", u), own.at[five, 0, :, :, 1 - y], low_b.at[four], at_y)
            remote(("b", u), own.at[five, 1, :, 1 - z1], low_d, at_z1)

    def stage2(u):
        five, four = slot(u)
        pending.pop(("a", u)).wait()
        pending.pop(("b", u)).wait()
        for a in range(2):
            for b in range(2):
                if straight(u):
                    for d in range(2):
                        own[five, 0, a, b, d, kept] = own[five, 0, a, b, d, kept] + mid[wide_slot(u), a, b, d]
                    own[five, 1, a, b, y] = own[five, 1, a, b, y] + low_b[four, a, b]
                else:
                    own[five, 0, a, b, y] = own[five, 0, a, b, y] + low_b[four, a, b]
                    own[five, 1, a, z1, b] = own[five, 1, a, z1, b] + low_d[a, b]
        if straight(u):
            remote(("a", u), own.at[five, 0, :, :, 1 - y, kept], low_a.at[four], at_y)
        else:
            remote(("a", u), own.at[five, 0, :, :, y, given], low_a.at[four], at_x)
        if straight(u):
            remote(("b", u), own.at[five, 1, :, 1 - z1, y], end_b.at[four], at_z1)
        else:
            remote(("b", u), own.at[five, 1, 1 - z2, z1], end_d, at_z2)

    def stage3(u):
        five, four = slot(u)
        pending.pop(("a", u)).wait()
        pending.pop(("b", u)).wait()
        for a in range(2):
            for b in range(2):
                own[five, 0, a, b, y, kept] = own[five, 0, a, b, y, kept] + low_a[four, a, b]
            if straight(u):
                own[five, 1, a, z1, y] = own[five, 1, a, z1, y] + end_b[four, a]
            else:
                own[five, 1, z2, z1, a] = own[five, 1, z2, z1, a] + end_d[a]
        remote(("a", u), own.at[five, 0, :, 1 - z1, y, kept], end_a.at[four], at_z1)
        if straight(u):
            remote(("b", u), own.at[five, 1, 1 - z2, z1, y], tail_b.at[four], at_z2)
        else:
            remote(("b", u), own.at[five, 1, z2, z1, 1 - y], tail_d, at_y)

    def stage4(u):
        five, four = slot(u)
        pending.pop(("a", u)).wait()
        pending.pop(("b", u)).wait()
        for a in range(2):
            own[five, 0, a, z1, y, kept] = own[five, 0, a, z1, y, kept] + end_a[four, a]
        own[five, 1, z2, z1, y] = own[five, 1, z2, z1, y] + (tail_b[four] if straight(u) else tail_d[...])
        remote(("a", u), own.at[five, 0, 1 - z2, z1, y, kept], tail_a.at[four], at_z2)
        remote(("b", u), own.at[five, 1, z2, z1, y], tail_x.at[four], at_x)

    def stage5(u):
        five, four = slot(u)
        pending.pop(("a", u)).wait()
        pending.pop(("b", u)).wait()
        result[u % 6, 0, kept, mine] = own[five, 0, z2, z1, y, kept] + tail_a[four]
        result[u % 6, 1, :, mine] = own[five, 1, z2, z1, y] + tail_x[four]
        piece = result.at[u % 6, 0, kept, mine]
        remote(("a", u), piece, piece, at_x)

    def stage6(u):
        pending.pop(("a", u)).wait()
        piece = result.at[u % 6, :, :, mine]
        remote(("a", u), piece, piece, at_core)

    def stage7(u):
        pending.pop(("a", u)).wait()
        for k, (matrix, block) in enumerate(UNITS[u]):
            if matrix in DOWN:
                target = outs[matrix].at[pl.ds(block * rows, rows)]
            else:
                target = outs[matrix].at[:, pl.ds(block * D, D)]
            local(("out", u), result.at[u % 6, k], target)

    def stage8(u):
        arrived(("out", u))

    stages = (stage0, stage1, stage2, stage3, stage4, stage5, stage6, stage7, stage8)


    def carry_feed():
        arrived("feed")
        total = None
        for f in range(4):
            lanes = pl.ds(f * D, D)
            rounded = (dot_nt(grad_in[...], down_w[lanes]) * slope_in[:, lanes].astype(F32)).astype(BF16)
            rising_grad[tile(f // 2), pl.ds((2 + f % 2) * D, D)] = rounded
            back = dot_nt(rounded, wide[pl.ds(0, D), lanes])
            total = back if total is None else total + back
        total = grad_in[...].astype(F32) + norm_back_tile(
            total, plain_in[...].astype(F32), inverse_in[:, :1], given_refs["feed_gain"][...]
        )
        upper[...] = total
        cross_in = (total * live_rows(TILE, given_refs["length"][0])).astype(BF16)
        some_a[tile(2)] = cross_in
        arrived("cross")
        down_in[tile(1)] = dot_nt(cross_in, merge_w[0]).astype(BF16)
        load("weights", "coderdown", down_w)
        load("weights", "coderup", wide.at[pl.ds(0, D)])
        load("self", "selfmerge", merge_w.at[0])
        load("enter", "dec_plain_a", plain_in)
        load("enter", "dec_inverse_a", inverse_in)

    def carry_spans(begin, end):
        def one(span, carry):
            window = pl.ds(pl.multiple_of(span * CH, CH), CH)
            shifted = pl.ds(pl.multiple_of(TILE + span * CH, CH), CH)
            around = pl.ds(pl.multiple_of(span * TILE, TILE), TILE)
            items = [
                (down_in[window, col(p)], rising_grad[around, col(p, 0)], rising_grad[around, col(p, 1)], down_in[shifted, col(p)])
                for p in range(PAIRS)
            ]
            for p, (dq, dk, dv) in enumerate(pairs_backward(items)):
                some_a[pl.ds(pl.multiple_of(3 * TILE + span * CH, CH), CH), col(p)] = dq
                some_b[around, col(p, 0)] = dk
                some_b[around, col(p, 1)] = dv
            return carry

        lax.fori_loop(begin, end, one, 0)

    def carry_back():
        arrived("map")

        def one(block, carry):
            window = pl.ds(pl.multiple_of(block * TILE, TILE), TILE)
            down_in[window] = dot_nt(some_b[window], joint_grad[pl.ds(0, D), pl.ds(0, 2 * D)]).astype(BF16)
            return carry

        lax.fori_loop(0, blocks, one, 0)
        load("enter", "selfjoint", joint_grad.at[pl.ds(0, D)])
        for k in range(2 * blocks):
            place = given_refs["place_of"][k]
            total = None
            for span in range(2 * blocks):
                weight = (place == span).astype(F32)
                part_of = down_in[pl.ds(span * places, places)].astype(F32) * weight
                total = part_of if total is None else total + part_of
            merge_in[pl.ds(k * places, places)] = total.astype(BF16)
        for m in range(1, blocks):
            remote(("y", m), merge_in.at[tile(m)], y_in.at[m - 1], at_seq[m])

    def carry_self():
        arrived("self")
        total = upper[...] + norm_back_tile(
            dot_nt(some_a[tile(3)], merge_w[1]), plain_in_b[...].astype(F32), inverse_in_b[:, :1], given_refs["cross_gain"][...]
        )
        upper[...] = total
        self_in[...] = total.astype(BF16)
        load("weights", "codermerge", merge_w.at[1])
        feed_a[:, pl.ds(3 * D, D)] = dot_nt(self_in[...], merge_w[0]).astype(BF16)
        allowed = causal_mask(TILE, given_refs["length"][0])
        for group in range(0, PAIRS, 3):
            pairs = range(group, group + 3)
            items = [tuple(joint_grad[tile(3), col(p, third)] for third in range(3)) + (feed_a[:, pl.ds(3 * D + p * LANES, LANES)],) for p in pairs]
            for p, pieces in zip(pairs, pairs_backward(items, allowed)):
                for third in range(3):
                    dec_joint_grad[:, col(p, third)] = pieces[third]

    def carry_enter():
        arrived("enter")
        back = dot_nt(dec_joint_grad[...], joint_grad[pl.ds(0, D)])
        upper[...] = upper[...] + norm_back_tile(
            back, plain_in[...].astype(F32), inverse_in[:, :1], given_refs["self_gain"][...]
        )
        local("input", upper, input_grad)
        fetch_rows(0)


    def fetch_rows(block):
        window = tile(block)
        local("rows", given_refs["plain_c"].at[window], plain_in)
        local("rows", given_refs["inverse_c"].at[window], inverse_in)
        local("rows", given_refs["slope"].at[window], slope_in)
        local("rows", given_refs["plain_b"].at[window], plain_in_b)
        local("rows", given_refs["inverse_b"].at[window], inverse_in_b)

    def fetch_heads(block):
        local("heads", given_refs["joint"].at[tile(block)], dec_joint_grad)

    def carry_rows(block):
        window = tile(block)
        arrived("rows")
        if block == 0:
            arrived("weights")
            arrived("input")
            came = merge_in[window]
        else:
            pending.pop(("y", block)).wait()
            came = y_in[block - 1]
        total = norm_back_tile(
            came.astype(F32), plain_in[...].astype(F32), inverse_in[:, :1], given_refs["gain_c"][...]
        )
        upper[...] = total
        down_in[window] = total.astype(BF16)
        for f in range(4):
            lanes = pl.ds(f * D, D)
            rounded = (dot_nt(down_in[window], down_w[lanes]) * slope_in[:, lanes].astype(F32)).astype(BF16)
            rising_grad[window, lanes] = rounded
            back = dot_nt(rounded, wide[pl.ds(0, D), lanes])
            total = back if f == 0 else total + back
        total = upper[...] + norm_back_tile(
            total, plain_in_b[...].astype(F32), inverse_in_b[:, :1], given_refs["gain_b"][...]
        )
        rounded = total.astype(BF16)
        merge_in[window] = rounded
        feed_a[:, pl.ds(block * D, D)] = dot_nt(rounded, merge_w[1]).astype(BF16)
        if block + 1 < blocks:
            fetch_rows(block + 1)
        else:
            fetch(8)
            fetch_heads(0)

    def carry_heads(block, which):
        if which[0] == 0:
            arrived("heads")

        def one(k, carry):
            inside = pl.ds(pl.multiple_of(k * places, 128), places)
            outside = pl.ds(pl.multiple_of(block * TILE + k * places, 128), places)
            items = [
                tuple(dec_joint_grad[inside, col(p, third)] for third in range(3)) + (feed_a[inside, pl.ds(block * D + p * LANES, LANES)],)
                for p in range(PAIRS)
            ]
            for p, pieces in enumerate(pairs_backward(items)):
                for third in range(3):
                    joint_grad[outside, col(p, third)] = pieces[third]
            return carry

        lax.fori_loop(which[0], which[-1] + 1, one, 0)
        if which[-1] == 1 and block + 1 < blocks:
            fetch_heads(block + 1)

    carried = {
        "feed": carry_feed,
        "spans": carry_spans,
        "back": carry_back,
        "self": carry_self,
        "enter": carry_enter,
        "rows": carry_rows,
        "heads": carry_heads,
    }
    load(("unit", 0), "out_grad", grad_in)
    fetch(0)
    load("feed", "feeddown", down_w)
    local("feed", given_refs["hidden_slope"].at[1], slope_in)
    load("feed", "feedup", wide.at[pl.ds(0, D)])
    load("feed", "dec_plain_c", plain_in)
    load("feed", "dec_inverse_c", inverse_in)
    load("cross", "crossmerge", merge_w.at[0])
    load("cross", "asked", down_in.at[tile(0)])
    load("cross", "memory", rising_grad.at[:, pl.ds(0, 2 * D)])
    load("map", "memorymap", joint_grad.at[pl.ds(0, D), pl.ds(0, 2 * D)])
    load("self", "crossquery", merge_w.at[1])
    load("self", "dec_plain_b", plain_in_b)
    load("self", "dec_inverse_b", inverse_in_b)
    load("self", "dec_joint", joint_grad.at[tile(3)])
    pl.semaphore_wait(barrier, 6)
    for tick in range(len(UNITS) + len(stages) - 1):
        for level in (1, 0) + tuple(range(2, len(stages))):
            if 0 <= tick - level < len(UNITS):
                stages[level](tick - level)
        if 1 <= tick < 7:
            fetch(tick + 1)
        for kind, *details in CARRIED.get(tick, ()):
            carried[kind](*details)


def backward(blocks, given, values, heights):
    rows = D // 8
    part = rows // 2
    flat = blocks * TILE
    anywhere = pl.BlockSpec(memory_space=pl.ANY)
    spaces = [pltpu.SMEM] * 2 + [pltpu.VMEM] * 5 + [pl.ANY] * (len(BACK_IN) - 7 + MATRICES)

    def room(*shape, dtype=BF16):
        return pltpu.VMEM(shape, dtype)

    return pl.pallas_call(
        partial(backward_kernel, blocks),
        in_specs=[pl.BlockSpec(memory_space=space) for space in spaces],
        out_specs=[anywhere] * (MATRICES + 1),
        out_shape=[jax.ShapeDtypeStruct(height, BF16) for height in heights] + [jax.ShapeDtypeStruct((TILE, D), F32)],
        scratch_shapes=[
            room(2, 8, rows, D),
            room(2, 2, 8, rows, HALF),
            room(5, 2, 2, 2, 2, rows, HALF),
            room(4, 2, 2, 2, part, HALF),
            room(4, 2, 2, part, HALF),
            room(4, 2, part, HALF),
            room(4, part, HALF),
            room(4, 2, 2, rows, HALF),
            room(4, 2, rows, HALF),
            room(4, rows, HALF),
            room(2, 2, rows, HALF),
            room(2, rows, HALF),
            room(rows, HALF),
            room(4, rows, HALF),
            room(6, 2, rows, D),
            room(4 * D, D),
            room(flat, 4 * D),
            room(2, D, D),
            room(flat, 4 * D),
            room(flat, D),
            room(flat, D),
            room(flat, 3 * D),
            room(blocks - 1, TILE, D),
            room(TILE, D),
            room(TILE, LANES, dtype=F32),
            room(TILE, 4 * D),
            room(TILE, D),
            room(TILE, LANES, dtype=F32),
            room(TILE, D, dtype=F32),
            room(TILE, 4 * D),
            room(flat, D),
            room(flat, 2 * D),
            room(TILE, D),
            room(TILE, D),
            room(TILE, 3 * D),
            pltpu.SemaphoreType.DMA((len(UNITS) * 12,)),
            pltpu.SemaphoreType.DMA((len(UNITS) * 12,)),
            pltpu.SemaphoreType.DMA((128,)),
        ],
        compiler_params=pltpu.CompilerParams(
            collective_id=0, has_side_effects=True, vmem_limit_bytes=62 * 2**20
        ),
        cost_estimate=estimate(55e9, 120e6),
        name="backward_and_sums",
    )(*[given[name] for name in BACK_IN], *values)


GAINED = (6, 3, 1, 10, 8, 4)


def finish_kernel(nnbr, *refs):
    gains, sums, weights, outs, gain_outs = refs[:6], refs[6:17], refs[17:23], refs[23:34], refs[34:40]
    sums_in, weights_in, wide = refs[40:51], refs[51:57], refs[57:68]
    sum_sems, weight_sems, out_sems = refs[68:]
    rows = gain_outs[0].shape[1]
    n = lax.axis_index("nbr")
    own = pl.ds(pl.multiple_of(n * rows, 8), rows)
    loads = Loads(sum_sems, *zip(sums, sums_in))
    weight_loads = Loads(weight_sems, *[(weight.at[own], inside) for weight, inside in zip(weights, weights_in)])
    row = lax.broadcasted_iota(jnp.int32, (D, rows), 0)
    place = lax.broadcasted_iota(jnp.int32, (D, rows), 1) + n * rows
    own_gains = lax.dot_general(
        jnp.concatenate([gain[...][None] for gain in gains], axis=0),
        (row == place).astype(F32),
        (((1,), (0,)), ((), ())),
        precision=lax.Precision.HIGHEST,
        preferred_element_type=F32,
    )
    diagonal = lax.broadcasted_iota(jnp.int32, (rows, rows), 0) == lax.broadcasted_iota(jnp.int32, (rows, rows), 1)
    stores = []
    for matrix in range(len(sums)):
        loads.wait(matrix)
        wide[matrix][...] = sums_in[matrix][...].astype(F32)
        stores.append(pltpu.make_async_copy(wide[matrix], outs[matrix], out_sems.at[matrix]))
        stores[-1].start()
    for k, matrix in enumerate(GAINED):
        weight_loads.wait(k)
        product = weights_in[k][...].astype(F32) * wide[matrix][...]
        summed = jnp.sum(product, axis=1, keepdims=True)
        across = jnp.sum(jnp.where(diagonal, summed, 0.0), axis=0, keepdims=True)
        gain_outs[k][...] = across / own_gains[k : k + 1]
    for copy in stores:
        copy.wait()


def finish(sums, gains, weights, nnbr):
    rows = D // nnbr
    anywhere = pl.BlockSpec(memory_space=pl.ANY)
    inside = pl.BlockSpec(memory_space=pltpu.VMEM)
    results = pl.pallas_call(
        partial(finish_kernel, nnbr),
        in_specs=[inside] * 6 + [anywhere] * (len(sums) + len(weights)),
        out_specs=[pl.BlockSpec(memory_space=pltpu.HBM)] * len(sums) + [inside] * len(weights),
        out_shape=[jax.ShapeDtypeStruct(total.shape, F32) for total in sums]
        + [jax.ShapeDtypeStruct((1, rows), F32)] * len(weights),
        scratch_shapes=[pltpu.VMEM(total.shape, total.dtype) for total in sums]
        + [pltpu.VMEM((rows, weight.shape[1]), BF16) for weight in weights]
        + [pltpu.VMEM(total.shape, F32) for total in sums]
        + [
            pltpu.SemaphoreType.DMA((len(sums),)),
            pltpu.SemaphoreType.DMA((len(weights),)),
            pltpu.SemaphoreType.DMA((len(sums),)),
        ],
        compiler_params=pltpu.CompilerParams(vmem_limit_bytes=56 * 2**20),
        cost_estimate=estimate(1e7, 20e6),
        name="finish",
    )(*gains, *sums, *weights)
    return results[: len(sums)], [grad.reshape(rows) for grad in results[len(sums) :]]


def body(
    sizes,
    tokens,
    neighbours,
    out_grad,
    lengths,
    slot_order,
    selfgain,
    selfjoint,
    selfmerge,
    crossgain,
    crossquery,
    crossmerge,
    feedgain,
    feedup,
    feeddown,
    codergain,
    coderjoint,
    codermerge,
    codermid,
    coderup,
    coderdown,
    codertop,
    memorymap,
):
    nseq, nnbr = sizes
    count, places, _ = neighbours.shape
    flat = count * places

    (
        enc_normed, enc_joint, enc_mixed, enc_plain_b, enc_inverse_b, enc_normed_b, enc_slope, enc_hidden, enc_plain_c, enc_inverse_c,
        received,
    ) = encoder(
        neighbours,
        [codergain, codermid, codertop],
        [coderjoint, codermerge, coderup, coderdown],
        nseq,
    )

    (
        output, normed_a, plain_a, inverse_a, joint, mixed, normed_b, plain_b, inverse_b, asked, chosen, memory, crossed, normed_c,
        plain_c, inverse_c, hidden_slope, place_of,
    ) = decoder(
        tokens[0],
        lengths,
        slot_order,
        received,
        [selfgain, crossgain, feedgain],
        [selfjoint, selfmerge, crossquery, memorymap, crossmerge, feedup, feeddown],
        nseq,
    )
    values = [
        hidden_slope[0], normed_c, crossed, normed_b, chosen, mixed, normed_a, enc_hidden, enc_normed_b, enc_mixed, enc_normed,
    ]
    if nseq == 4 and nnbr == 8:
        weights = [
            feeddown, feedup, crossmerge, crossquery, memorymap, selfmerge, selfjoint, coderdown, coderup, codermerge, coderjoint
        ]
        given = dict(
            length=lengths, place_of=place_of, feed_gain=feedgain, cross_gain=crossgain, self_gain=selfgain, gain_c=codertop,
            gain_b=codermid, out_grad=out_grad[0], dec_plain_a=plain_a, dec_inverse_a=inverse_a, dec_plain_b=plain_b,
            dec_inverse_b=inverse_b, dec_plain_c=plain_c, dec_inverse_c=inverse_c, hidden_slope=hidden_slope, dec_joint=joint,
            asked=asked, memory=memory, plain_c=enc_plain_c, inverse_c=enc_inverse_c, slope=enc_slope, plain_b=enc_plain_b,
            inverse_b=enc_inverse_b, joint=enc_joint, feeddown=feeddown, feedup=feedup, crossmerge=crossmerge,
            memorymap=memorymap, crossquery=crossquery, selfmerge=selfmerge, selfjoint=selfjoint, coderdown=coderdown,
            coderup=coderup, codermerge=codermerge,
        )
        *sums, input_grad = backward(nseq, given, [normed_c] + values[1:], [(w.shape[0] // nnbr, w.shape[1]) for w in weights])
    else:
        down_in = out_grad[0]
        rising_grad = (hidden_slope[1].astype(F32) * times_back(down_in, feeddown)).astype(BF16)
        cross_total = down_in.astype(F32) + norm_backward(
            times_back(rising_grad, feedup), plain_c.astype(F32), inverse_c[:, :1], feedgain
        )
        live = (jnp.arange(tokens.shape[1], dtype=jnp.int32) // CH * CH < lengths[0]).astype(F32)[:, None]
        cross_in = (cross_total * live).astype(BF16)
        asked_grad, memory_grad = spans_backward(asked, memory, times_back(cross_in, crossmerge).astype(BF16))
        back = times_back(memory_grad, memorymap).astype(BF16).reshape(count, places, D)[place_of]
        back = back.reshape(nseq, flat // nseq, D)
        returned = [back[m] if m == 0 else swap(back[m], "seq", nseq, m) for m in range(nseq)]
        self_in, joint_grad, input_grad = self_back(
            lengths, asked_grad, cross_total, plain_b, inverse_b, crossgain, joint, plain_a, inverse_a, selfgain,
            [crossquery, selfmerge, selfjoint],
        )
        upper_total = norm_backward(
            jnp.concatenate(returned, axis=0).astype(F32), enc_plain_c.astype(F32), enc_inverse_c[:, :1], codertop
        )
        enc_down_in = upper_total.astype(BF16)
        enc_rising_grad = (enc_slope.astype(F32) * times_back(enc_down_in, coderdown)).astype(BF16)
        middle_total = upper_total + norm_backward(
            times_back(enc_rising_grad, coderup), enc_plain_b.astype(F32), enc_inverse_b[:, :1], codermid
        )
        enc_merge_in = middle_total.astype(BF16)
        enc_mixed_grad = times_back(enc_merge_in, codermerge).astype(BF16).reshape(count, places, D)
        enc_joint_grad = enc_attend_back(enc_joint.reshape(count, places, 3 * D), enc_mixed_grad).reshape(flat, 3 * D)
        grads = [
            down_in, rising_grad, cross_in, asked_grad, memory_grad, self_in, joint_grad, enc_down_in, enc_rising_grad, enc_merge_in,
            enc_joint_grad,
        ]
        sums = [weight_grad(v, g).astype(BF16) for v, g in zip(values, grads)]
        ways = (False, True, False, False, False, False, False, True, False, True, True)
        sums = [reduce_group([total], sizes, way)[0] for total, way in zip(sums, ways)]
    output, input_grad = output[None], input_grad[None]
    sums, gain_grads = finish(
        sums,
        [selfgain, crossgain, feedgain, codergain, codermid, codertop],
        [selfjoint, crossquery, feedup, coderjoint, coderup, memorymap],
        nnbr,
    )
    (
        grad_feeddown,
        grad_feedup,
        grad_crossmerge,
        grad_crossquery,
        grad_memorymap,
        grad_selfmerge,
        grad_selfjoint,
        grad_coderdown,
        grad_coderup,
        grad_codermerge,
        grad_coderjoint,
    ) = sums
    grad_selfgain, grad_crossgain, grad_feedgain, grad_codergain, grad_codermid, grad_codertop = gain_grads
    return (
        output,
        input_grad,
        grad_selfgain,
        grad_selfjoint,
        grad_selfmerge,
        grad_crossgain,
        grad_crossquery,
        grad_crossmerge,
        grad_feedgain,
        grad_feedup,
        grad_feeddown,
        grad_codergain,
        grad_coderjoint,
        grad_codermerge,
        grad_codermid,
        grad_coderup,
        grad_coderdown,
        grad_codertop,
        grad_memorymap,
    )


def solution(mesh):
    spread = ("seq", "nbr")
    sizes = (mesh.shape["seq"], mesh.shape["nbr"])
    placed = (
        P(spread, None, None),
        P(spread, None, None),
        P(spread, None, None),
        P(spread),
        P(spread, None),
    ) + (P(),) * 17
    gain, weight = P("nbr"), P("nbr", None)
    return jax.shard_map(
        partial(body, sizes),
        mesh=mesh,
        in_specs=placed,
        out_specs=(
            P(spread, None, None),
            P(spread, None, None),
            gain,
            weight,
            weight,
            gain,
            weight,
            weight,
            gain,
            weight,
            weight,
            gain,
            weight,
            weight,
            gain,
            weight,
            weight,
            gain,
            weight,
        ),
        check_vma=False,
    )
```

```python
from functools import partial

import jax
import jax.numpy as jnp
from jax import lax
from jax.experimental import pallas as pl
from jax.experimental.pallas import tpu as pltpu
from jax.sharding import PartitionSpec as P

D = 768
HEADS = 12
HD = 64
CH = 64
PAIRS = HEADS // 2
LANES = 2 * HD
SCALE = HD ** (-0.5)
F32 = jnp.float32
BF16 = jnp.bfloat16
MESH = pl.DeviceIdType.MESH


def norm_backward(grad, normed, inverse, gain):
    scaled = grad * gain
    inner = jnp.mean(scaled * normed, axis=-1, keepdims=True)
    return inverse * (scaled - jnp.mean(scaled, axis=-1, keepdims=True) - normed * inner)


def times(values, weight):
    return lax.dot_general(values, weight, (((1,), (0,)), ((), ())), preferred_element_type=F32)


def times_back(grad, weight):
    return lax.dot_general(grad, weight, (((1,), (1,)), ((), ())), preferred_element_type=F32)


def weight_grad(values, grad):
    return lax.dot_general(values, grad, (((0,), (0,)), ((), ())), preferred_element_type=F32)


def curve(rising):
    square = rising * rising
    bend = jnp.tanh(rising * (0.7978845608028654 + 0.035677408136300125 * square))
    half = 0.5 * (1.0 + bend)
    slope = half + 0.5 * rising * (1.0 - bend * bend) * (0.7978845608028654 + 0.10703222440890037 * square)
    return (rising * half).astype(BF16), slope.astype(BF16)


def dot_nt(a, b):
    return lax.dot_general(a, b, (((1,), (1,)), ((), ())), preferred_element_type=F32)


def dot_nn(a, b):
    return lax.dot_general(a, b, (((1,), (0,)), ((), ())), preferred_element_type=F32)


def dot_tn(a, b):
    return lax.dot_general(a, b, (((0,), (0,)), ((), ())), preferred_element_type=F32)


def stack_pair(block):
    lane = lax.broadcasted_iota(jnp.int32, block.shape, 1)
    zero = jnp.zeros_like(block)
    return jnp.concatenate([jnp.where(lane < HD, block, zero), jnp.where(lane >= HD, block, zero)], axis=0)


def unstack_pair(stacked):
    half = stacked.shape[0] // 2
    lane = lax.broadcasted_iota(jnp.int32, (half, LANES), 1)
    return jnp.where(lane < HD, stacked[:half], stacked[half:])


def halves(block):
    width = block.shape[1] // 2
    return block[:, :width], block[:, width:]


def exponents(products, allowed):
    parts = []
    for scores in halves(products):
        if allowed is not None:
            scores = jnp.where(allowed, scores, -1000000000.0)
        parts.append(jnp.exp((scores - jnp.max(scores, axis=-1, keepdims=True)) * SCALE).astype(BF16))
    return jnp.concatenate(parts, axis=1)


def summing(width, lanes):
    row = lax.broadcasted_iota(jnp.int32, (2 * width, lanes), 0)
    lane = lax.broadcasted_iota(jnp.int32, (2 * width, lanes), 1)
    return ((row < width) == (lane < lanes // 2)).astype(BF16)


def pairs_forward(items, allowed=None):
    ones = summing(items[0][1].shape[0], LANES)
    scores = [dot_nt(queries, stack_pair(keys)) for queries, keys, _ in items]
    raised = [exponents(block, allowed) for block in scores]
    mixed = [
        dot_nn(block, jnp.concatenate([stack_pair(values), ones], axis=1)) for block, (_, _, values) in zip(raised, items)
    ]
    return [(block[:, :LANES] / block[:, LANES:]).astype(BF16) for block in mixed]


def pairs_backward(items, allowed=None):
    width = items[0][1].shape[0]
    ones = summing(width, 2 * width)
    stacked = [stack_pair(keys) for _, keys, _, _ in items]
    scores = [dot_nt(item[0], keys) for item, keys in zip(items, stacked)]
    prob_grads = [dot_nt(item[3], stack_pair(item[2])) for item in items]
    raised = [exponents(block, allowed) for block in scores]
    totals = [dot_nn(block, ones) for block in raised]
    probs = [block.astype(F32) * (1.0 / total) for block, total in zip(raised, totals)]
    value_grads = [unstack_pair(dot_tn(block.astype(BF16), item[3])) for block, item in zip(probs, items)]
    score_grads = []
    for block, grad in zip(probs, prob_grads):
        parts = []
        for prob, part in zip(halves(block), halves(block * grad)):
            parts.append(((part - prob * jnp.sum(part, axis=-1, keepdims=True)) * SCALE).astype(BF16))
        score_grads.append(jnp.concatenate(parts, axis=1))
    query_grads = [dot_nn(grad, keys) for grad, keys in zip(score_grads, stacked)]
    key_grads = [unstack_pair(dot_tn(grad, item[0])) for grad, item in zip(score_grads, items)]
    return [tuple(g.astype(BF16) for g in grads) for grads in zip(query_grads, key_grads, value_grads)]


def col(pair, third=0):
    return slice(third * D + pair * LANES, third * D + (pair + 1) * LANES)


def estimate(flops, nbytes, exps=0):
    return pl.CostEstimate(flops=int(flops), bytes_accessed=int(nbytes), transcendentals=int(exps))


def spans_backward(asked, memory, outgoing):
    spans = asked.shape[0] // CH
    queries, grads = (block.reshape(spans, CH, HEADS, HD) for block in (asked, outgoing))
    keys, values = (memory[:, k * D : (k + 1) * D].reshape(spans, -1, HEADS, HD) for k in range(2))

    def product(form, left, right):
        return jnp.einsum(form, left, right, preferred_element_type=F32)

    probs = jax.nn.softmax(product("brhd,bshd->bhrs", queries, keys) * SCALE, axis=-1)
    value_grad = product("bhrs,brhd->bshd", probs.astype(BF16), grads)
    prob_grad = product("brhd,bshd->bhrs", grads, values)
    inner = jnp.sum(probs * prob_grad, axis=-1, keepdims=True)
    score_grad = (probs * (prob_grad - inner) * SCALE).astype(BF16)
    query_grad = product("bhrs,bshd->brhd", score_grad, keys)
    key_grad = product("bhrs,brhd->bshd", score_grad, queries)
    memory_grad = jnp.concatenate([block.reshape(-1, D) for block in (key_grad, value_grad)], axis=1)
    return query_grad.reshape(-1, D).astype(BF16), memory_grad.astype(BF16)


def enc_attend_back_kernel(joint_ref, grad_ref, out_ref):
    items = [
        tuple(joint_ref[0, :, col(p, third)] for third in range(3)) + (grad_ref[0, :, col(p)],) for p in range(PAIRS)
    ]
    for p, grads in enumerate(pairs_backward(items)):
        for third in range(3):
            out_ref[0, :, col(p, third)] = grads[third]


def enc_attend_back(joint, grad):
    count, rows, _ = joint.shape
    return pl.pallas_call(
        enc_attend_back_kernel,
        grid=(count,),
        in_specs=[
            pl.BlockSpec((1, rows, 3 * D), lambda i: (i, 0, 0)),
            pl.BlockSpec((1, rows, D), lambda i: (i, 0, 0)),
        ],
        out_specs=pl.BlockSpec((1, rows, 3 * D), lambda i: (i, 0, 0)),
        out_shape=jax.ShapeDtypeStruct((count, rows, 3 * D), BF16),
        cost_estimate=estimate(10 * count * rows * rows * D * 4, count * rows * D * 14, count * rows * rows * HEADS),
        name="enc_attend_back",
    )(joint, grad)


def causal_mask(rows, length):
    row = lax.broadcasted_iota(jnp.int32, (rows, rows), 0)
    column = lax.broadcasted_iota(jnp.int32, (rows, rows), 1)
    return (column <= row) & (column < length)


def norm_tile(values, gain):
    centred = values - jnp.mean(values, axis=-1, keepdims=True)
    inverse = lax.rsqrt(jnp.mean(centred * centred, axis=-1, keepdims=True) + 1e-05)
    plain = centred * inverse
    return (plain * gain).astype(BF16), plain, inverse


def norm_back_tile(grad, normed, inverse, gain):
    scaled = grad * gain
    inner = jnp.mean(scaled * normed, axis=-1, keepdims=True)
    return inverse * (scaled - jnp.mean(scaled, axis=-1, keepdims=True) - normed * inner)


class Loads:
    def __init__(self, sems, *pairs):
        self.copies = [pltpu.make_async_copy(src, dst, sems.at[k]) for k, (src, dst) in enumerate(pairs)]
        for copy in self.copies:
            copy.start()

    def wait(self, k):
        self.copies[k].wait()


def live_rows(rows, length):
    row = lax.broadcasted_iota(jnp.int32, (rows, 1), 0)
    return (row // CH * CH < length).astype(F32)


def decoder_kernel(nseq, length_ref, order_ref, tokens, gain_a, gain_b, gain_c, *refs):
    received, selfjoint, selfmerge, crossquery, memorymap, crossmerge, feedup, feeddown = refs[:8]
    outs, place_of = refs[8:25], refs[25]
    (
        output, normed_a, plain_a, inverse_a, joint, mixed, normed_b, plain_b, inverse_b, asked, chosen, memory, crossed, normed_c,
        plain_c, inverse_c, hidden_slope,
    ) = kept = refs[26:43]
    joint_w, merge_w, query_w, map_w, cross_w, up_w, down_w, sems, gather_sems, store_sems = refs[43:]
    rows = tokens.shape[0]
    count = order_ref.shape[1]
    flat = chosen.shape[0]
    places = flat // count
    cap = count // nseq
    length = length_ref[0]
    me = lax.axis_index("seq")
    stores = []

    def store(*done):
        for k, (src, dst) in enumerate(zip(kept, outs)):
            if any(src is ref for ref in done):
                stores.append(pltpu.make_async_copy(src, dst, store_sems.at[k]))
                stores[-1].start()

    gathers = []
    for k in range(count):
        slot = order_ref[0, k]
        source = ((slot // cap) ^ me) * cap + slot % cap
        place_of[source] = k
        gathers.append(
            pltpu.make_async_copy(
                received.at[pl.ds(pl.multiple_of(source * places, places), places)],
                chosen.at[pl.ds(k * places, places)],
                gather_sems.at[k],
            )
        )
    loads = Loads(
        sems,
        (selfjoint, joint_w),
        (selfmerge, merge_w),
        (crossquery, query_w),
        (memorymap, map_w),
        (crossmerge, cross_w),
        (feedup, up_w),
        (feeddown, down_w),
    )
    for copy in gathers:
        copy.start()

    def keep_inverse(ref, inverse):
        ref[...] = jnp.broadcast_to(inverse, ref.shape)

    sequence = tokens[...].astype(F32)
    normed, plain, inverse = norm_tile(sequence, gain_a[...])
    normed_a[...] = normed
    plain_a[...] = plain.astype(BF16)
    keep_inverse(inverse_a, inverse)
    store(normed_a, plain_a, inverse_a)
    loads.wait(0)
    for third in range(3):
        lanes = slice(third * D, (third + 1) * D)
        joint[:, lanes] = dot_nn(normed_a[...], joint_w[:, lanes]).astype(BF16)
    store(joint)
    allowed = causal_mask(rows, length)
    for group in range(0, PAIRS, 3):
        chosen_pairs = range(group, group + 3)
        items = [tuple(joint[:, col(p, third)] for third in range(3)) for p in chosen_pairs]
        for p, block in zip(chosen_pairs, pairs_forward(items, allowed)):
            mixed[:, col(p)] = block
    loads.wait(1)
    after_self = sequence + dot_nn(mixed[...], merge_w[...])
    normed, plain, inverse = norm_tile(after_self, gain_b[...])
    normed_b[...] = normed
    plain_b[...] = plain.astype(BF16)
    keep_inverse(inverse_b, inverse)
    store(mixed, normed_b, plain_b, inverse_b)
    loads.wait(2)
    asked[...] = dot_nn(normed_b[...], query_w[...]).astype(BF16)
    store(asked)

    for copy in gathers:
        copy.wait()
    store(chosen)
    loads.wait(3)

    def project(block, carry):
        window = pl.ds(pl.multiple_of(block * rows, rows), rows)
        for half in range(2):
            lanes = slice(half * D, (half + 1) * D)
            memory[window, lanes] = dot_nn(chosen[window], map_w[:, lanes]).astype(BF16)
        return carry

    lax.fori_loop(0, flat // rows, project, 0)
    store(memory)

    def cross_forward(span, carry):
        window = pl.ds(pl.multiple_of(span * CH, CH), CH)
        around = pl.ds(pl.multiple_of(span * 2 * places, places), 2 * places)
        items = [(asked[window, col(p)], memory[around, col(p, 0)], memory[around, col(p, 1)]) for p in range(PAIRS)]
        for p, block in enumerate(pairs_forward(items)):
            crossed[window, col(p)] = block
        return carry

    lax.fori_loop(0, rows // CH, cross_forward, 0)
    loads.wait(4)
    after_cross = after_self + dot_nn(crossed[...], cross_w[...]) * live_rows(rows, length)
    normed, plain, inverse = norm_tile(after_cross, gain_c[...])
    normed_c[...] = normed
    plain_c[...] = plain.astype(BF16)
    keep_inverse(inverse_c, inverse)
    store(crossed, normed_c, plain_c, inverse_c)
    loads.wait(5)
    loads.wait(6)
    total = after_cross
    for f in range(hidden_slope.shape[2] // D):
        lanes = slice(f * D, (f + 1) * D)
        bent, tilt = curve(dot_nn(normed_c[...], up_w[:, lanes]))
        hidden_slope[0, :, lanes] = bent
        hidden_slope[1, :, lanes] = tilt
        total = total + dot_nn(bent, down_w[lanes])
    output[...] = total.astype(BF16)
    store(output, hidden_slope)
    for copy in stores:
        copy.wait()


def decoder(tokens, lengths, order, received, gains, weights, nseq):
    rows = tokens.shape[0]
    flat = received.shape[0]
    count = order.shape[1]
    inside = pl.BlockSpec(memory_space=pltpu.VMEM)
    scalar = pl.BlockSpec(memory_space=pltpu.SMEM)
    anywhere = pl.BlockSpec(memory_space=pl.ANY)
    narrow = jax.ShapeDtypeStruct((rows, D), BF16)
    inverse = jax.ShapeDtypeStruct((rows, LANES), F32)
    outs = [
        narrow, narrow, narrow, inverse, jax.ShapeDtypeStruct((rows, 3 * D), BF16), narrow, narrow, narrow, inverse, narrow,
        jax.ShapeDtypeStruct((flat, D), BF16), jax.ShapeDtypeStruct((flat, 2 * D), BF16), narrow, narrow, narrow, inverse,
        jax.ShapeDtypeStruct((2, rows, weights[5].shape[1]), BF16),
    ]
    return pl.pallas_call(
        partial(decoder_kernel, nseq),
        in_specs=[scalar] * 2 + [inside] * 4 + [anywhere] * 8,
        out_specs=[pl.BlockSpec(memory_space=pltpu.HBM)] * len(outs) + [scalar],
        out_shape=outs + [jax.ShapeDtypeStruct((count,), jnp.int32)],
        scratch_shapes=[pltpu.VMEM(out.shape, out.dtype) for out in outs]
        + [pltpu.VMEM(weight.shape, BF16) for weight in weights]
        + [
            pltpu.SemaphoreType.DMA((7,)),
            pltpu.SemaphoreType.DMA((count,)),
            pltpu.SemaphoreType.DMA((len(outs),)),
        ],
        compiler_params=pltpu.CompilerParams(vmem_limit_bytes=60 * 2**20),
        cost_estimate=estimate(10e9, 40e6),
        name="decoder",
    )(lengths, order, tokens, *gains, received, *weights)


def self_back_kernel(length_ref, *refs):
    asked_grad, cross_total, plain_b, inverse_b, gain_b, joint, plain_a, inverse_a, gain_a = refs[:9]
    crossquery, selfmerge, selfjoint = refs[9:12]
    self_in, joint_grad, input_grad = refs[12:15]
    query_w, merge_w, joint_w, mixed_grad, sems = refs[15:]
    rows = joint.shape[0]
    loads = Loads(sems, (crossquery, query_w), (selfmerge, merge_w), (selfjoint, joint_w))
    loads.wait(0)
    total = cross_total[...] + norm_back_tile(
        dot_nt(asked_grad[...], query_w[...]), plain_b[...].astype(F32), inverse_b[:, :1], gain_b[...]
    )
    self_in[...] = total.astype(BF16)
    loads.wait(1)
    mixed_grad[...] = dot_nt(self_in[...], merge_w[...]).astype(BF16)
    allowed = causal_mask(rows, length_ref[0])
    for group in range(0, PAIRS, 3):
        chosen = range(group, group + 3)
        items = [tuple(joint[:, col(p, third)] for third in range(3)) + (mixed_grad[:, col(p)],) for p in chosen]
        for p, grads in zip(chosen, pairs_backward(items, allowed)):
            for third in range(3):
                joint_grad[:, col(p, third)] = grads[third]
    loads.wait(2)
    back = dot_nt(joint_grad[...], joint_w[...])
    input_grad[...] = total + norm_back_tile(back, plain_a[...].astype(F32), inverse_a[:, :1], gain_a[...])


def self_back(lengths, asked_grad, cross_total, plain_b, inverse_b, gain_b, joint, plain_a, inverse_a, gain_a, weights):
    rows = joint.shape[0]
    inside = pl.BlockSpec(memory_space=pltpu.VMEM)
    return pl.pallas_call(
        self_back_kernel,
        in_specs=[pl.BlockSpec(memory_space=pltpu.SMEM)] + [inside] * 9 + [pl.BlockSpec(memory_space=pl.ANY)] * 3,
        out_specs=[inside] * 3,
        out_shape=[
            jax.ShapeDtypeStruct((rows, D), BF16),
            jax.ShapeDtypeStruct((rows, 3 * D), BF16),
            jax.ShapeDtypeStruct((rows, D), F32),
        ],
        scratch_shapes=[pltpu.VMEM(weight.shape, BF16) for weight in weights]
        + [pltpu.VMEM((rows, D), BF16), pltpu.SemaphoreType.DMA((3,))],
        compiler_params=pltpu.CompilerParams(vmem_limit_bytes=40 * 2**20),
        cost_estimate=estimate(8e9, 15e6),
        name="self_back",
    )(lengths, asked_grad, cross_total, plain_b, inverse_b, gain_b, joint, plain_a, inverse_a, gain_a, *weights)


def swap(value, axis, size, mask):
    return lax.ppermute(value, axis, [(i, i ^ mask) for i in range(size)])


def bit_of(axis, mask):
    return (lax.axis_index(axis) // mask) % 2


def pick(value, dim, index):
    return lax.dynamic_index_in_dim(value, index, dim, keepdims=False)


def halve(value, dim, axis, size, mask):
    bit = bit_of(axis, mask)
    arrived = swap(pick(value, dim, 1 - bit), axis, size, mask)
    return (pick(value, dim, bit).astype(F32) + arrived.astype(F32)).astype(BF16)


def join(value, dim, axis, size, mask):
    arrived = swap(value, axis, size, mask)
    bit = bit_of(axis, mask)
    return jnp.where(
        bit == 0, jnp.concatenate([value, arrived], axis=dim), jnp.concatenate([arrived, value], axis=dim)
    )


def masks(size):
    found, mask = [], 1
    while mask < size:
        found.append(mask)
        mask *= 2
    return found


def reduce_group(totals, sizes, rows_first):
    nseq, nnbr = sizes
    core = bit_of("seq", 1)
    parts = []
    for whole in totals:
        height, width = whole.shape
        parts.append(halve(whole.reshape(height, 2, width // 2), 1, "seq", nseq, 1))
    widths = [part.shape[1] for part in parts]
    total = parts[0] if len(parts) == 1 else jnp.concatenate(parts, axis=1)
    bits = masks(nnbr)
    rows = total.shape[0] // nnbr
    total = total.reshape((2,) * len(bits) + (rows, total.shape[1]))
    seq_bits = masks(nseq)[1:]

    def over_seq(total):
        for mask in seq_bits:
            shape = total.shape
            total = total.reshape(shape[:-2] + (2, shape[-2] // 2, shape[-1]))
            total = halve(total, total.ndim - 3, "seq", nseq, mask)
        return total

    def over_nbr(total):
        left = list(reversed(bits))
        for mask in bits:
            total = halve(total, left.index(mask), "nbr", nnbr, mask)
            left.remove(mask)
        return total

    if rows_first:
        total = over_nbr(over_seq(total))
        for mask in reversed(seq_bits):
            total = join(total, 0, "seq", nseq, mask)
    else:
        total = over_nbr(total)
        for mask in seq_bits:
            total = (total.astype(F32) + swap(total, "seq", nseq, mask).astype(F32)).astype(BF16)
    other = swap(total, "seq", nseq, 1)
    results, start = [], 0
    for width in widths:
        mine, theirs = total[:, start : start + width], other[:, start : start + width]
        results.append(
            jnp.where(
                core == 0, jnp.concatenate([mine, theirs], axis=1), jnp.concatenate([theirs, mine], axis=1)
            ).astype(F32)
        )
        start += width
    return results


def flip(index, mask):
    for bit in masks(mask + 1):
        if mask & bit:
            index = index + bit * (1 - 2 * ((lax.axis_index("seq") // bit) % 2))
    return index


def encoder_kernel(nseq, count, *refs):
    neighbours, gain_a, gain_b, gain_c, coderjoint, codermerge, coderup, coderdown = refs[:8]
    outs, received = refs[8:18], refs[18]
    entering, joint_w, merge_w, up_w, down_w = refs[19:24]
    kept, normed_c = refs[24:34], refs[34]
    load_sem, weight_sem, store_sem, send_sem, recv_sem = refs[35:]
    normed, joint, mixed, plain_b, inverse_b, normed_b, slope, hidden, plain_c, inverse_c = kept
    flat = entering.shape[0]
    rows, places = flat // nseq, flat // count
    s, n = lax.axis_index("seq"), lax.axis_index("nbr")

    barrier = pltpu.get_barrier_semaphore()
    for m in range(1, nseq):
        pl.semaphore_signal(barrier, inc=1, device_id=(flip(s, m), n), device_id_type=MESH)
    order = list(reversed(range(nseq)))
    loads = {}
    for m in order:
        source = pl.ds(pl.multiple_of(flip(s, m) * rows, rows), rows)
        loads[m] = pltpu.make_async_copy(neighbours.at[source], entering.at[pl.ds(m * rows, rows)], load_sem.at[m])
        loads[m].start()
    weights = Loads(weight_sem, (coderjoint, joint_w), (codermerge, merge_w), (coderup, up_w), (coderdown, down_w))
    pl.semaphore_wait(barrier, nseq - 1)

    stores, sends = [], []

    def store(src, dst):
        stores.append(pltpu.make_async_copy(src, dst, store_sem.at[len(stores)]))
        stores[-1].start()

    for turn, group in enumerate([(m,) for m in order[: nseq - 2]] + [(0, 1)]):
        begin, size = group[0] * rows, len(group) * rows
        window = pl.ds(begin, size)

        def put(*numbers, window=window):
            for k in numbers:
                store(kept[k].at[window], outs[k].at[window])

        for m in group:
            loads[m].wait()
        embedded = entering[window].astype(F32)
        normed[window] = norm_tile(embedded, gain_a[...])[0]
        if turn == 0:
            weights.wait(0)
        for third in range(3):
            lanes = slice(third * D, (third + 1) * D)
            joint[window, lanes] = dot_nn(normed[window], joint_w[:, lanes]).astype(BF16)
        put(0, 1)

        def attend(k, carry, begin=begin):
            inside = pl.ds(pl.multiple_of(begin + k * places, places), places)
            items = [tuple(joint[inside, col(p, third)] for third in range(3)) for p in range(PAIRS)]
            for p, block in enumerate(pairs_forward(items)):
                mixed[inside, col(p)] = block
            return carry

        lax.fori_loop(0, size // places, attend, 0)
        if turn == 0:
            weights.wait(1)
        middle = embedded + dot_nn(mixed[window], merge_w[...])
        rounded, plain, inverse = norm_tile(middle, gain_b[...])
        normed_b[window] = rounded
        plain_b[window] = plain.astype(BF16)
        inverse_b[window] = jnp.broadcast_to(inverse, (size, LANES))
        put(2, 3, 4, 5)
        if turn == 0:
            weights.wait(2)
            weights.wait(3)
        total = middle
        for f in range(hidden.shape[1] // D):
            lanes = slice(f * D, (f + 1) * D)
            bent, tilt = curve(dot_nn(rounded, up_w[:, lanes]))
            hidden[window, lanes] = bent
            slope[window, lanes] = tilt
            store(hidden.at[window, lanes], outs[7].at[window, lanes])
            store(slope.at[window, lanes], outs[6].at[window, lanes])
            total = total + dot_nn(bent, down_w[lanes])
        rounded, plain, inverse = norm_tile(total, gain_c[...])
        normed_c[window] = rounded
        plain_c[window] = plain.astype(BF16)
        inverse_c[window] = jnp.broadcast_to(inverse, (size, LANES))
        for m in reversed(group):
            part = pl.ds(m * rows, rows)
            if m == 0:
                store(normed_c.at[part], received.at[part])
            else:
                copy = pltpu.make_async_remote_copy(
                    src_ref=normed_c.at[part],
                    dst_ref=received.at[part],
                    send_sem=send_sem.at[m],
                    recv_sem=recv_sem.at[m],
                    device_id=(flip(s, m), n),
                    device_id_type=MESH,
                )
                copy.start()
                sends.append(copy)
        put(8, 9)
    for copy in stores + sends:
        copy.wait()


def encoder(neighbours, gains, weights, nseq):
    count, places, _ = neighbours.shape
    flat = count * places
    hidden = weights[2].shape[1]
    widths = (D, 3 * D, D, D, LANES, D, hidden, hidden, D, LANES)
    kinds = (BF16, BF16, BF16, BF16, F32, BF16, BF16, BF16, BF16, F32)
    anywhere = pl.BlockSpec(memory_space=pl.ANY)
    inside = pl.BlockSpec(memory_space=pltpu.VMEM)
    return pl.pallas_call(
        partial(encoder_kernel, nseq, count),
        in_specs=[anywhere] + [inside] * 3 + [anywhere] * 4,
        out_specs=[anywhere] * 11,
        out_shape=[jax.ShapeDtypeStruct((flat, w), k) for w, k in zip(widths, kinds)]
        + [jax.ShapeDtypeStruct((flat, D), BF16)],
        scratch_shapes=[pltpu.VMEM((flat, D), BF16)]
        + [pltpu.VMEM(weight.shape, BF16) for weight in weights]
        + [pltpu.VMEM((flat, w), k) for w, k in zip(widths, kinds)]
        + [
            pltpu.VMEM((flat, D), BF16),
            pltpu.SemaphoreType.DMA((nseq,)),
            pltpu.SemaphoreType.DMA((4,)),
            pltpu.SemaphoreType.DMA((20 * nseq,)),
            pltpu.SemaphoreType.DMA((nseq,)),
            pltpu.SemaphoreType.DMA((nseq,)),
        ],
        compiler_params=pltpu.CompilerParams(collective_id=1, has_side_effects=True, vmem_limit_bytes=60 * 2**20),
        cost_estimate=estimate(18e9, 50e6),
        name="encoder",
    )(neighbours.reshape(flat, D), *gains, *weights)


HALF = D // 2


MATRICES = 11
DOWN = (0, 7)
UNITS = (
    ((0, 0), (0, 1)),
    ((0, 2), (0, 3)),
    ((1, 0), (1, 1)),
    ((1, 2), (1, 3)),
    ((2, 0), (3, 0)),
    ((4, 0), (4, 1)),
    ((5, 0), (6, 0)),
    ((6, 1), (6, 2)),
    ((7, 0), (7, 1)),
    ((7, 2), (7, 3)),
    ((8, 0), (8, 1)),
    ((8, 2), (8, 3)),
    ((9, 0), (10, 0)),
    ((10, 1), (10, 2)),
)
CARRIED = {
    0: (("feed",),),
    1: (("spans", 0, 2),),
    2: (("spans", 2, 4), ("back",)),
    3: (("self",),),
    4: (("enter",), ("rows", 0)),
    5: (("rows", 1),),
    6: (("rows", 2),),
    7: (("rows", 3),),
    8: (("heads", 0, (0, 1)),),
    9: (("heads", 1, (0, 1)),),
    10: (("heads", 2, (0, 1)),),
    11: (("heads", 3, (0, 1)),),
}
TILE = 256
BACK_IN = (
    "length", "place_of", "feed_gain", "cross_gain", "self_gain", "gain_c", "gain_b",
    "out_grad", "dec_plain_a", "dec_inverse_a", "dec_plain_b", "dec_inverse_b", "dec_plain_c", "dec_inverse_c", "hidden_slope",
    "dec_joint", "asked", "memory",
    "plain_c", "inverse_c", "slope", "plain_b", "inverse_b", "joint",
    "feeddown", "feedup", "crossmerge", "memorymap", "crossquery", "selfmerge", "selfjoint", "coderdown", "coderup", "codermerge",
)


def backward_kernel(blocks, *refs):
    refs = list(refs)

    def take(number):
        taken = refs[:number]
        del refs[:number]
        return taken

    given_refs = dict(zip(BACK_IN, take(len(BACK_IN))))
    values = take(MATRICES)
    outs = take(MATRICES)
    (input_grad,) = take(1)
    (
        stage, first, own, mid, low_a, end_a, tail_a, low_b, end_b, tail_b, low_d, end_d, tail_d, tail_x, result,
        down_w, wide, merge_w, rising_grad, down_in, merge_in, joint_grad,
        y_in, plain_in, inverse_in, slope_in, plain_in_b, inverse_in_b, upper,
        feed_a, some_a, some_b, grad_in, self_in, dec_joint_grad,
        send_sem, recv_sem, local_sem,
    ) = refs
    rows = D // 8
    part = rows // 2
    flat = blocks * TILE
    places = TILE // 2
    s, n = lax.axis_index("seq"), lax.axis_index("nbr")
    c, x = s % 2, s // 2
    y, z1, z2 = n % 2, (n // 2) % 2, n // 4
    at_core, at_x = (s + 1 - 2 * c, n), (s + 2 - 4 * x, n)
    at_y, at_z1, at_z2 = (s, n + 1 - 2 * y), (s, n + 2 - 4 * z1), (s, n + 4 - 8 * z2)
    at_seq = (None, at_core, at_x, (3 - s, n))
    mine = pl.ds(pl.multiple_of(c * HALF, 128), HALF)
    other = pl.ds(pl.multiple_of((1 - c) * HALF, 128), HALF)
    kept = pl.ds(pl.multiple_of(x * part, 16), part)
    given = pl.ds(pl.multiple_of((1 - x) * part, 16), part)

    barrier = pltpu.get_barrier_semaphore()
    for partner in at_seq[1:] + (at_y, at_z1, at_z2):
        pl.semaphore_signal(barrier, inc=1, device_id=partner, device_id_type=MESH)

    pending = {}
    counts = {"local": 0, "remote": 0}

    def remote(key, src, dst, partner):
        index = counts["remote"]
        counts["remote"] += 1
        copy = pltpu.make_async_remote_copy(
            src_ref=src,
            dst_ref=dst,
            send_sem=send_sem.at[index],
            recv_sem=recv_sem.at[index],
            device_id=partner,
            device_id_type=MESH,
        )
        copy.start()
        pending[key] = copy

    def local(key, src, dst):
        copy = pltpu.make_async_copy(src, dst, local_sem.at[counts["local"]])
        counts["local"] += 1
        copy.start()
        pending.setdefault(key, []).append(copy)

    def load(key, name, dst):
        local(key, given_refs[name], dst)

    def arrived(key):
        for copy in pending.pop(key, []):
            copy.wait()

    def tile(block, number=1):
        return pl.ds(block * TILE, number * TILE)


    def fetch(u):
        if u == 0:
            local(("unit", 0), given_refs["hidden_slope"].at[0], feed_a)
        elif u == 2:
            local(("unit", u), values[1], some_a.at[tile(0)])
        elif u in (4, 6):
            for k in range(2):
                local(("unit", u), values[u - 2 + k if u == 4 else u - 1 + k], some_a.at[tile(k)])
        elif u == 5:
            local(("unit", u), values[4], some_a)
        elif u == 8:
            local(("unit", 8), values[7], wide)
            for k in range(3):
                local(("unit", 10), values[8 + k], down_w.at[pl.ds(k * flat, flat)])

    def operands(u, k):
        left = pl.ds(k * D, D)
        if u in (2, 3):
            return some_a.at[tile(0)], rising_grad.at[tile(u - 2), pl.ds((2 + k) * D, D)]
        if u == 4:
            return some_a.at[tile(k)], some_a.at[tile(2 + k)]
        if u == 5:
            return some_a, some_b.at[:, left]
        if u == 6:
            return some_a.at[tile(k)], self_in if k == 0 else dec_joint_grad.at[:, pl.ds(0, D)]
        if u == 7:
            return some_a.at[tile(1)], dec_joint_grad.at[:, pl.ds((1 + k) * D, D)]
        if u in (10, 11):
            return down_w.at[pl.ds(0, flat)], rising_grad.at[:, pl.ds(((u - 10) * 2 + k) * D, D)]
        if u == 12:
            return down_w.at[pl.ds((1 + k) * flat, flat)], merge_in if k == 0 else joint_grad.at[:, pl.ds(0, D)]
        return down_w.at[pl.ds(2 * flat, flat)], joint_grad.at[:, pl.ds((1 + k) * D, D)]

    def product(u):
        if UNITS[u][0][0] in DOWN:
            left, right = (feed_a, grad_in) if u < 2 else (wide, down_in)
            begin = (u % 2) * 2 * rows

            def one(shard, carry):
                columns = left[:, pl.ds(pl.multiple_of(shard * 4 * rows, 128), 4 * rows)]
                block = dot_tn(columns[:, begin : begin + 2 * rows], right[...]).astype(BF16)
                stage[0, shard] = block[:rows]
                stage[1, shard] = block[rows:]
                return carry

            lax.fori_loop(0, 8, one, 0)
            return
        for k in range(2):
            left, right = operands(u, k)
            stage[k] = dot_tn(left[...], right[...]).astype(BF16).reshape(8, rows, D)


    def slot(u):
        return u % 5, u % 4

    def straight(u):
        return u % 4 != 2

    def wide_slot(u):
        return (u // 4 * 3 + (0, 1, None, 2)[u % 4]) % 4

    def stage0(u):
        arrived(("unit", u))
        product(u)
        remote(("core", u), stage.at[:, :, :, other], first.at[u % 2], at_core)

    def stage1(u):
        five, four = slot(u)
        pending.pop(("core", u)).wait()

        def one(k, carry):
            k, a, b, d = k // 8, (k // 4) % 2, (k // 2) % 2, k % 2
            shard = 4 * a + 2 * b + d
            own[five, k, a, b, d] = stage[k, shard, :, mine] + first[u % 2, k, shard]
            return carry

        lax.fori_loop(0, 16, one, 0)
        if straight(u):
            remote(("a", u), own.at[five, 0, :, :, :, given], mid.at[wide_slot(u)], at_x)
            remote(("b", u), own.at[five, 1, :, :, 1 - y], low_b.at[four], at_y)
        else:
            remote(("a", u), own.at[five, 0, :, :, 1 - y], low_b.at[four], at_y)
            remote(("b", u), own.at[five, 1, :, 1 - z1], low_d, at_z1)

    def stage2(u):
        five, four = slot(u)
        pending.pop(("a", u)).wait()
        pending.pop(("b", u)).wait()
        for a in range(2):
            for b in range(2):
                if straight(u):
                    for d in range(2):
                        own[five, 0, a, b, d, kept] = own[five, 0, a, b, d, kept] + mid[wide_slot(u), a, b, d]
                    own[five, 1, a, b, y] = own[five, 1, a, b, y] + low_b[four, a, b]
                else:
                    own[five, 0, a, b, y] = own[five, 0, a, b, y] + low_b[four, a, b]
                    own[five, 1, a, z1, b] = own[five, 1, a, z1, b] + low_d[a, b]
        if straight(u):
            remote(("a", u), own.at[five, 0, :, :, 1 - y, kept], low_a.at[four], at_y)
        else:
            remote(("a", u), own.at[five, 0, :, :, y, given], low_a.at[four], at_x)
        if straight(u):
            remote(("b", u), own.at[five, 1, :, 1 - z1, y], end_b.at[four], at_z1)
        else:
            remote(("b", u), own.at[five, 1, 1 - z2, z1], end_d, at_z2)

    def stage3(u):
        five, four = slot(u)
        pending.pop(("a", u)).wait()
        pending.pop(("b", u)).wait()
        for a in range(2):
            for b in range(2):
                own[five, 0, a, b, y, kept] = own[five, 0, a, b, y, kept] + low_a[four, a, b]
            if straight(u):
                own[five, 1, a, z1, y] = own[five, 1, a, z1, y] + end_b[four, a]
            else:
                own[five, 1, z2, z1, a] = own[five, 1, z2, z1, a] + end_d[a]
        remote(("a", u), own.at[five, 0, :, 1 - z1, y, kept], end_a.at[four], at_z1)
        if straight(u):
            remote(("b", u), own.at[five, 1, 1 - z2, z1, y], tail_b.at[four], at_z2)
        else:
            remote(("b", u), own.at[five, 1, z2, z1, 1 - y], tail_d, at_y)

    def stage4(u):
        five, four = slot(u)
        pending.pop(("a", u)).wait()
        pending.pop(("b", u)).wait()
        for a in range(2):
            own[five, 0, a, z1, y, kept] = own[five, 0, a, z1, y, kept] + end_a[four, a]
        own[five, 1, z2, z1, y] = own[five, 1, z2, z1, y] + (tail_b[four] if straight(u) else tail_d[...])
        remote(("a", u), own.at[five, 0, 1 - z2, z1, y, kept], tail_a.at[four], at_z2)
        remote(("b", u), own.at[five, 1, z2, z1, y], tail_x.at[four], at_x)

    def stage5(u):
        five, four = slot(u)
        pending.pop(("a", u)).wait()
        pending.pop(("b", u)).wait()
        result[u % 6, 0, kept, mine] = own[five, 0, z2, z1, y, kept] + tail_a[four]
        result[u % 6, 1, :, mine] = own[five, 1, z2, z1, y] + tail_x[four]
        piece = result.at[u % 6, 0, kept, mine]
        remote(("a", u), piece, piece, at_x)

    def stage6(u):
        pending.pop(("a", u)).wait()
        piece = result.at[u % 6, :, :, mine]
        remote(("a", u), piece, piece, at_core)

    def stage7(u):
        pending.pop(("a", u)).wait()
        for k, (matrix, block) in enumerate(UNITS[u]):
            if matrix in DOWN:
                target = outs[matrix].at[pl.ds(block * rows, rows)]
            else:
                target = outs[matrix].at[:, pl.ds(block * D, D)]
            local(("out", u), result.at[u % 6, k], target)

    def stage8(u):
        arrived(("out", u))

    stages = (stage0, stage1, stage2, stage3, stage4, stage5, stage6, stage7, stage8)


    def carry_feed():
        arrived("feed")
        total = None
        for f in range(4):
            lanes = pl.ds(f * D, D)
            rounded = (dot_nt(grad_in[...], down_w[lanes]) * slope_in[:, lanes].astype(F32)).astype(BF16)
            rising_grad[tile(f // 2), pl.ds((2 + f % 2) * D, D)] = rounded
            back = dot_nt(rounded, wide[pl.ds(0, D), lanes])
            total = back if total is None else total + back
        total = grad_in[...].astype(F32) + norm_back_tile(
            total, plain_in[...].astype(F32), inverse_in[:, :1], given_refs["feed_gain"][...]
        )
        upper[...] = total
        cross_in = (total * live_rows(TILE, given_refs["length"][0])).astype(BF16)
        some_a[tile(2)] = cross_in
        arrived("cross")
        down_in[tile(1)] = dot_nt(cross_in, merge_w[0]).astype(BF16)
        load("weights", "coderdown", down_w)
        load("weights", "coderup", wide.at[pl.ds(0, D)])
        load("self", "selfmerge", merge_w.at[0])
        load("enter", "dec_plain_a", plain_in)
        load("enter", "dec_inverse_a", inverse_in)

    def carry_spans(begin, end):
        def one(span, carry):
            window = pl.ds(pl.multiple_of(span * CH, CH), CH)
            shifted = pl.ds(pl.multiple_of(TILE + span * CH, CH), CH)
            around = pl.ds(pl.multiple_of(span * TILE, TILE), TILE)
            items = [
                (down_in[window, col(p)], rising_grad[around, col(p, 0)], rising_grad[around, col(p, 1)], down_in[shifted, col(p)])
                for p in range(PAIRS)
            ]
            for p, (dq, dk, dv) in enumerate(pairs_backward(items)):
                some_a[pl.ds(pl.multiple_of(3 * TILE + span * CH, CH), CH), col(p)] = dq
                some_b[around, col(p, 0)] = dk
                some_b[around, col(p, 1)] = dv
            return carry

        lax.fori_loop(begin, end, one, 0)

    def carry_back():
        arrived("map")

        def one(block, carry):
            window = pl.ds(pl.multiple_of(block * TILE, TILE), TILE)
            down_in[window] = dot_nt(some_b[window], joint_grad[pl.ds(0, D), pl.ds(0, 2 * D)]).astype(BF16)
            return carry

        lax.fori_loop(0, blocks, one, 0)
        load("enter", "selfjoint", joint_grad.at[pl.ds(0, D)])
        for k in range(2 * blocks):
            place = given_refs["place_of"][k]
            total = None
            for span in range(2 * blocks):
                weight = jnp.broadcast_to((place == span).astype(F32), (places, LANES)).astype(BF16)
                part_of = down_in[pl.ds(span * places, places)] * jnp.concatenate([weight] * PAIRS, axis=1)
                total = part_of if total is None else total + part_of
            merge_in[pl.ds(k * places, places)] = total
        for m in range(1, blocks):
            remote(("y", m), merge_in.at[tile(m)], y_in.at[m - 1], at_seq[m])

    def carry_self():
        arrived("self")
        total = upper[...] + norm_back_tile(
            dot_nt(some_a[tile(3)], merge_w[1]), plain_in_b[...].astype(F32), inverse_in_b[:, :1], given_refs["cross_gain"][...]
        )
        upper[...] = total
        self_in[...] = total.astype(BF16)
        load("weights", "codermerge", merge_w.at[1])
        feed_a[:, pl.ds(3 * D, D)] = dot_nt(self_in[...], merge_w[0]).astype(BF16)
        allowed = causal_mask(TILE, given_refs["length"][0])
        for group in range(0, PAIRS, 3):
            pairs = range(group, group + 3)
            items = [tuple(joint_grad[tile(3), col(p, third)] for third in range(3)) + (feed_a[:, pl.ds(3 * D + p * LANES, LANES)],) for p in pairs]
            for p, pieces in zip(pairs, pairs_backward(items, allowed)):
                for third in range(3):
                    dec_joint_grad[:, col(p, third)] = pieces[third]

    def carry_enter():
        arrived("enter")
        back = dot_nt(dec_joint_grad[...], joint_grad[pl.ds(0, D)])
        upper[...] = upper[...] + norm_back_tile(
            back, plain_in[...].astype(F32), inverse_in[:, :1], given_refs["self_gain"][...]
        )
        local("input", upper, input_grad)
        fetch_rows(0)


    def fetch_rows(block):
        window = tile(block)
        local("rows", given_refs["plain_c"].at[window], plain_in)
        local("rows", given_refs["inverse_c"].at[window], inverse_in)
        local("rows", given_refs["slope"].at[window], slope_in)
        local("rows", given_refs["plain_b"].at[window], plain_in_b)
        local("rows", given_refs["inverse_b"].at[window], inverse_in_b)

    def fetch_heads(block):
        local("heads", given_refs["joint"].at[tile(block)], dec_joint_grad)

    def carry_rows(block):
        window = tile(block)
        arrived("rows")
        if block == 0:
            arrived("weights")
            arrived("input")
            came = merge_in[window]
        else:
            pending.pop(("y", block)).wait()
            came = y_in[block - 1]
        total = norm_back_tile(
            came.astype(F32), plain_in[...].astype(F32), inverse_in[:, :1], given_refs["gain_c"][...]
        )
        upper[...] = total
        down_in[window] = total.astype(BF16)
        for f in range(4):
            lanes = pl.ds(f * D, D)
            rounded = (dot_nt(down_in[window], down_w[lanes]) * slope_in[:, lanes].astype(F32)).astype(BF16)
            rising_grad[window, lanes] = rounded
            back = dot_nt(rounded, wide[pl.ds(0, D), lanes])
            total = back if f == 0 else total + back
        total = upper[...] + norm_back_tile(
            total, plain_in_b[...].astype(F32), inverse_in_b[:, :1], given_refs["gain_b"][...]
        )
        rounded = total.astype(BF16)
        merge_in[window] = rounded
        feed_a[:, pl.ds(block * D, D)] = dot_nt(rounded, merge_w[1]).astype(BF16)
        if block + 1 < blocks:
            fetch_rows(block + 1)
        else:
            fetch(8)
            fetch_heads(0)

    def carry_heads(block, which):
        if which[0] == 0:
            arrived("heads")

        def one(k, carry):
            inside = pl.ds(pl.multiple_of(k * places, 128), places)
            outside = pl.ds(pl.multiple_of(block * TILE + k * places, 128), places)
            items = [
                tuple(dec_joint_grad[inside, col(p, third)] for third in range(3)) + (feed_a[inside, pl.ds(block * D + p * LANES, LANES)],)
                for p in range(PAIRS)
            ]
            for p, pieces in enumerate(pairs_backward(items)):
                for third in range(3):
                    joint_grad[outside, col(p, third)] = pieces[third]
            return carry

        lax.fori_loop(which[0], which[-1] + 1, one, 0)
        if which[-1] == 1 and block + 1 < blocks:
            fetch_heads(block + 1)

    carried = {
        "feed": carry_feed,
        "spans": carry_spans,
        "back": carry_back,
        "self": carry_self,
        "enter": carry_enter,
        "rows": carry_rows,
        "heads": carry_heads,
    }
    load(("unit", 0), "out_grad", grad_in)
    fetch(0)
    load("feed", "feeddown", down_w)
    local("feed", given_refs["hidden_slope"].at[1], slope_in)
    load("feed", "feedup", wide.at[pl.ds(0, D)])
    load("feed", "dec_plain_c", plain_in)
    load("feed", "dec_inverse_c", inverse_in)
    load("cross", "crossmerge", merge_w.at[0])
    load("cross", "asked", down_in.at[tile(0)])
    load("cross", "memory", rising_grad.at[:, pl.ds(0, 2 * D)])
    load("map", "memorymap", joint_grad.at[pl.ds(0, D), pl.ds(0, 2 * D)])
    load("self", "crossquery", merge_w.at[1])
    load("self", "dec_plain_b", plain_in_b)
    load("self", "dec_inverse_b", inverse_in_b)
    load("self", "dec_joint", joint_grad.at[tile(3)])
    pl.semaphore_wait(barrier, 6)
    for tick in range(len(UNITS) + len(stages) - 1):
        for level in (1, 0) + tuple(range(2, len(stages))):
            if 0 <= tick - level < len(UNITS):
                stages[level](tick - level)
        if 1 <= tick < 7:
            fetch(tick + 1)
        for kind, *details in CARRIED.get(tick, ()):
            carried[kind](*details)


def backward(blocks, given, values, heights):
    rows = D // 8
    part = rows // 2
    flat = blocks * TILE
    anywhere = pl.BlockSpec(memory_space=pl.ANY)
    spaces = [pltpu.SMEM] * 2 + [pltpu.VMEM] * 5 + [pl.ANY] * (len(BACK_IN) - 7 + MATRICES)

    def room(*shape, dtype=BF16):
        return pltpu.VMEM(shape, dtype)

    return pl.pallas_call(
        partial(backward_kernel, blocks),
        in_specs=[pl.BlockSpec(memory_space=space) for space in spaces],
        out_specs=[anywhere] * (MATRICES + 1),
        out_shape=[jax.ShapeDtypeStruct(height, BF16) for height in heights] + [jax.ShapeDtypeStruct((TILE, D), F32)],
        scratch_shapes=[
            room(2, 8, rows, D),
            room(2, 2, 8, rows, HALF),
            room(5, 2, 2, 2, 2, rows, HALF),
            room(4, 2, 2, 2, part, HALF),
            room(4, 2, 2, part, HALF),
            room(4, 2, part, HALF),
            room(4, part, HALF),
            room(4, 2, 2, rows, HALF),
            room(4, 2, rows, HALF),
            room(4, rows, HALF),
            room(2, 2, rows, HALF),
            room(2, rows, HALF),
            room(rows, HALF),
            room(4, rows, HALF),
            room(6, 2, rows, D),
            room(4 * D, D),
            room(flat, 4 * D),
            room(2, D, D),
            room(flat, 4 * D),
            room(flat, D),
            room(flat, D),
            room(flat, 3 * D),
            room(blocks - 1, TILE, D),
            room(TILE, D),
            room(TILE, LANES, dtype=F32),
            room(TILE, 4 * D),
            room(TILE, D),
            room(TILE, LANES, dtype=F32),
            room(TILE, D, dtype=F32),
            room(TILE, 4 * D),
            room(flat, D),
            room(flat, 2 * D),
            room(TILE, D),
            room(TILE, D),
            room(TILE, 3 * D),
            pltpu.SemaphoreType.DMA((len(UNITS) * 12,)),
            pltpu.SemaphoreType.DMA((len(UNITS) * 12,)),
            pltpu.SemaphoreType.DMA((128,)),
        ],
        compiler_params=pltpu.CompilerParams(
            collective_id=0, has_side_effects=True, vmem_limit_bytes=62 * 2**20
        ),
        cost_estimate=estimate(55e9, 120e6),
        name="backward_and_sums",
    )(*[given[name] for name in BACK_IN], *values)


GAINED = (6, 3, 1, 10, 8, 4)


def finish_kernel(nnbr, *refs):
    gains, sums, weights, passed = refs[:6], refs[6:17], refs[17:23], refs[23]
    outs, gain_outs, passed_out = refs[24:35], refs[35:41], refs[41]
    sums_in, weights_in, wide = refs[42:53], refs[53:59], refs[59:70]
    passed_in, sum_sems, weight_sems, out_sems = refs[70:]
    rows = gain_outs[0].shape[1]
    n = lax.axis_index("nbr")
    own = pl.ds(pl.multiple_of(n * rows, 8), rows)
    loads = Loads(sum_sems, (passed, passed_in), *zip(sums, sums_in))
    weight_loads = Loads(weight_sems, *[(weight.at[own], inside) for weight, inside in zip(weights, weights_in)])
    row = lax.broadcasted_iota(jnp.int32, (D, rows), 0)
    place = lax.broadcasted_iota(jnp.int32, (D, rows), 1) + n * rows
    own_gains = lax.dot_general(
        jnp.concatenate([gain[...][None] for gain in gains], axis=0),
        (row == place).astype(F32),
        (((1,), (0,)), ((), ())),
        precision=lax.Precision.HIGHEST,
        preferred_element_type=F32,
    )
    diagonal = lax.broadcasted_iota(jnp.int32, (rows, rows), 0) == lax.broadcasted_iota(jnp.int32, (rows, rows), 1)
    loads.wait(0)
    stores = [pltpu.make_async_copy(passed_in, passed_out, out_sems.at[len(sums)])]
    stores[0].start()
    for matrix in range(len(sums)):
        loads.wait(matrix + 1)
        wide[matrix][...] = sums_in[matrix][...].astype(F32)
        stores.append(pltpu.make_async_copy(wide[matrix], outs[matrix], out_sems.at[matrix]))
        stores[-1].start()
    for k, matrix in enumerate(GAINED):
        weight_loads.wait(k)
        product = weights_in[k][...].astype(F32) * wide[matrix][...]
        summed = jnp.sum(product, axis=1, keepdims=True)
        across = jnp.sum(jnp.where(diagonal, summed, 0.0), axis=0, keepdims=True)
        gain_outs[k][...] = across / own_gains[k : k + 1]
    for copy in stores:
        copy.wait()


def finish(sums, gains, weights, passed, nnbr):
    rows = D // nnbr
    anywhere = pl.BlockSpec(memory_space=pl.ANY)
    inside = pl.BlockSpec(memory_space=pltpu.VMEM)
    results = pl.pallas_call(
        partial(finish_kernel, nnbr),
        in_specs=[inside] * 6 + [anywhere] * (len(sums) + len(weights) + 1),
        out_specs=[pl.BlockSpec(memory_space=pltpu.HBM)] * len(sums)
        + [inside] * len(weights)
        + [pl.BlockSpec(memory_space=pltpu.HBM)],
        out_shape=[jax.ShapeDtypeStruct(total.shape, F32) for total in sums]
        + [jax.ShapeDtypeStruct((1, rows), F32)] * len(weights)
        + [jax.ShapeDtypeStruct(passed.shape, passed.dtype)],
        scratch_shapes=[pltpu.VMEM(total.shape, total.dtype) for total in sums]
        + [pltpu.VMEM((rows, weight.shape[1]), BF16) for weight in weights]
        + [pltpu.VMEM(total.shape, F32) for total in sums]
        + [
            pltpu.VMEM(passed.shape, passed.dtype),
            pltpu.SemaphoreType.DMA((len(sums) + 1,)),
            pltpu.SemaphoreType.DMA((len(weights),)),
            pltpu.SemaphoreType.DMA((len(sums) + 1,)),
        ],
        compiler_params=pltpu.CompilerParams(vmem_limit_bytes=56 * 2**20),
        cost_estimate=estimate(1e7, 20e6),
        name="finish",
    )(*gains, *sums, *weights, passed)
    return results[: len(sums)], [grad.reshape(rows) for grad in results[len(sums) : -1]], results[-1]


def body(
    sizes,
    tokens,
    neighbours,
    out_grad,
    lengths,
    slot_order,
    selfgain,
    selfjoint,
    selfmerge,
    crossgain,
    crossquery,
    crossmerge,
    feedgain,
    feedup,
    feeddown,
    codergain,
    coderjoint,
    codermerge,
    codermid,
    coderup,
    coderdown,
    codertop,
    memorymap,
):
    nseq, nnbr = sizes
    count, places, _ = neighbours.shape
    flat = count * places

    (
        enc_normed, enc_joint, enc_mixed, enc_plain_b, enc_inverse_b, enc_normed_b, enc_slope, enc_hidden, enc_plain_c, enc_inverse_c,
        received,
    ) = encoder(
        neighbours,
        [codergain, codermid, codertop],
        [coderjoint, codermerge, coderup, coderdown],
        nseq,
    )

    (
        output, normed_a, plain_a, inverse_a, joint, mixed, normed_b, plain_b, inverse_b, asked, chosen, memory, crossed, normed_c,
        plain_c, inverse_c, hidden_slope, place_of,
    ) = decoder(
        tokens[0],
        lengths,
        slot_order,
        received,
        [selfgain, crossgain, feedgain],
        [selfjoint, selfmerge, crossquery, memorymap, crossmerge, feedup, feeddown],
        nseq,
    )
    values = [
        hidden_slope[0], normed_c, crossed, normed_b, chosen, mixed, normed_a, enc_hidden, enc_normed_b, enc_mixed, enc_normed,
    ]
    if nseq == 4 and nnbr == 8:
        weights = [
            feeddown, feedup, crossmerge, crossquery, memorymap, selfmerge, selfjoint, coderdown, coderup, codermerge, coderjoint
        ]
        given = dict(
            length=lengths, place_of=place_of, feed_gain=feedgain, cross_gain=crossgain, self_gain=selfgain, gain_c=codertop,
            gain_b=codermid, out_grad=out_grad[0], dec_plain_a=plain_a, dec_inverse_a=inverse_a, dec_plain_b=plain_b,
            dec_inverse_b=inverse_b, dec_plain_c=plain_c, dec_inverse_c=inverse_c, hidden_slope=hidden_slope, dec_joint=joint,
            asked=asked, memory=memory, plain_c=enc_plain_c, inverse_c=enc_inverse_c, slope=enc_slope, plain_b=enc_plain_b,
            inverse_b=enc_inverse_b, joint=enc_joint, feeddown=feeddown, feedup=feedup, crossmerge=crossmerge,
            memorymap=memorymap, crossquery=crossquery, selfmerge=selfmerge, selfjoint=selfjoint, coderdown=coderdown,
            coderup=coderup, codermerge=codermerge,
        )
        *sums, input_grad = backward(nseq, given, [normed_c] + values[1:], [(w.shape[0] // nnbr, w.shape[1]) for w in weights])
    else:
        down_in = out_grad[0]
        rising_grad = (hidden_slope[1].astype(F32) * times_back(down_in, feeddown)).astype(BF16)
        cross_total = down_in.astype(F32) + norm_backward(
            times_back(rising_grad, feedup), plain_c.astype(F32), inverse_c[:, :1], feedgain
        )
        live = (jnp.arange(tokens.shape[1], dtype=jnp.int32) // CH * CH < lengths[0]).astype(F32)[:, None]
        cross_in = (cross_total * live).astype(BF16)
        asked_grad, memory_grad = spans_backward(asked, memory, times_back(cross_in, crossmerge).astype(BF16))
        back = times_back(memory_grad, memorymap).astype(BF16).reshape(count, places, D)[place_of]
        back = back.reshape(nseq, flat // nseq, D)
        returned = [back[m] if m == 0 else swap(back[m], "seq", nseq, m) for m in range(nseq)]
        self_in, joint_grad, input_grad = self_back(
            lengths, asked_grad, cross_total, plain_b, inverse_b, crossgain, joint, plain_a, inverse_a, selfgain,
            [crossquery, selfmerge, selfjoint],
        )
        upper_total = norm_backward(
            jnp.concatenate(returned, axis=0).astype(F32), enc_plain_c.astype(F32), enc_inverse_c[:, :1], codertop
        )
        enc_down_in = upper_total.astype(BF16)
        enc_rising_grad = (enc_slope.astype(F32) * times_back(enc_down_in, coderdown)).astype(BF16)
        middle_total = upper_total + norm_backward(
            times_back(enc_rising_grad, coderup), enc_plain_b.astype(F32), enc_inverse_b[:, :1], codermid
        )
        enc_merge_in = middle_total.astype(BF16)
        enc_mixed_grad = times_back(enc_merge_in, codermerge).astype(BF16).reshape(count, places, D)
        enc_joint_grad = enc_attend_back(enc_joint.reshape(count, places, 3 * D), enc_mixed_grad).reshape(flat, 3 * D)
        grads = [
            down_in, rising_grad, cross_in, asked_grad, memory_grad, self_in, joint_grad, enc_down_in, enc_rising_grad, enc_merge_in,
            enc_joint_grad,
        ]
        sums = [weight_grad(v, g).astype(BF16) for v, g in zip(values, grads)]
        ways = (False, True, False, False, False, False, False, True, False, True, True)
        sums = [reduce_group([total], sizes, way)[0] for total, way in zip(sums, ways)]
    sums, gain_grads, input_grad = finish(
        sums,
        [selfgain, crossgain, feedgain, codergain, codermid, codertop],
        [selfjoint, crossquery, feedup, coderjoint, coderup, memorymap],
        input_grad,
        nnbr,
    )
    output, input_grad = output[None], input_grad[None]
    (
        grad_feeddown,
        grad_feedup,
        grad_crossmerge,
        grad_crossquery,
        grad_memorymap,
        grad_selfmerge,
        grad_selfjoint,
        grad_coderdown,
        grad_coderup,
        grad_codermerge,
        grad_coderjoint,
    ) = sums
    grad_selfgain, grad_crossgain, grad_feedgain, grad_codergain, grad_codermid, grad_codertop = gain_grads
    return (
        output,
        input_grad,
        grad_selfgain,
        grad_selfjoint,
        grad_selfmerge,
        grad_crossgain,
        grad_crossquery,
        grad_crossmerge,
        grad_feedgain,
        grad_feedup,
        grad_feeddown,
        grad_codergain,
        grad_coderjoint,
        grad_codermerge,
        grad_codermid,
        grad_coderup,
        grad_coderdown,
        grad_codertop,
        grad_memorymap,
    )


def solution(mesh):
    spread = ("seq", "nbr")
    sizes = (mesh.shape["seq"], mesh.shape["nbr"])
    placed = (
        P(spread, None, None),
        P(spread, None, None),
        P(spread, None, None),
        P(spread),
        P(spread, None),
    ) + (P(),) * 17
    gain, weight = P("nbr"), P("nbr", None)
    return jax.shard_map(
        partial(body, sizes),
        mesh=mesh,
        in_specs=placed,
        out_specs=(
            P(spread, None, None),
            P(spread, None, None),
            gain,
            weight,
            weight,
            gain,
            weight,
            weight,
            gain,
            weight,
            weight,
            gain,
            weight,
            weight,
            gain,
            weight,
            weight,
            gain,
            weight,
        ),
        check_vma=False,
    )
```
